32 devices in a mesh: ctx: 16 (over z, x, core), fsdp: 2 (over y).
Axes of the slice: x: 2, y: 2, z: 4, core: 2. Of those that a mesh axis runs over, the one named last changes fastest.
Arguments:
- queries: bfloat16 [2, 4096, 2048], P(None, 'ctx', 'fsdp'), may hold values from -5.5 to 5.5
- keys_values: bfloat16 [2, 2, 4096, 2048], P(None, None, 'ctx', 'fsdp'), may hold values from -5.5 to 5.5
- block_mask: int32 [64, 32], P('ctx'), may hold values 0 or 1
- out_weight: bfloat16 [2048, 4096], P('fsdp'), may hold values from -3 to 3
Outputs:
- mixed: bfloat16 [2, 4096, 4096], P(None, 'ctx', 'fsdp')
The draws below stay inside these ranges and needn't reach their ends.
All inputs are finite; a program needn't handle non-finite values. No bound on the sum of `block_mask` on one device may be relied on, other than what follows from the above.
Results may differ from the reference program's by a relative error of at most 0.0058.
Values may be sent and summed in bfloat16 or wider, within the bound.
No kernel may reach another device: no remote copies, remote signals or barrier semaphores. Data moves between devices by JAX's collectives and lax.ppermute only.
A program may use at most 128 MiB of HBM per device.

```python
import math
import jax
import jax.numpy as jnp
from jax import lax

D = 4096
HD = 128
BLK = 64
WINB = 32
TOK_DEV = 256
HH = 2048
LEN = 4096
NBLOCKS = 64
N_CTX = 16


def drawn_rows(key, salt, shape):
    base = jax.random.normal(jax.random.fold_in(key, salt), shape, jnp.float32)
    return jnp.clip(base, -5.5, 5.5)


def draw_queries(key, part):
    return drawn_rows(key, 11, (2, LEN, HH)).astype(jnp.bfloat16)


def draw_keys_values(key, part):
    keys = drawn_rows(key, 21, (2, LEN, HH))
    values = jax.random.normal(jax.random.fold_in(key, 31), (2, LEN, HH), jnp.float32)
    values = jnp.clip(values, -5.5, 5.5)
    return jnp.stack([keys, values]).astype(jnp.bfloat16)


def place_ends(drawn, key, smallest, largest):
    extent = drawn.shape
    place = [jax.random.randint(jax.random.fold_in(key, axis), (), 0, extent[axis]) for axis in range(len(extent))]
    drawn = drawn.at[tuple(place)].set(smallest)
    longest = extent.index(max(extent))
    place[longest] = (place[longest] + 1) % extent[longest]
    return drawn.at[tuple(place)].set(largest)


def shard_levels(own_key, extent, cuts, low, top_value):
    def one(position, shards_of):
        steps = jax.random.uniform(jax.random.fold_in(jax.random.fold_in(own_key, 6), position), (shards_of,), jnp.float32, low / len(cuts), top_value / len(cuts))
        return jnp.repeat(jnp.exp(steps), extent[position] // shards_of).reshape((-1,) + (1,) * (len(extent) - position - 1))

    level = one(*cuts[0])
    for cut in cuts[1:]:
        level = level * one(*cut)
    return level


def normal_values(rng, extent, spread, bound, cuts=(), kind=jnp.bfloat16):
    factor_of = shard_levels(rng, extent, cuts, -0.22, 0.18) if cuts else 1.0
    values = jax.random.normal(rng, extent, jnp.float32) * spread * factor_of
    return jnp.minimum(jnp.maximum(values, -bound), bound).astype(kind)


def setup_inputs(seed: int = 0) -> dict:
    key_of = jax.random.split(jax.random.key(seed), 5)
    return {
        "queries": draw_queries(jax.random.fold_in(key_of[4], 71), 0),
        "keys_values": draw_keys_values(jax.random.fold_in(key_of[4], 71), 0),
        "block_mask": place_ends((jax.random.randint(key_of[2], (NBLOCKS, WINB), 0, 2) < 1).astype(jnp.int32), jax.random.fold_in(key_of[2], 1), 0, 1),
        "out_weight": normal_values(key_of[3], (HH, D), (max(1, HH // 512)) ** -0.5, 3.0, ((0, 2),)),
    }


def block_rules(first_block, query_count, key_start, key_count, mask_rows):
    query_blocks = first_block + jnp.arange(query_count, dtype=jnp.int32)
    key_blocks = key_start + jnp.arange(key_count, dtype=jnp.int32)
    block_gap = query_blocks[:, None] - key_blocks[None, :]
    present = key_blocks[None, :] >= 0
    clean_ok = (block_gap >= 0) & (block_gap < WINB) & present
    offsets = jnp.arange(WINB, dtype=jnp.int32)
    picked = ((block_gap - 1)[:, :, None] == offsets[None, None, :]) & (mask_rows[:, None, :] == 1)
    noisy_ok = jnp.any(picked, axis=2) & present
    own_block = query_blocks[:, None] == query_blocks[None, :]

    def widen(table):
        return jnp.repeat(jnp.repeat(table, BLK, axis=0), BLK, axis=1)
    return (widen(clean_ok), widen(noisy_ok), widen(own_block))

def attend(query, keys, values, allowed):
    count, width = query.shape
    heads = width // HD
    query_three = query.astype(jnp.float32).reshape(count, heads, HD)
    key_three = keys.astype(jnp.float32).reshape(-1, heads, HD)
    value_three = values.astype(jnp.float32).reshape(-1, heads, HD)
    scores = jnp.einsum('qhd,khd->hqk', query_three, key_three) * (1.0 / math.sqrt(HD))
    scores = jnp.where(allowed[None], scores, jnp.float32(-1e+30))
    top = lax.optimization_barrier(jnp.max(scores, axis=-1, keepdims=True))
    expo = jnp.exp(scores - top)
    weights = (expo / lax.optimization_barrier(jnp.sum(expo, axis=-1, keepdims=True))).astype(jnp.bfloat16)
    result = jnp.einsum('hqk,khd->qhd', weights.astype(jnp.float32), value_three)
    return result.reshape(count, width).astype(jnp.bfloat16)

def reference(queries, keys_values, block_mask, out_weight):
    span = WINB * BLK
    blocks_dev = TOK_DEV // BLK
    clean_pair = jnp.pad(keys_values[:, 0], ((0, 0), (span, 0), (0, 0)))
    noisy_pair = keys_values[:, 1]

    def group_step(index):
        start = index * TOK_DEV
        zero = jnp.int32(0)
        window = lax.dynamic_slice(clean_pair, (zero, start, zero), (2, span + TOK_DEV, HH))
        own_query = lax.dynamic_slice(queries, (zero, start, zero), (2, TOK_DEV, HH))
        own_pair = lax.dynamic_slice(noisy_pair, (zero, start, zero), (2, TOK_DEV, HH))
        mask_rows = lax.dynamic_slice(block_mask, (index * blocks_dev, zero), (blocks_dev, WINB))
        first_block = index * blocks_dev
        clean_ok, noisy_ok, own_ok = block_rules(first_block, blocks_dev, first_block - WINB, blocks_dev + WINB, mask_rows)
        clean_out = attend(own_query[0], window[0], window[1], clean_ok)
        noisy_keys = jnp.concatenate([window[0], own_pair[0]], axis=0)
        noisy_values = jnp.concatenate([window[1], own_pair[1]], axis=0)
        noisy_allowed = jnp.concatenate([noisy_ok, own_ok], axis=1)
        noisy_out = attend(own_query[1], noisy_keys, noisy_values, noisy_allowed)
        return jnp.stack([clean_out, noisy_out])
    pieces = lax.map(group_step, jnp.arange(N_CTX, dtype=jnp.int32))
    attended = jnp.transpose(pieces, (1, 0, 2, 3)).reshape(2 * LEN, HH)
    mixed = jnp.dot(attended, out_weight, preferred_element_type=jnp.float32)
    return mixed.astype(jnp.bfloat16).reshape(2, LEN, D)
```

```python
import math

import jax
import jax.numpy as jnp
from jax import lax
from jax.experimental import pallas as pl
from jax.experimental.pallas import tpu as pltpu
from jax.sharding import PartitionSpec as P

HD = 128
BLK = 64
WINB = 32
MASKED = -1e30
SCALE = math.log2(math.e) / math.sqrt(HD)


def moved(array, n, go):
    pairs = [(i, go(i)) for i in range(n) if go(i) is not None]
    return lax.ppermute(array, "ctx", pairs)


def moved_both(array, n, f, go):
    pairs = [(i * f + k, go(i, k)[0] * f + go(i, k)[1]) for i in range(n) for k in range(f)]
    return lax.ppermute(array, ("ctx", "fsdp"), pairs)


def mask_table(first_block, rows, mask_rows):
    count = WINB + rows
    query = jnp.arange(rows)
    gap = WINB + query[None, :] - jnp.arange(count)[:, None]
    present = (first_block - WINB + jnp.arange(count) >= 0)[:, None]
    clean = (gap >= 0) & (gap < WINB) & present
    offsets = jnp.arange(WINB)
    picked = ((gap - 1)[:, :, None] == offsets[None, None, :]) & (mask_rows[None] == 1)
    noisy = jnp.any(picked, axis=2) & present
    own_clean = jnp.zeros((rows, rows), bool)
    own_noisy = jnp.eye(rows, dtype=bool)
    allowed = jnp.concatenate(
        [jnp.concatenate([clean, noisy], 1), jnp.concatenate([own_clean, own_noisy], 1)], 0
    )
    table = jnp.where(allowed, 0.0, MASKED).astype(jnp.float32)
    return jnp.pad(table, ((0, 0), (0, HD - table.shape[1])))


def attend_kernel(tokens, info, q_here, kn_here, there, own, one, two, swap, extra, table,
                  mine, give, keys, values):
    core, side = info[0], info[1]
    rows = tokens // BLK
    span = WINB * BLK + tokens

    def place(ref, pair):
        for slot in range(2):
            half = core if slot == 0 else 1 - core
            at = pl.multiple_of(pair * 2 * tokens + half * tokens, tokens)
            keys[pl.ds(at, tokens), :] = ref[slot, 0]
            values[pl.ds(at, tokens), :] = ref[slot, 1]

    back = WINB * BLK // (2 * tokens)
    place(two, 0)
    place(extra, jnp.where(side == 0, 1, 3))
    place(one, 2)
    place(swap, jnp.where(side == 0, 3, 1))
    place(own, back)

    spot = lax.broadcasted_iota(jnp.int32, (2 * tokens, HD), 0) // BLK
    lane = lax.broadcasted_iota(jnp.int32, (2 * tokens, HD), 1)
    hot = jnp.where(spot == lane, 1.0, 0.0).astype(jnp.bfloat16)
    contract = (((1,), (1,)), ((), ()))
    for tile in range(2):
        half = core if tile == 0 else 1 - core
        at = pl.multiple_of(half * tokens, tokens)
        if tile == 0:
            query = q_here[...].reshape(2 * tokens, HD)
            key_n, value_n = kn_here[0, 0], kn_here[1, 0]
        else:
            query = there[0:2].reshape(2 * tokens, HD)
            key_n, value_n = there[2], there[3]
        bias = jnp.broadcast_to(
            table[tile][:, None, :], (span // BLK + rows, BLK, HD)
        ).reshape(span + tokens, HD).astype(jnp.bfloat16)
        key = jnp.concatenate([keys[pl.ds(at, span), :], key_n], 0)
        key = jnp.concatenate([key, bias], 1)
        value = jnp.concatenate([values[pl.ds(at, span), :], value_n], 0)
        value = jnp.concatenate([value, jnp.ones_like(value)], 1)
        query = jnp.concatenate([query, hot], 1)
        scores = lax.dot_general(query, key, contract, preferred_element_type=jnp.float32)
        top = jnp.max(scores, axis=1, keepdims=True)
        expo = jnp.exp2((scores - top) * SCALE).astype(jnp.bfloat16)
        total = jnp.dot(expo, value, preferred_element_type=jnp.float32)
        out = (total[:, :HD] / total[:, HD:]).astype(jnp.bfloat16).reshape(2, tokens, HD)
        if tile == 0:
            mine[...] = out
        else:
            give[...] = out


def attend(info, queries, keys_values, there, blocks, table, chunk, heads_chunk, heads_half):
    tokens = queries.shape[1]
    span = WINB * BLK + 2 * tokens

    def col(h, info):
        return info[0] * heads_half + chunk * heads_chunk + h

    pair_spec = pl.BlockSpec((2, 2, tokens, HD), lambda h, info: (0, 0, 0, h))
    out_spec = pl.BlockSpec((2, tokens, HD), lambda h, info: (0, 0, h))
    out = jax.ShapeDtypeStruct((2, tokens, heads_chunk * HD), jnp.bfloat16)
    work = heads_chunk * 2 * 2 * tokens * (WINB * BLK + 2 * tokens)
    return pl.pallas_call(
        lambda *refs: attend_kernel(tokens, *refs),
        grid_spec=pltpu.PrefetchScalarGridSpec(
            num_scalar_prefetch=1,
            grid=(heads_chunk,),
            in_specs=[
                pl.BlockSpec((2, tokens, HD), lambda h, info: (0, 0, col(h, info))),
                pl.BlockSpec((2, 1, tokens, HD), lambda h, info: (0, 1, 0, col(h, info))),
                pl.BlockSpec((4, tokens, HD), lambda h, info: (0, 0, chunk * heads_chunk + h)),
                pair_spec, pair_spec, pair_spec, pair_spec, pair_spec,
                pl.BlockSpec(table.shape, lambda h, info: (0, 0, 0)),
            ],
            out_specs=[out_spec, out_spec],
            scratch_shapes=[
                pltpu.VMEM((span, HD), jnp.bfloat16),
                pltpu.VMEM((span, HD), jnp.bfloat16),
            ],
        ),
        out_shape=[out, out],
        compiler_params=pltpu.CompilerParams(vmem_limit_bytes=48 * 1024 * 1024),
        cost_estimate=pl.CostEstimate(
            flops=work * 4 * 2 * HD, bytes_accessed=4 * 1024 * 1024, transcendentals=work
        ),
    )(info, queries, keys_values, there, *blocks, table)


def project_kernel(pieces, sizes, info, *refs):
    out = refs[-1]
    acts, weights = refs[:pieces], refs[pieces:-1]
    total = None
    place = 0
    for weight, count in zip(weights, sizes):
        row = 0
        for act in acts[place:place + count]:
            wide = act.shape[2]
            part = jnp.dot(
                act[...].reshape(-1, wide), weight[row:row + wide, :],
                preferred_element_type=jnp.float32,
            )
            total = part if total is None else total + part
            row += wide
        place += count
    out[...] = total.astype(jnp.bfloat16).reshape(out.shape)


def project(info, acts, out_weight, others, features):
    tokens = acts[0][0].shape[1]
    half = out_weight.shape[0] // 2
    tile = min(256, features)
    steps = features // tile
    flat = [a for group in acts for a in group]
    weights = [out_weight, out_weight] + others
    specs = [pl.BlockSpec(a.shape, lambda s, info: (0, 0, 0)) for a in flat]
    specs += [
        pl.BlockSpec((half, tile), lambda s, info: (info[0], info[2] * steps + s)),
        pl.BlockSpec((half, tile), lambda s, info: (1 - info[0], info[2] * steps + s)),
    ]
    specs += [pl.BlockSpec((half, tile), lambda s, info: (0, s)) for _ in others]
    sizes = [len(group) for group in acts]
    return pl.pallas_call(
        lambda *refs: project_kernel(len(flat), sizes, *refs),
        grid_spec=pltpu.PrefetchScalarGridSpec(
            num_scalar_prefetch=1,
            grid=(steps,),
            in_specs=specs,
            out_specs=pl.BlockSpec((2, tokens, tile), lambda s, info: (0, 0, s)),
        ),
        out_shape=jax.ShapeDtypeStruct((2, tokens, features), jnp.bfloat16),
        compiler_params=pltpu.CompilerParams(vmem_limit_bytes=32 * 1024 * 1024),
        cost_estimate=pl.CostEstimate(
            flops=2 * 2 * tokens * half * len(weights) * features,
            bytes_accessed=2 * half * len(weights) * features + 8 * tokens * features,
            transcendentals=0,
        ),
    )(info, *flat, *weights)


def on_device(queries, keys_values, block_mask, out_weight):
    tokens = queries.shape[1]
    n, f = lax.axis_size("ctx"), lax.axis_size("fsdp")
    index, place = lax.axis_index("ctx"), lax.axis_index("fsdp")
    core, side = index % 2, (index // 2) % 2
    info = jnp.stack([core, side, place]).astype(jnp.int32)
    width = queries.shape[2] // 2
    heads_half = width // HD
    chunks = 2 if heads_half % 2 == 0 else 1
    heads_chunk = heads_half // chunks
    part = heads_chunk * HD
    rows = tokens // BLK
    features = out_weight.shape[1] // f

    def columns(array, start, size):
        return lax.dynamic_slice_in_dim(array, start, size, array.ndim - 1)

    clean = keys_values[:, 0]
    pair = lambda i: i ^ 1
    got = moved(columns(clean, (1 - core) * width, width), n, pair)
    keep = columns(clean, core * width, width)
    later = jnp.concatenate(
        [columns(queries, (1 - core) * width, width),
         columns(keys_values[:, 1], (1 - core) * width, width)], 0
    )
    there = moved(later, n, pair)
    mask_there = moved(block_mask, n, pair)

    others = []
    for r in range(1, f):
        block = lax.dynamic_slice(
            out_weight, (core * width, ((place + r) % f) * features), (width, features)
        )
        same = moved_both(block, n, f, lambda i, k: (i, (k + r) % f))
        others += [same, moved(same, n, pair)]

    first = index * rows
    sibling = (index ^ 1) * rows
    table = jnp.stack([
        mask_table(first, rows, block_mask), mask_table(sibling, rows, mask_there)
    ])

    ahead = lambda i: i + 4 if i + 4 < n else None
    across = lambda i: i ^ 2
    acts = [[] for _ in range(2 * f)]
    for chunk in range(chunks):
        cut = slice(chunk * part, (chunk + 1) * part)
        own = jnp.stack([keep[:, :, cut], got[:, :, cut]])
        one = moved(own, n, ahead)
        two = moved(one, n, ahead)
        swap = moved(one, n, across)
        extra = moved(jnp.where(side == 0, own, two), n, across)
        mine, give = attend(
            info, queries, keys_values, there, [own, one, two, swap, extra], table,
            chunk, heads_chunk, heads_half,
        )
        acts[0].append(mine)
        acts[1].append(moved(give, n, pair))
        for r in range(1, f):
            acts[2 * r].append(moved_both(mine, n, f, lambda i, k: (i, (k + r) % f)))
            acts[2 * r + 1].append(moved_both(give, n, f, lambda i, k: (i ^ 1, (k + r) % f)))
    return project(info, acts, out_weight, others, features)


def solution(mesh):
    in_specs = (
        P(None, "ctx", "fsdp"),
        P(None, None, "ctx", "fsdp"),
        P("ctx", None),
        P("fsdp", None),
    )
    out_specs = P(None, "ctx", "fsdp")
    return jax.shard_map(
        on_device, mesh=mesh, in_specs=in_specs, out_specs=out_specs, check_vma=False
    )
```

```python
import math

import jax
import jax.numpy as jnp
from jax import lax
from jax.experimental import pallas as pl
from jax.experimental.pallas import tpu as pltpu
from jax.sharding import PartitionSpec as P

HD = 128
BLK = 64
WINB = 32
MASKED = -1e30
SCALE = math.log2(math.e) / math.sqrt(HD)
VMEM = 60 * 1024 * 1024


def moved(array, n, go):
    pairs = [(i, go(i)) for i in range(n) if go(i) is not None]
    return lax.ppermute(array, "ctx", pairs)


def moved_both(array, n, f, go):
    pairs = [(i * f + k, go(i, k)[0] * f + go(i, k)[1]) for i in range(n) for k in range(f)]
    return lax.ppermute(array, ("ctx", "fsdp"), pairs)


def mask_table(first_block, rows, mask_rows):
    count = WINB + rows
    query = jnp.arange(rows)
    gap = WINB + query[None, :] - jnp.arange(count)[:, None]
    present = (first_block - WINB + jnp.arange(count) >= 0)[:, None]
    clean = (gap >= 0) & (gap < WINB) & present
    offsets = jnp.arange(WINB)
    picked = ((gap - 1)[:, :, None] == offsets[None, None, :]) & (mask_rows[None] == 1)
    noisy = jnp.any(picked, axis=2) & present
    own_clean = jnp.zeros((rows, rows), bool)
    own_noisy = jnp.eye(rows, dtype=bool)
    allowed = jnp.concatenate(
        [jnp.concatenate([clean, noisy], 1), jnp.concatenate([own_clean, own_noisy], 1)], 0
    )
    table = jnp.where(allowed, 0.0, MASKED).astype(jnp.float32)
    return jnp.pad(table, ((0, 0), (0, HD - table.shape[1])))


def behind(array, *others):
    return lax.optimization_barrier((array,) + others)[0]


def cut_kernel(info, source, out):
    out[...] = source[...]


def cut_weight(info, out_weight, features, step):
    half = out_weight.shape[0] // 2
    tiles = 4 if half % 64 == 0 else 1
    count = out_weight.shape[1] // features
    return pl.pallas_call(
        cut_kernel,
        grid_spec=pltpu.PrefetchScalarGridSpec(
            num_scalar_prefetch=1,
            grid=(tiles,),
            in_specs=[pl.BlockSpec(
                (half // tiles, features),
                lambda s, info: (info[0] * tiles + s, lax.rem(info[2] + step, count)),
            )],
            out_specs=pl.BlockSpec((half // tiles, features), lambda s, info: (s, 0)),
        ),
        out_shape=jax.ShapeDtypeStruct((half, features), out_weight.dtype),
        compiler_params=pltpu.CompilerParams(vmem_limit_bytes=VMEM),
        cost_estimate=pl.CostEstimate(
            flops=0, bytes_accessed=4 * half * features, transcendentals=0
        ),
    )(info, out_weight)


def join_kernel(info, here, got, out):
    out[0] = here[:, 0]
    out[1] = got[...]


def join_pair(info, keys_values, got, first, heads, heads_half):
    tokens = keys_values.shape[2]
    return pl.pallas_call(
        join_kernel,
        grid_spec=pltpu.PrefetchScalarGridSpec(
            num_scalar_prefetch=1,
            grid=(heads,),
            in_specs=[
                pl.BlockSpec(
                    (2, 1, tokens, HD),
                    lambda h, info: (0, 0, 0, info[0] * heads_half + first + h),
                ),
                pl.BlockSpec((2, tokens, HD), lambda h, info: (0, 0, first + h)),
            ],
            out_specs=pl.BlockSpec((2, 2, tokens, HD), lambda h, info: (0, 0, 0, h)),
        ),
        out_shape=jax.ShapeDtypeStruct((2, 2, tokens, heads * HD), keys_values.dtype),
        compiler_params=pltpu.CompilerParams(vmem_limit_bytes=VMEM),
        cost_estimate=pl.CostEstimate(
            flops=0, bytes_accessed=16 * tokens * heads * HD, transcendentals=0
        ),
    )(info, keys_values, got)


def attend_kernel(tokens, count, info, *refs):
    core, side = info[0], info[1]
    refs = refs[:6 + 4 * count] + refs[-4:]
    q_here, kn_here, there, own, low = refs[:5]
    blocks = [refs[5 + 4 * h:9 + 4 * h] for h in range(count)]
    table, mine, give, keys, values = refs[5 + 4 * count:]
    rows = tokens // BLK
    span = WINB * BLK + tokens
    back = WINB * BLK // (2 * tokens)

    def place(head, ref, pair, lanes):
        for slot in range(2):
            half = core if slot == 0 else 1 - core
            at = pl.multiple_of(pair * 2 * tokens + half * tokens, tokens)
            keys[head, pl.ds(at, tokens), :] = ref[slot, 0, :, lanes]
            values[head, pl.ds(at, tokens), :] = ref[slot, 1, :, lanes]

    only = slice(0, HD)
    for head, (one, two, swap, far) in enumerate(blocks):
        lanes = slice(head * HD, (head + 1) * HD)
        place(head, two, 0, only)
        place(head, one, 2, only)
        place(head, swap, jnp.where(side == 0, 3, 1), only)
        place(head, own, back, lanes)

    @pl.when(side == 0)
    def _():
        for head in range(count):
            place(head, blocks[head][3], 1, only)

    @pl.when(side != 0)
    def _():
        for head in range(count):
            place(head, low, 3, slice(head * HD, (head + 1) * HD))

    spot = lax.broadcasted_iota(jnp.int32, (2 * tokens, HD), 0) // BLK
    lane = lax.broadcasted_iota(jnp.int32, (2 * tokens, HD), 1)
    hot = jnp.where(spot == lane, 1.0, 0.0).astype(jnp.bfloat16)
    contract = (((1,), (1,)), ((), ()))
    biases = [
        jnp.broadcast_to(table[tile][:, None, :], (span // BLK + rows, BLK, HD))
        .reshape(span + tokens, HD).astype(jnp.bfloat16)
        for tile in range(2)
    ]

    def scores_of(head, tile):
        lanes = slice(head * HD, (head + 1) * HD)
        half = core if tile == 0 else 1 - core
        at = pl.multiple_of(half * tokens, tokens)
        if tile == 0:
            query = q_here[:, :, lanes].reshape(2 * tokens, HD)
            key_n = kn_here[0, 0, :, lanes]
        else:
            query = there[0:2, :, lanes].reshape(2 * tokens, HD)
            key_n = there[2, :, lanes]
        key = jnp.concatenate([keys[head, pl.ds(at, span), :], key_n], 0)
        key = jnp.concatenate([key, biases[tile]], 1)
        query = jnp.concatenate([query, hot], 1)
        return lax.dot_general(query, key, contract, preferred_element_type=jnp.float32)

    def attended(head, tile, scores):
        lanes = slice(head * HD, (head + 1) * HD)
        half = core if tile == 0 else 1 - core
        at = pl.multiple_of(half * tokens, tokens)
        value_n = kn_here[1, 0, :, lanes] if tile == 0 else there[3, :, lanes]
        value = jnp.concatenate([values[head, pl.ds(at, span), :], value_n], 0)
        value = jnp.concatenate([value, jnp.ones_like(value)], 1)
        top = jnp.max(scores, axis=1, keepdims=True)
        expo = jnp.exp2((scores - top) * SCALE).astype(jnp.bfloat16)
        total = jnp.dot(expo, value, preferred_element_type=jnp.float32)
        out = (total[:, :HD] / total[:, HD:]).astype(jnp.bfloat16).reshape(2, tokens, HD)
        (mine if tile == 0 else give)[:, :, lanes] = out

    jobs = [(head, tile) for head in range(count) for tile in range(2)]
    scores = scores_of(*jobs[0])
    for job, later in zip(jobs, jobs[1:] + [None]):
        upcoming = scores_of(*later) if later else None
        attended(*job, scores)
        scores = upcoming


def attend(info, queries, keys_values, there, own, low, blocks, table, first, heads_half,
           room, at, into):
    tokens = queries.shape[1]
    span = WINB * BLK + 2 * tokens
    count = len(blocks)
    wide = count * HD
    per = heads_half // count if heads_half % count == 0 and first % count == 0 else None
    assert per is not None
    here = lambda s, info: (0, 0, info[0] * per + first // count)
    out_spec = pl.BlockSpec((2, tokens, wide), lambda s, info: (0, 0, at // count))
    out = jax.ShapeDtypeStruct((2, tokens, room * HD), jnp.bfloat16)
    work = count * 2 * 2 * tokens * (WINB * BLK + 2 * tokens)
    whole = pl.BlockSpec((2, 2, tokens, wide), lambda s, info: (0, 0, 0, first // count))
    one_head = pl.BlockSpec((2, 2, tokens, HD), lambda s, info: (0, 0, 0, 0))
    return pl.pallas_call(
        lambda *refs: attend_kernel(tokens, count, *refs),
        grid_spec=pltpu.PrefetchScalarGridSpec(
            num_scalar_prefetch=1,
            grid=(1,),
            in_specs=[
                pl.BlockSpec((2, tokens, wide), here),
                pl.BlockSpec((2, 1, tokens, wide), lambda s, info: (0, 1) + here(s, info)[1:]),
                pl.BlockSpec((4, tokens, wide), lambda s, info: (0, 0, first // count)),
                whole, whole,
                *[one_head] * (4 * count),
                pl.BlockSpec(table.shape, lambda s, info: (0, 0, 0)),
                *[pl.BlockSpec(memory_space=pl.ANY) for _ in into],
            ],
            out_specs=[out_spec, out_spec],
            scratch_shapes=[
                pltpu.VMEM((count, span, HD), jnp.bfloat16),
                pltpu.VMEM((count, span, HD), jnp.bfloat16),
            ],
        ),
        out_shape=[out, out],
        input_output_aliases={7 + 4 * count + k: k for k in range(len(into))},
        compiler_params=pltpu.CompilerParams(vmem_limit_bytes=VMEM),
        cost_estimate=pl.CostEstimate(
            flops=work * 8, bytes_accessed=count * 64 * 1024, transcendentals=0
        ),
    )(info, queries, keys_values, there, own, low, *[b for group in blocks for b in group], table,
      *into)


def project_kernel(count, groups, add, info, *refs):
    out = refs[-1]
    acts, weights = refs[:count], refs[count:count + groups]
    act = jnp.concatenate([a[...].reshape(-1, a.shape[2]) for a in acts], 1)
    weight = jnp.concatenate([w[...] for w in weights], 0)
    total = jnp.dot(act, weight, preferred_element_type=jnp.float32)
    if add:
        total = total + refs[count + groups][...].reshape(total.shape)
    out[...] = total.astype(out.dtype).reshape(out.shape)


def project(info, pieces, weights, features, dtype, before=None):
    tokens = pieces[0][2].shape[1]
    tile = min(256, features)
    steps = features // tile
    half = weights[0].shape[0] // 2 // HD
    used, rows = [], []
    for group, first, act in pieces:
        for head in range(first, first + act.shape[2] // HD):
            used.append(weights[group])
            if group == 0:
                row = lambda s, info, at=head: (info[0] * half + at, info[2] * steps + s)
            elif group == 1:
                row = lambda s, info, at=head: ((1 - info[0]) * half + at, info[2] * steps + s)
            else:
                row = lambda s, info, at=head: (at, s)
            rows.append(pl.BlockSpec((HD, tile), row))
    flat = [act for _, _, act in pieces]
    spec = pl.BlockSpec((2, tokens, tile), lambda s, info: (0, 0, s))
    specs = [pl.BlockSpec(a.shape, lambda s, info: (0, 0, 0)) for a in flat] + rows
    operands = flat + used
    if before is not None:
        specs.append(spec)
        operands.append(before)
    depth = HD * len(used)
    return pl.pallas_call(
        lambda *refs: project_kernel(len(flat), len(used), before is not None, *refs),
        grid_spec=pltpu.PrefetchScalarGridSpec(
            num_scalar_prefetch=1, grid=(steps,), in_specs=specs, out_specs=spec
        ),
        out_shape=jax.ShapeDtypeStruct((2, tokens, features), dtype),
        compiler_params=pltpu.CompilerParams(vmem_limit_bytes=VMEM),
        cost_estimate=pl.CostEstimate(
            flops=2 * 2 * tokens * depth * features,
            bytes_accessed=2 * depth * features + 8 * tokens * features,
            transcendentals=0,
        ),
    )(info, *operands)


def on_device(queries, keys_values, block_mask, out_weight):
    tokens = queries.shape[1]
    n, f = lax.axis_size("ctx"), lax.axis_size("fsdp")
    index, place = lax.axis_index("ctx"), lax.axis_index("fsdp")
    core, side = index % 2, (index // 2) % 2
    info = jnp.stack([core, side, place]).astype(jnp.int32)
    width = queries.shape[2] // 2
    heads_half = width // HD
    rows = tokens // BLK
    features = out_weight.shape[1] // f
    shares = [[0, 1], [2, 3]] if heads_half == 4 else [[h] for h in range(heads_half)]

    pair = lambda i: i ^ 1
    ahead = lambda i: i + 4 if i + 4 < n else None
    across = lambda i: i ^ 2
    upper = lambda i: i + 2 if i & 2 == 0 else None
    lower = lambda i: i - 2 if i & 2 else None

    clean = lax.dynamic_slice(
        keys_values, (0, 0, 0, (1 - core) * width), (2, 1, tokens, width)
    ).reshape(2, tokens, width)
    got = moved(clean, n, pair)
    own = [join_pair(info, keys_values, got, h, 1, heads_half) for h in range(1)]
    own.append(join_pair(info, keys_values, got, 0, heads_half, heads_half))
    own, whole = own[:1], own[1]
    for h in range(1, heads_half):
        own.append(join_pair(info, keys_values, got, h, 1, heads_half))

    low = moved(whole, n, upper)
    blocks = []
    for h in range(heads_half):
        last = blocks[-1] if blocks else None
        in_turn = lambda array, k: behind(array, last[k]) if last else array
        one = moved(in_turn(own[h], 0), n, ahead)
        two = moved(in_turn(one, 1), n, ahead)
        swap = moved(in_turn(one, 2), n, across)
        far = moved(in_turn(two, 3), n, lower)
        blocks.append((one, two, swap, far))

    later = jnp.concatenate(
        [lax.dynamic_slice(queries, (0, 0, (1 - core) * width), (2, tokens, width)),
         lax.dynamic_slice(
             keys_values, (0, 1, 0, (1 - core) * width), (2, 1, tokens, width)
         ).reshape(2, tokens, width)], 0
    )
    there = moved(behind(later, own[0]), n, pair)
    mask_there = moved(behind(block_mask, own[0]), n, pair)
    table = jnp.stack([
        mask_table(index * rows, rows, block_mask),
        mask_table((index ^ 1) * rows, rows, mask_there),
    ])

    sames = [
        moved_both(
            cut_weight(behind(info, own[0]), out_weight, features, r),
            n, f, lambda i, k: (i, (k + r) % f),
        )
        for r in range(1, f)
    ]

    acts = [[] for _ in range(2 * f)]
    for k, share in enumerate(shares):
        final = k == len(shares) - 1
        runs = [[h] for h in share] if final else [share]
        into = ()
        for run in runs:
            if run[-1] < heads_half - 1:
                after = [blocks[-1][1 if final else 0]]
            else:
                after = [a[0] for a in acts[1:] if a]
            into = attend(
                behind(info, *after, *into, *acts[0][-1:]), queries, keys_values, there, whole, low,
                [blocks[h] for h in run], table, run[0], heads_half,
                len(share), run[0] - share[0], into,
            )
        mine, give = into
        acts[0].append(mine)
        for r in range(1, f):
            acts[2 * r].append(moved_both(mine, n, f, lambda i, k: (i, (k + r) % f)))
            acts[2 * r + 1].append(moved_both(give, n, f, lambda i, k: (i ^ 1, (k + r) % f)))
        acts[1].append(moved(give, n, pair))
    others = []
    for same in sames:
        same = behind(same, blocks[-1][3])
        others += [same, moved(same, n, pair)]

    weights = [out_weight, out_weight] + others
    early, late = [], []
    for g in range(2 * f):
        for k, (share, act) in enumerate(zip(shares, acts[g])):
            (late if g % 2 and g > 1 or g and k == len(shares) - 1 else early).append((g, share[0], act))
    before = project(info, early, weights, features, jnp.float32)
    return project(info, late, weights, features, jnp.bfloat16, before)


def solution(mesh):
    in_specs = (
        P(None, "ctx", "fsdp"),
        P(None, None, "ctx", "fsdp"),
        P("ctx", None),
        P("fsdp", None),
    )
    out_specs = P(None, "ctx", "fsdp")
    return jax.shard_map(
        on_device, mesh=mesh, in_specs=in_specs, out_specs=out_specs, check_vma=False
    )
```

```python
import math

import jax
import jax.numpy as jnp
from jax import lax
from jax.experimental import pallas as pl
from jax.experimental.pallas import tpu as pltpu
from jax.sharding import PartitionSpec as P

HD = 128
BLK = 64
WINB = 32
MASKED = -1e30
SCALE = math.log2(math.e) / math.sqrt(HD)
VMEM = 60 * 1024 * 1024


def moved(array, n, go):
    pairs = [(i, go(i)) for i in range(n) if go(i) is not None]
    return lax.ppermute(array, "ctx", pairs)


def moved_both(array, n, f, go):
    pairs = [(i * f + k, go(i, k)[0] * f + go(i, k)[1]) for i in range(n) for k in range(f)]
    return lax.ppermute(array, ("ctx", "fsdp"), pairs)


def behind(array, *others):
    return lax.optimization_barrier((array,) + others)[0] if others else array


def gated(array, tie):
    return pl.pallas_call(
        lambda *refs: None,
        in_specs=[pl.BlockSpec(memory_space=pl.ANY)] * 2,
        out_specs=pl.BlockSpec(memory_space=pl.ANY),
        out_shape=jax.ShapeDtypeStruct(array.shape, array.dtype),
        input_output_aliases={0: 0},
        compiler_params=pltpu.CompilerParams(vmem_limit_bytes=VMEM),
        cost_estimate=pl.CostEstimate(flops=0, bytes_accessed=0, transcendentals=0),
    )(array, tie)


def mask_table(first_block, rows, mask_rows):
    count = WINB + rows
    query = jnp.arange(rows)
    gap = WINB + query[None, :] - jnp.arange(count)[:, None]
    present = (first_block - WINB + jnp.arange(count) >= 0)[:, None]
    clean = (gap >= 0) & (gap < WINB) & present
    offsets = jnp.arange(WINB)
    picked = ((gap - 1)[:, :, None] == offsets[None, None, :]) & (mask_rows[None] == 1)
    noisy = jnp.any(picked, axis=2) & present
    own_clean = jnp.zeros((rows, rows), bool)
    own_noisy = jnp.eye(rows, dtype=bool)
    allowed = jnp.concatenate(
        [jnp.concatenate([clean, noisy], 1), jnp.concatenate([own_clean, own_noisy], 1)], 0
    )
    table = jnp.where(allowed, 0.0, MASKED).astype(jnp.float32)
    return jnp.pad(table, ((0, 0), (0, HD - table.shape[1])))


def copies(info, sources, outs, plan):
    total = sum(math.prod(o.shape) for o in outs)

    def kernel(info, *refs):
        ins, rest = refs[:len(sources)], refs[len(sources):]
        pairs = plan(info[0], info[2], ins, rest[:len(outs)])
        started = [
            pltpu.make_async_copy(a, b, rest[-1].at[k]) for k, (a, b) in enumerate(pairs)
        ]
        for copy in started:
            copy.start()
        for copy in started:
            copy.wait()

    return pl.pallas_call(
        kernel,
        grid_spec=pltpu.PrefetchScalarGridSpec(
            num_scalar_prefetch=1,
            grid=(),
            in_specs=[pl.BlockSpec(memory_space=pl.ANY)] * len(sources),
            out_specs=[pl.BlockSpec(memory_space=pl.ANY)] * len(outs),
            scratch_shapes=[pltpu.SemaphoreType.DMA((32,))],
        ),
        out_shape=[jax.ShapeDtypeStruct(o.shape, o.dtype) for o in outs],
        compiler_params=pltpu.CompilerParams(vmem_limit_bytes=VMEM),
        cost_estimate=pl.CostEstimate(flops=0, bytes_accessed=total, transcendentals=0),
    )(info, *sources)


def attend_kernel(tokens, count, info, *refs):
    core, side = info[0], info[1]
    refs = refs[:6 + 4 * count] + refs[-5:]
    q_here, kn_here, there, own, low = refs[:5]
    blocks = [refs[5 + 4 * h:9 + 4 * h] for h in range(count)]
    table, mine, give, tie, keys, values = refs[5 + 4 * count:]
    tie[...] = jnp.zeros_like(tie)
    rows = tokens // BLK
    span = WINB * BLK + tokens
    back = WINB * BLK // (2 * tokens)

    def place(head, ref, pair, lanes):
        for slot in range(2):
            half = core if slot == 0 else 1 - core
            at = pl.multiple_of(pair * 2 * tokens + half * tokens, tokens)
            keys[head, pl.ds(at, tokens), :] = ref[slot, 0, :, lanes]
            values[head, pl.ds(at, tokens), :] = ref[slot, 1, :, lanes]

    only = slice(0, HD)
    for head, (one, two, swap, far) in enumerate(blocks):
        lanes = slice(head * HD, (head + 1) * HD)
        place(head, two, 0, only)
        place(head, one, 2, only)
        place(head, swap, jnp.where(side == 0, 3, 1), only)
        place(head, own, back, lanes)

    @pl.when(side == 0)
    def _():
        for head in range(count):
            place(head, blocks[head][3], 1, only)

    @pl.when(side != 0)
    def _():
        for head in range(count):
            place(head, low, 3, slice(head * HD, (head + 1) * HD))

    spot = lax.broadcasted_iota(jnp.int32, (2 * tokens, HD), 0) // BLK
    lane = lax.broadcasted_iota(jnp.int32, (2 * tokens, HD), 1)
    hot = jnp.where(spot == lane, 1.0, 0.0).astype(jnp.bfloat16)
    contract = (((1,), (1,)), ((), ()))
    biases = [
        jnp.broadcast_to(table[tile][:, None, :], (span // BLK + rows, BLK, HD))
        .reshape(span + tokens, HD).astype(jnp.bfloat16)
        for tile in range(2)
    ]

    def scores_of(head, tile):
        lanes = slice(head * HD, (head + 1) * HD)
        half = core if tile == 0 else 1 - core
        at = pl.multiple_of(half * tokens, tokens)
        if tile == 0:
            query = q_here[:, :, lanes].reshape(2 * tokens, HD)
            key_n = kn_here[0, 0, :, lanes]
        else:
            query = there[0:2, :, lanes].reshape(2 * tokens, HD)
            key_n = there[2, :, lanes]
        key = jnp.concatenate([keys[head, pl.ds(at, span), :], key_n], 0)
        key = jnp.concatenate([key, biases[tile]], 1)
        query = jnp.concatenate([query, hot], 1)
        return lax.dot_general(query, key, contract, preferred_element_type=jnp.float32)

    def attended(head, tile, scores):
        lanes = slice(head * HD, (head + 1) * HD)
        half = core if tile == 0 else 1 - core
        at = pl.multiple_of(half * tokens, tokens)
        value_n = kn_here[1, 0, :, lanes] if tile == 0 else there[3, :, lanes]
        value = jnp.concatenate([values[head, pl.ds(at, span), :], value_n], 0)
        value = jnp.concatenate([value, jnp.ones_like(value)], 1)
        top = jnp.max(scores, axis=1, keepdims=True)
        expo = jnp.exp2((scores - top) * SCALE).astype(jnp.bfloat16)
        total = jnp.dot(expo, value, preferred_element_type=jnp.float32)
        out = (total[:, :HD] / total[:, HD:]).astype(jnp.bfloat16).reshape(2, tokens, HD)
        (mine if tile == 0 else give)[:, :, lanes] = out

    jobs = [(head, tile) for head in range(count) for tile in range(2)]
    scores = scores_of(*jobs[0])
    for job, later in zip(jobs, jobs[1:] + [None]):
        upcoming = scores_of(*later) if later else None
        attended(*job, scores)
        scores = upcoming


def attend(info, queries, keys_values, there, own, low, blocks, table, first, heads_half,
           room, at, into, after):
    tokens = queries.shape[1]
    span = WINB * BLK + 2 * tokens
    count = len(blocks)
    wide = count * HD
    per = heads_half // count if heads_half % count == 0 and first % count == 0 else None
    assert per is not None
    here = lambda s, info: (0, 0, info[0] * per + first // count)
    out_spec = pl.BlockSpec((2, tokens, wide), lambda s, info: (0, 0, at // count))
    out = jax.ShapeDtypeStruct((2, tokens, room * HD), jnp.bfloat16)
    work = count * 2 * 2 * tokens * (WINB * BLK + 2 * tokens)
    whole = pl.BlockSpec((2, 2, tokens, wide), lambda s, info: (0, 0, 0, first // count))
    one_head = pl.BlockSpec((2, 2, tokens, HD), lambda s, info: (0, 0, 0, 0))
    return pl.pallas_call(
        lambda *refs: attend_kernel(tokens, count, *refs),
        grid_spec=pltpu.PrefetchScalarGridSpec(
            num_scalar_prefetch=1,
            grid=(1,),
            in_specs=[
                pl.BlockSpec((2, tokens, wide), here),
                pl.BlockSpec((2, 1, tokens, wide), lambda s, info: (0, 1) + here(s, info)[1:]),
                pl.BlockSpec((4, tokens, wide), lambda s, info: (0, 0, first // count)),
                whole, whole,
                *[one_head] * (4 * count),
                pl.BlockSpec(table.shape, lambda s, info: (0, 0, 0)),
                *[pl.BlockSpec(memory_space=pl.ANY)] * (len(into) + len(after)),
            ],
            out_specs=[out_spec, out_spec, pl.BlockSpec((8, HD), lambda s, info: (0, 0))],
            scratch_shapes=[
                pltpu.VMEM((count, span, HD), jnp.bfloat16),
                pltpu.VMEM((count, span, HD), jnp.bfloat16),
            ],
        ),
        out_shape=[out, out, jax.ShapeDtypeStruct((8, HD), jnp.float32)],
        input_output_aliases={7 + 4 * count + k: k for k in range(len(into))},
        compiler_params=pltpu.CompilerParams(vmem_limit_bytes=VMEM),
        cost_estimate=pl.CostEstimate(
            flops=work * 8, bytes_accessed=count * 64 * 1024, transcendentals=0
        ),
    )(info, queries, keys_values, there, own, low, *[b for group in blocks for b in group], table,
      *into, *after)

def project_kernel(count, groups, add, info, *refs):
    out = refs[-1]
    acts, weights = refs[:count], refs[count:count + groups]
    act = jnp.concatenate([a[...].reshape(-1, a.shape[2]) for a in acts], 1)
    weight = jnp.concatenate([w[...] for w in weights], 0)
    total = jnp.dot(act, weight, preferred_element_type=jnp.float32)
    if add:
        total = total + refs[count + groups][...].reshape(total.shape)
    out[...] = total.astype(out.dtype).reshape(out.shape)


def project(info, pieces, weights, features, dtype, before=None):
    tokens = pieces[0][2].shape[1]
    tile = min(512, features)
    steps = features // tile
    half = weights[0].shape[0] // 2
    used, specs = [], []
    for group, first, act in pieces:
        wide = act.shape[2]
        per, at = half // wide, first * HD // wide
        used.append(weights[group])
        if group == 0:
            row = lambda s, info, at=at, per=per: (info[0] * per + at, info[2] * steps + s)
        elif group == 1:
            row = lambda s, info, at=at, per=per: ((1 - info[0]) * per + at, info[2] * steps + s)
        else:
            row = lambda s, info, at=at: (at, s)
        specs.append(pl.BlockSpec((wide, tile), row))
    flat = [act for _, _, act in pieces]
    spec = pl.BlockSpec((2, tokens, tile), lambda s, info: (0, 0, s))
    specs = [pl.BlockSpec(a.shape, lambda s, info: (0, 0, 0)) for a in flat] + specs
    operands = flat + used
    if before is not None:
        specs.append(spec)
        operands.append(before)
    depth = sum(a.shape[2] for a in flat)
    return pl.pallas_call(
        lambda *refs: project_kernel(len(flat), len(used), before is not None, *refs),
        grid_spec=pltpu.PrefetchScalarGridSpec(
            num_scalar_prefetch=1, grid=(steps,), in_specs=specs, out_specs=spec
        ),
        out_shape=jax.ShapeDtypeStruct((2, tokens, features), dtype),
        compiler_params=pltpu.CompilerParams(vmem_limit_bytes=40 * 1024 * 1024),
        cost_estimate=pl.CostEstimate(
            flops=2 * 2 * tokens * depth * features // 8,
            bytes_accessed=2 * depth * features // 8,
            transcendentals=0,
        ),
    )(info, *operands)


def on_device(queries, keys_values, block_mask, out_weight):
    tokens = queries.shape[1]
    n, f = lax.axis_size("ctx"), lax.axis_size("fsdp")
    index, place = lax.axis_index("ctx"), lax.axis_index("fsdp")
    core, side = index % 2, (index // 2) % 2
    info = jnp.stack([core, side, place]).astype(jnp.int32)
    width = queries.shape[2] // 2
    heads_half = width // HD
    rows = tokens // BLK
    features = out_weight.shape[1] // f
    bf16 = jnp.bfloat16
    shares = [[0, 1], [2, 3]] if heads_half == 4 else [[h] for h in range(heads_half)]

    pair = lambda i: i ^ 1
    ahead = lambda i: i + 4 if i + 4 < n else None
    across = lambda i: i ^ 2
    upper = lambda i: i + 2 if i & 2 == 0 else None
    lower = lambda i: i - 2 if i & 2 else None
    lanes = lambda start, size: pl.ds(pl.multiple_of(start, HD), size)

    def cut_clean(core, place, ins, outs):
        return [(ins[0].at[:, 0, :, lanes((1 - core) * width, width)], outs[0])]

    clean, = copies(info, [keys_values], [jax.ShapeDtypeStruct((2, tokens, width), bf16)], cut_clean)
    got = moved(clean, n, pair)

    def join(head, heads, kv, got, out):
        def pairs(core):
            return [
                (kv.at[:, 0, :, lanes(core * width + head * HD, heads * HD)], out.at[0]),
                (got.at[:, :, head * HD:(head + heads) * HD], out.at[1]),
            ]
        return pairs

    pair_shape = lambda heads: jax.ShapeDtypeStruct((2, 2, tokens, heads * HD), bf16)
    first, = copies(
        info, [keys_values, got], [pair_shape(1)],
        lambda core, place, ins, outs: join(0, 1, ins[0], ins[1], outs[0])(core),
    )
    one = moved(first, n, ahead)

    def cut_rest(core, place, ins, outs):
        kv, got, q, w, _ = ins
        give = lanes((1 - core) * width, width)
        plan = join(0, heads_half, kv, got, outs[0])(core)
        for h in range(1, heads_half):
            plan += join(h, 1, kv, got, outs[h])(core)
        plan += [(q.at[:, :, give], outs[heads_half].at[0:2]),
                 (kv.at[:, 1, :, give], outs[heads_half].at[2:4])]
        for r in range(1, f):
            out = outs[heads_half + r]
            column = pl.multiple_of(lax.rem(place + r, f) * features, HD)
            pieces = max(1, 4 // f)
            step = width // pieces
            for p in range(pieces):
                row = pl.multiple_of(core * width + p * step, step)
                plan.append((w.at[pl.ds(row, step), pl.ds(column, features)],
                             out.at[p * step:(p + 1) * step]))
        return plan

    whole, *rest = copies(
        info, [keys_values, got, queries, out_weight, first],
        [pair_shape(heads_half)] + [pair_shape(1)] * (heads_half - 1)
        + [jax.ShapeDtypeStruct((4, tokens, width), bf16)]
        + [jax.ShapeDtypeStruct((width, features), bf16)] * (f - 1),
        cut_rest,
    )
    own = [first] + rest[:heads_half - 1]
    later, panels = rest[heads_half - 1], rest[heads_half:]

    sames = [
        moved_both(panel, n, f, lambda i, k: (i, (k + r) % f))
        for r, panel in enumerate(panels, 1)
    ]

    blocks = []
    for h in range(heads_half):
        last = blocks[-1] if blocks else None
        in_turn = lambda array, k: behind(array, last[k]) if last else array
        if h:
            one = moved(in_turn(own[h], 0), n, ahead)
        two = moved(in_turn(one, 1), n, ahead)
        swap = moved(in_turn(one, 2), n, across)
        far = moved(in_turn(two, 3), n, lower)
        blocks.append((one, two, swap, far))
    low = moved(whole, n, upper)
    there = moved(later, n, pair)
    mask_there = moved(behind(block_mask, first), n, pair)
    table = jnp.stack([
        mask_table(index * rows, rows, block_mask),
        mask_table((index ^ 1) * rows, rows, mask_there),
    ])

    acts = [[] for _ in range(2 * f)]
    ties = []
    for k, share in enumerate(shares):
        final = k == len(shares) - 1
        into = ()
        for run in [[h] for h in share] if final else [share]:
            after = ([blocks[-1][0], blocks[-2][1]] if not final else [blocks[-1][1]]) \
                if run[-1] < heads_half - 1 else [a[0] for a in acts[1:] if a]
            mine, give, tie = attend(
                info, queries, keys_values, there, whole, low,
                [blocks[h] for h in run], table, run[0], heads_half,
                len(share), run[0] - share[0], into, after + ties[-1:],
            )
            into = (mine, give)
            ties.append(tie)
        acts[0].append(mine)
        for r in range(1, f):
            acts[2 * r].append(moved_both(mine, n, f, lambda i, k: (i, (k + r) % f)))
            acts[2 * r + 1].append(moved_both(give, n, f, lambda i, k: (i ^ 1, (k + r) % f)))
        acts[1].append(moved(give, n, pair))
    others = []
    for same in sames:
        same = gated(same, ties[-1])
        others += [same, moved(same, n, pair)]

    weights = [out_weight, out_weight] + others
    early, late = [], []
    for g in range(2 * f):
        for k, (share, act) in enumerate(zip(shares, acts[g])):
            (late if g and k == len(shares) - 1 else early).append((g, share[0], act))
    before = project(info, early, weights, features, jnp.float32)
    return project(info, late, weights, features, jnp.bfloat16, before)


def solution(mesh):
    in_specs = (
        P(None, "ctx", "fsdp"),
        P(None, None, "ctx", "fsdp"),
        P("ctx", None),
        P("fsdp", None),
    )
    out_specs = P(None, "ctx", "fsdp")
    return jax.shard_map(
        on_device, mesh=mesh, in_specs=in_specs, out_specs=out_specs, check_vma=False
    )
```

```python
import math

import jax
import jax.numpy as jnp
from jax import lax
from jax.experimental import pallas as pl
from jax.experimental.pallas import tpu as pltpu
from jax.sharding import PartitionSpec as P

HD = 128
BLK = 64
WINB = 32
MASKED = -1e30
SCALE = math.log2(math.e) / math.sqrt(HD)
VMEM = 60 * 1024 * 1024


def moved(array, n, go):
    pairs = [(i, go(i)) for i in range(n) if go(i) is not None]
    return lax.ppermute(array, "ctx", pairs)


def moved_both(array, n, f, go):
    pairs = [(i * f + k, go(i, k)[0] * f + go(i, k)[1]) for i in range(n) for k in range(f)]
    return lax.ppermute(array, ("ctx", "fsdp"), pairs)


def behind(array, *others):
    return lax.optimization_barrier((array,) + others)[0] if others else array


def gated(array, tie):
    return pl.pallas_call(
        lambda *refs: None,
        in_specs=[pl.BlockSpec(memory_space=pl.ANY)] * 2,
        out_specs=pl.BlockSpec(memory_space=pl.ANY),
        out_shape=jax.ShapeDtypeStruct(array.shape, array.dtype),
        input_output_aliases={0: 0},
        compiler_params=pltpu.CompilerParams(vmem_limit_bytes=VMEM),
        cost_estimate=pl.CostEstimate(flops=0, bytes_accessed=0, transcendentals=0),
    )(array, tie)


def mask_table(first_block, rows, mask_rows):
    count = WINB + rows
    query = jnp.arange(rows)
    gap = WINB + query[None, :] - jnp.arange(count)[:, None]
    present = (first_block - WINB + jnp.arange(count) >= 0)[:, None]
    clean = (gap >= 0) & (gap < WINB) & present
    offsets = jnp.arange(WINB)
    picked = ((gap - 1)[:, :, None] == offsets[None, None, :]) & (mask_rows[None] == 1)
    noisy = jnp.any(picked, axis=2) & present
    own_clean = jnp.zeros((rows, rows), bool)
    own_noisy = jnp.eye(rows, dtype=bool)
    allowed = jnp.concatenate(
        [jnp.concatenate([clean, noisy], 1), jnp.concatenate([own_clean, own_noisy], 1)], 0
    )
    table = jnp.where(allowed, 0.0, MASKED).astype(jnp.float32)
    table = jnp.concatenate([table, jnp.ones((count + rows, 1), jnp.float32)], 1)
    return jnp.pad(table, ((0, 0), (0, HD - table.shape[1])))


def copies(info, sources, outs, shapes, plan):
    total = sum(math.prod(o.shape) for o in outs)

    def kernel(info, *refs):
        ins, rest = refs[:len(sources)], refs[len(sources):]
        pieces = plan(info[0], info[2], ins, rest[:len(outs)])
        room, arrive, leave = rest[len(outs):-2], rest[-2], rest[-1]
        reads = [
            pltpu.make_async_copy(source, held, arrive.at[k])
            for k, ((source, _), held) in enumerate(zip(pieces, room))
        ]
        for read in reads:
            read.start()
        writes = []
        for read, (_, targets), held in zip(reads, pieces, room):
            read.wait()
            for part, target in targets:
                write = pltpu.make_async_copy(held.at[part], target, leave.at[len(writes)])
                write.start()
                writes.append(write)
        for write in writes:
            write.wait()

    return pl.pallas_call(
        kernel,
        grid_spec=pltpu.PrefetchScalarGridSpec(
            num_scalar_prefetch=1,
            grid=(),
            in_specs=[pl.BlockSpec(memory_space=pl.ANY)] * len(sources),
            out_specs=[pl.BlockSpec(memory_space=pl.ANY)] * len(outs),
            scratch_shapes=[
                *[pltpu.VMEM(shape, jnp.bfloat16) for shape in shapes],
                pltpu.SemaphoreType.DMA((len(shapes),)),
                pltpu.SemaphoreType.DMA((32,)),
            ],
        ),
        out_shape=[jax.ShapeDtypeStruct(o.shape, o.dtype) for o in outs],
        compiler_params=pltpu.CompilerParams(vmem_limit_bytes=VMEM),
        cost_estimate=pl.CostEstimate(flops=0, bytes_accessed=total, transcendentals=0),
    )(info, *sources)


def attend_kernel(tokens, count, info, *refs):
    core, side = info[0], info[1]
    refs = refs[:7 + 4 * count] + refs[-6:]
    q_here, n_here, q_there, n_there, own, low = refs[:6]
    blocks = [refs[6 + 4 * h:10 + 4 * h] for h in range(count)]
    table, mine, give, tie, keys, values, least = refs[6 + 4 * count:]
    tie[...] = jnp.zeros_like(tie)
    rows = tokens // BLK
    span = WINB * BLK + tokens
    back = WINB * BLK // (2 * tokens)

    def place(head, ref, pair, lanes):
        for slot in range(2):
            half = core if slot == 0 else 1 - core
            at = pl.multiple_of(pair * 2 * tokens + half * tokens, tokens)
            keys[head, pl.ds(at, tokens), :] = ref[slot, 0, :, lanes]
            values[head, pl.ds(at, tokens), :] = ref[slot, 1, :, lanes]

    only = slice(0, HD)
    for head, (one, two, swap, far) in enumerate(blocks):
        lanes = slice(head * HD, (head + 1) * HD)
        place(head, two, 0, only)
        place(head, one, 2, only)
        place(head, swap, jnp.where(side == 0, 3, 1), only)
        place(head, own, back, lanes)

    @pl.when(side == 0)
    def _():
        for head in range(count):
            place(head, blocks[head][3], 1, only)

    @pl.when(side != 0)
    def _():
        for head in range(count):
            place(head, low, 3, slice(head * HD, (head + 1) * HD))

    spot = lax.broadcasted_iota(jnp.int32, (2 * tokens, HD), 0) // BLK
    lane = lax.broadcasted_iota(jnp.int32, (2 * tokens, HD), 1)
    hot = jnp.where(spot == lane, 1.0, 0.0)
    contract = (((1,), (1,)), ((), ()))
    step = tokens
    tiles = (span + tokens) // step

    def operands(head, tile):
        lanes = slice(head * HD, (head + 1) * HD)
        half = core if tile == 0 else 1 - core
        q_ref, n_ref = (q_here, n_here) if tile == 0 else (q_there, n_there)
        query = q_ref[:, :, lanes].reshape(2 * tokens, HD)
        key, value = [], []
        for k in range(tiles):
            at = pl.multiple_of((half + k) * tokens, tokens)
            if k == tiles - 1:
                key.append(n_ref[0, 0, :, lanes])
                value.append(n_ref[1, 0, :, lanes])
            else:
                key.append(keys[head, pl.ds(at, step), :])
                value.append(values[head, pl.ds(at, step), :])
        bias = [
            jnp.broadcast_to(
                table[tile, k * rows:(k + 1) * rows][:, None, :], (rows, BLK, HD)
            ).reshape(step, HD).astype(jnp.bfloat16)
            for k in range(tiles)
        ]
        return query, key, bias, value

    def store(head, tile, out):
        lanes = slice(head * HD, (head + 1) * HD)
        (mine if tile == 0 else give)[:, :, lanes] = out.astype(jnp.bfloat16).reshape(
            2, tokens, HD)

    shift_lane = 2 * rows
    jobs = [(head, tile) for head in range(count) for tile in range(2)]
    low_sum = None
    for head, tile in jobs:
        query, key, bias, value = operands(head, tile)
        wide = query.astype(jnp.float32)
        longest = None
        for k in key:
            k = k.astype(jnp.float32)
            size = jnp.max(jnp.sum(k * k, axis=1, keepdims=True), axis=0, keepdims=True)
            longest = size if longest is None else jnp.maximum(longest, size)
        bound = jnp.sqrt(jnp.sum(wide * wide, axis=1, keepdims=True) * longest)
        extra = jnp.where(lane == shift_lane, -bound, hot).astype(jnp.bfloat16)
        query = jnp.concatenate([query, extra], 1)
        parts = []
        for k in range(tiles):
            scores = lax.dot_general(
                query, jnp.concatenate([key[k], bias[k]], 1), contract,
                preferred_element_type=jnp.float32,
            )
            parts.append(jnp.exp2(scores * SCALE).astype(jnp.bfloat16))
        expo = jnp.concatenate(parts, 1)
        value = jnp.concatenate(value, 0)
        value = jnp.concatenate([value, jnp.ones_like(value)], 1)
        total = jnp.dot(expo, value, preferred_element_type=jnp.float32)
        sums = total[:, HD:]
        store(head, tile, total[:, :HD] / sums)
        smallest = jnp.min(sums.reshape(-1, 8, HD), axis=0)
        low_sum = smallest if low_sum is None else jnp.minimum(low_sum, smallest)
    least[...] = low_sum

    @pl.when(jnp.logical_not(jnp.min(least[...]) > 2.0 ** -40))
    def _():
        for head, tile in jobs:
            query, key, bias, value = operands(head, tile)
            query = jnp.concatenate([query, hot.astype(jnp.bfloat16)], 1)
            key = jnp.concatenate(
                [jnp.concatenate(key, 0), jnp.concatenate(bias, 0)], 1)
            scores = lax.dot_general(query, key, contract, preferred_element_type=jnp.float32)
            top = jnp.max(scores, axis=1, keepdims=True)
            expo = jnp.exp2((scores - top) * SCALE).astype(jnp.bfloat16)
            value = jnp.concatenate(value, 0)
            value = jnp.concatenate([value, jnp.ones_like(value)], 1)
            total = jnp.dot(expo, value, preferred_element_type=jnp.float32)
            store(head, tile, total[:, :HD] / total[:, HD:])


def attend(info, queries, keys_values, there, got, own, low, blocks, table, first, heads_half,
           room, at, into, after):
    tokens = queries.shape[1]
    span = WINB * BLK + 2 * tokens
    count = len(blocks)
    wide = count * HD
    per = heads_half // count if heads_half % count == 0 and first % count == 0 else None
    assert per is not None
    here = lambda s, info: (0, 0, info[0] * per + first // count)
    out_spec = pl.BlockSpec((2, tokens, wide), lambda s, info: (0, 0, at // count))
    out = jax.ShapeDtypeStruct((2, tokens, room * HD), jnp.bfloat16)
    work = count * 2 * 2 * tokens * (WINB * BLK + 2 * tokens)
    whole = pl.BlockSpec((2, 2, tokens, wide), lambda s, info: (0, 0, 0, first // count))
    one_head = pl.BlockSpec((2, 2, tokens, HD), lambda s, info: (0, 0, 0, 0))
    return pl.pallas_call(
        lambda *refs: attend_kernel(tokens, count, *refs),
        grid_spec=pltpu.PrefetchScalarGridSpec(
            num_scalar_prefetch=1,
            grid=(1,),
            in_specs=[
                *[
                    pl.BlockSpec((2, tokens, wide), here),
                    pl.BlockSpec((2, 1, tokens, wide), lambda s, info: (0, 1) + here(s, info)[1:]),
                ] * 2,
                whole, whole,
                *[one_head] * (4 * count),
                pl.BlockSpec(table.shape, lambda s, info: (0, 0, 0)),
                *[pl.BlockSpec(memory_space=pl.ANY)] * (len(into) + len(after)),
            ],
            out_specs=[out_spec, out_spec, pl.BlockSpec((8, HD), lambda s, info: (0, 0))],
            scratch_shapes=[
                pltpu.VMEM((count, span, HD), jnp.bfloat16),
                pltpu.VMEM((count, span, HD), jnp.bfloat16),
                pltpu.VMEM((8, HD), jnp.float32),
            ],
        ),
        out_shape=[out, out, jax.ShapeDtypeStruct((8, HD), jnp.float32)],
        input_output_aliases={8 + 4 * count + k: k for k in range(len(into))},
        compiler_params=pltpu.CompilerParams(vmem_limit_bytes=VMEM),
        cost_estimate=pl.CostEstimate(
            flops=work * 8, bytes_accessed=count * 64 * 1024, transcendentals=0
        ),
    )(info, queries, keys_values, there, got, own, low, *[b for group in blocks for b in group], table,
      *into, *after)

def project_kernel(count, groups, add, info, *refs):
    out = refs[-1]
    acts, weights = refs[:count], refs[count:count + groups]
    act = jnp.concatenate([a[...].reshape(-1, a.shape[2]) for a in acts], 1)
    weight = jnp.concatenate([w[...] for w in weights], 0)
    total = jnp.dot(act, weight, preferred_element_type=jnp.float32)
    if add:
        total = total + refs[count + groups][...].reshape(total.shape)
    out[...] = total.astype(out.dtype).reshape(out.shape)


def project(info, pieces, weights, features, dtype, before=None):
    tokens = pieces[0][2].shape[1]
    tile = min(512, features)
    steps = features // tile
    half = weights[0].shape[0] // 2
    used, specs = [], []
    for group, first, act in pieces:
        wide = act.shape[2]
        per, at = half // wide, first * HD // wide
        used.append(weights[group])
        if group == 0:
            row = lambda s, info, at=at, per=per: (info[0] * per + at, info[2] * steps + s)
        elif group == 1:
            row = lambda s, info, at=at, per=per: ((1 - info[0]) * per + at, info[2] * steps + s)
        else:
            row = lambda s, info, at=at: (at, s)
        specs.append(pl.BlockSpec((wide, tile), row))
    flat = [act for _, _, act in pieces]
    spec = pl.BlockSpec((2, tokens, tile), lambda s, info: (0, 0, s))
    specs = [pl.BlockSpec(a.shape, lambda s, info: (0, 0, 0)) for a in flat] + specs
    operands = flat + used
    if before is not None:
        specs.append(spec)
        operands.append(before)
    depth = sum(a.shape[2] for a in flat)
    return pl.pallas_call(
        lambda *refs: project_kernel(len(flat), len(used), before is not None, *refs),
        grid_spec=pltpu.PrefetchScalarGridSpec(
            num_scalar_prefetch=1, grid=(steps,), in_specs=specs, out_specs=spec
        ),
        out_shape=jax.ShapeDtypeStruct((2, tokens, features), dtype),
        compiler_params=pltpu.CompilerParams(vmem_limit_bytes=40 * 1024 * 1024),
        cost_estimate=pl.CostEstimate(
            flops=2 * 2 * tokens * depth * features // 8,
            bytes_accessed=2 * depth * features // 8,
            transcendentals=0,
        ),
    )(info, *operands)


def on_device(queries, keys_values, block_mask, out_weight):
    tokens = queries.shape[1]
    n, f = lax.axis_size("ctx"), lax.axis_size("fsdp")
    index, place = lax.axis_index("ctx"), lax.axis_index("fsdp")
    core, side = index % 2, (index // 2) % 2
    info = jnp.stack([core, side, place]).astype(jnp.int32)
    width = queries.shape[2] // 2
    heads_half = width // HD
    rows = tokens // BLK
    features = out_weight.shape[1] // f
    bf16 = jnp.bfloat16
    shares = [[0, 1], [2, 3]] if heads_half == 4 else [[h] for h in range(heads_half)]

    pair = lambda i: i ^ 1
    ahead = lambda i: i + 4 if i + 4 < n else None
    across = lambda i: i ^ 2
    upper = lambda i: i + 2 if i & 2 == 0 else None
    lower = lambda i: i - 2 if i & 2 else None
    lanes = lambda start, size: pl.ds(pl.multiple_of(start, HD), size)

    got = moved(keys_values, n, pair)
    there = moved(queries, n, pair)

    def cut_panels(core, place, ins, outs):
        pieces = []
        for r in range(1, f):
            column = pl.multiple_of(lax.rem(place + r, f) * features, HD)
            for p in range(cuts):
                row = pl.multiple_of(core * width + p * (width // cuts), width // cuts)
                at = pl.ds(p * (width // cuts), width // cuts)
                pieces.append((ins[0].at[pl.ds(row, width // cuts), pl.ds(column, features)],
                               [(slice(None), outs[r - 1].at[at])]))
        return pieces

    cuts = 4 if f == 2 else 1
    panels = copies(
        info, [out_weight], [jax.ShapeDtypeStruct((width, features), bf16)] * (f - 1),
        [(width // cuts, features)] * (cuts * (f - 1)), cut_panels,
    )

    def join(core, ins, outs):
        pieces = []
        for slot, source in enumerate(ins[:2]):
            for head_at, target in outs:
                wide = target.shape[-1]
                here = lanes(core * width + head_at * HD, wide)
                pieces.append((source.at[:, 0, :, here], [(slice(None), target.at[slot])]))
        return pieces

    pair_shape = lambda heads: jax.ShapeDtypeStruct((2, 2, tokens, heads * HD), bf16)
    held = lambda heads: (2, tokens, heads * HD)
    first, = copies(
        info, [keys_values, got], [pair_shape(1)], [held(1)] * 2,
        lambda core, place, ins, outs: join(core, ins, [(0, outs[0])]),
    )
    one = moved(first, n, ahead)
    whole, *rest = copies(
        info, [keys_values, got, first], [pair_shape(heads_half)] + [pair_shape(1)] * (heads_half - 1),
        [held(heads_half)] + [held(1)] * (heads_half - 1) + [held(heads_half)]
        + [held(1)] * (heads_half - 1),
        lambda core, place, ins, outs: join(
            core, ins,
            [(0, outs[0])] + [(h, outs[h]) for h in range(1, heads_half)]),
    )
    own = [first] + rest

    sames = [
        moved_both(panel, n, f, lambda i, k: (i, (k + r) % f))
        for r, panel in enumerate(panels, 1)
    ]

    blocks = []
    for h in range(heads_half):
        last = blocks[-1] if blocks else None
        in_turn = lambda array, k: behind(array, last[k]) if last else array
        if h:
            one = moved(behind(own[h], blocks[-2][0]) if h > 1 else own[h], n, ahead)
        two = moved(in_turn(one, 1), n, ahead)
        swap = moved(in_turn(one, 2), n, across)
        far = moved(in_turn(two, 3), n, lower)
        blocks.append((one, two, swap, far))
    low = moved(whole, n, upper)
    mask_there = moved(behind(block_mask, first), n, pair)
    table = jnp.stack([
        mask_table(index * rows, rows, block_mask),
        mask_table((index ^ 1) * rows, rows, mask_there),
    ])

    acts = [[] for _ in range(2 * f)]
    ties = []
    for k, share in enumerate(shares):
        final = k == len(shares) - 1
        into = ()
        for run in [[h] for h in share] if final else [share]:
            after = ([blocks[-1][0], blocks[-2][1]] if not final else [blocks[-1][1]]) \
                if run[-1] < heads_half - 1 else [a[0] for a in acts[1:] if a]
            mine, give, tie = attend(
                info, queries, keys_values, there, got, whole, low,
                [blocks[h] for h in run], table, run[0], heads_half,
                len(share), run[0] - share[0], into, after + ties[-1:],
            )
            into = (mine, give)
            ties.append(tie)
        acts[0].append(mine)
        for r in range(1, f):
            acts[2 * r].append(moved_both(mine, n, f, lambda i, k: (i, (k + r) % f)))
            acts[2 * r + 1].append(moved_both(give, n, f, lambda i, k: (i ^ 1, (k + r) % f)))
        acts[1].append(moved(give, n, pair))
    others = []
    for same in sames:
        same = gated(same, ties[-1])
        others += [same, moved(same, n, pair)]

    weights = [out_weight, out_weight] + others
    early, late = [], []
    for g in range(2 * f):
        for k, (share, act) in enumerate(zip(shares, acts[g])):
            (late if g and k == len(shares) - 1 else early).append((g, share[0], act))
    before = project(info, early, weights, features, jnp.float32)
    return project(info, late, weights, features, jnp.bfloat16, before)


def solution(mesh):
    in_specs = (
        P(None, "ctx", "fsdp"),
        P(None, None, "ctx", "fsdp"),
        P("ctx", None),
        P("fsdp", None),
    )
    out_specs = P(None, "ctx", "fsdp")
    return jax.shard_map(
        on_device, mesh=mesh, in_specs=in_specs, out_specs=out_specs, check_vma=False
    )
```

```python
import math

import jax
import jax.numpy as jnp
from jax import lax
from jax.experimental import pallas as pl
from jax.experimental.pallas import tpu as pltpu
from jax.sharding import PartitionSpec as P

HD = 128
BLK = 64
WINB = 32
MASKED = -1e30
SCALE = math.log2(math.e) / math.sqrt(HD)
VMEM = 60 * 1024 * 1024


def moved(array, n, go, name):
    pairs = [(i, go(i)) for i in range(n) if go(i) is not None]
    with jax.named_scope(name):
        return lax.ppermute(array, "ctx", pairs)


def moved_both(array, n, f, go, name):
    pairs = [(i * f + k, go(i, k)[0] * f + go(i, k)[1]) for i in range(n) for k in range(f)]
    with jax.named_scope(name):
        return lax.ppermute(array, ("ctx", "fsdp"), pairs)


def behind(array, *others):
    return lax.optimization_barrier((array,) + others)[0] if others else array


def gated(arrays, *ties):
    some = pl.BlockSpec(memory_space=pl.ANY)
    return pl.pallas_call(
        lambda *refs: None,
        in_specs=[some] * (len(arrays) + len(ties)),
        out_specs=[some] * len(arrays),
        out_shape=[jax.ShapeDtypeStruct(a.shape, a.dtype) for a in arrays],
        input_output_aliases={k: k for k in range(len(arrays))},
        compiler_params=pltpu.CompilerParams(vmem_limit_bytes=VMEM),
        cost_estimate=pl.CostEstimate(flops=0, bytes_accessed=0, transcendentals=0),
    )(*arrays, *ties)


def mask_table(first_block, rows, mask_rows):
    count = WINB + rows
    query = jnp.arange(rows)
    gap = WINB + query[None, :] - jnp.arange(count)[:, None]
    present = (first_block - WINB + jnp.arange(count) >= 0)[:, None]
    clean = (gap >= 0) & (gap < WINB) & present
    offsets = jnp.arange(WINB)
    picked = ((gap - 1)[:, :, None] == offsets[None, None, :]) & (mask_rows[None] == 1)
    noisy = jnp.any(picked, axis=2) & present
    own_clean = jnp.zeros((rows, rows), bool)
    own_noisy = jnp.eye(rows, dtype=bool)
    allowed = jnp.concatenate(
        [jnp.concatenate([clean, noisy], 1), jnp.concatenate([own_clean, own_noisy], 1)], 0
    )
    table = jnp.where(allowed, 0.0, MASKED).astype(jnp.float32)
    table = jnp.concatenate([table, jnp.ones((count + rows, 1), jnp.float32)], 1)
    return jnp.pad(table, ((0, 0), (0, HD - table.shape[1])))


def copies(info, sources, outs, shapes, plan):
    total = sum(math.prod(o.shape) for o in outs)

    def kernel(info, *refs):
        ins, rest = refs[:len(sources)], refs[len(sources):]
        pieces = plan(info[0], info[2], ins, rest[:len(outs)])
        room, arrive, leave = rest[len(outs):-2], rest[-2], rest[-1]
        reads = [
            pltpu.make_async_copy(source, held, arrive.at[k])
            for k, ((source, _), held) in enumerate(zip(pieces, room))
        ]
        for read in reads:
            read.start()
        writes = []
        for read, (_, targets), held in zip(reads, pieces, room):
            read.wait()
            for part, target in targets:
                write = pltpu.make_async_copy(held.at[part], target, leave.at[len(writes)])
                write.start()
                writes.append(write)
        for write in writes:
            write.wait()

    return pl.pallas_call(
        kernel,
        grid_spec=pltpu.PrefetchScalarGridSpec(
            num_scalar_prefetch=1,
            grid=(),
            in_specs=[pl.BlockSpec(memory_space=pl.ANY)] * len(sources),
            out_specs=[pl.BlockSpec(memory_space=pl.ANY)] * len(outs),
            scratch_shapes=[
                *[pltpu.VMEM(shape, jnp.bfloat16) for shape in shapes],
                pltpu.SemaphoreType.DMA((len(shapes),)),
                pltpu.SemaphoreType.DMA((32,)),
            ],
        ),
        out_shape=[jax.ShapeDtypeStruct(o.shape, o.dtype) for o in outs],
        compiler_params=pltpu.CompilerParams(vmem_limit_bytes=VMEM),
        cost_estimate=pl.CostEstimate(flops=0, bytes_accessed=total, transcendentals=0),
    )(info, *sources)


def attend_kernel(tokens, count, info, *refs):
    core, side = info[0], info[1]
    ins, refs = refs[:4 * count + 2 * count + 4], refs[-7:]
    views, pairs, blocks = ins[:4 * count], ins[4 * count:6 * count], ins[6 * count:]
    table, mine, give, tie, keys, values, least = refs
    tie[...] = jnp.zeros_like(tie)
    rows = tokens // BLK
    span = WINB * BLK + tokens
    back = WINB * BLK // (2 * tokens)

    def place(head, ref, pair, lanes):
        for slot in range(2):
            half = core if slot == 0 else 1 - core
            at = pl.multiple_of(pair * 2 * tokens + half * tokens, tokens)
            keys[head, pl.ds(at, tokens), :] = ref[slot, 0, :, lanes]
            values[head, pl.ds(at, tokens), :] = ref[slot, 1, :, lanes]

    one, two, swap, far = blocks
    for head in range(count):
        lanes = slice(head * HD, (head + 1) * HD)
        place(head, two, 0, lanes)
        place(head, one, 2, lanes)
        place(head, swap, jnp.where(side == 0, 3, 1), lanes)
        place(head, pairs[2 * head], back, slice(None))

    @pl.when(side == 0)
    def _():
        for head in range(count):
            place(head, far, 1, slice(head * HD, (head + 1) * HD))

    @pl.when(side != 0)
    def _():
        for head in range(count):
            place(head, pairs[2 * head + 1], 3, slice(None))

    spot = lax.broadcasted_iota(jnp.int32, (2 * tokens, HD), 0) // BLK
    lane = lax.broadcasted_iota(jnp.int32, (2 * tokens, HD), 1)
    hot = jnp.where(spot == lane, 1.0, 0.0)
    contract = (((1,), (1,)), ((), ()))
    step = tokens
    tiles = (span + tokens) // step

    def operands(head, tile):
        half = core if tile == 0 else 1 - core
        q_ref, n_ref = views[4 * head + 2 * tile:4 * head + 2 * tile + 2]
        query = q_ref[...].reshape(2 * tokens, HD)
        key, value = [], []
        for k in range(tiles):
            at = pl.multiple_of((half + k) * tokens, tokens)
            if k == tiles - 1:
                key.append(n_ref[0, 0])
                value.append(n_ref[1, 0])
            else:
                key.append(keys[head, pl.ds(at, step), :])
                value.append(values[head, pl.ds(at, step), :])
        bias = [
            jnp.broadcast_to(
                table[tile, k * rows:(k + 1) * rows][:, None, :], (rows, BLK, HD)
            ).reshape(step, HD).astype(jnp.bfloat16)
            for k in range(tiles)
        ]
        return query, key, bias, value

    def store(head, tile, out):
        lanes = slice(head * HD, (head + 1) * HD)
        (mine if tile == 0 else give)[:, :, lanes] = out.astype(jnp.bfloat16).reshape(
            2, tokens, HD)

    shift_lane = 2 * rows
    jobs = [(head, tile) for head in range(count) for tile in range(2)]
    low_sum = None
    for head, tile in jobs:
        query, key, bias, value = operands(head, tile)
        wide = query.astype(jnp.float32)
        longest = None
        for k in key:
            k = k.astype(jnp.float32)
            size = jnp.max(jnp.sum(k * k, axis=1, keepdims=True), axis=0, keepdims=True)
            longest = size if longest is None else jnp.maximum(longest, size)
        bound = jnp.sqrt(jnp.sum(wide * wide, axis=1, keepdims=True) * longest)
        extra = jnp.where(lane == shift_lane, -bound, hot).astype(jnp.bfloat16)
        query = jnp.concatenate([query, extra], 1)
        parts = []
        for k in range(tiles):
            scores = lax.dot_general(
                query, jnp.concatenate([key[k], bias[k]], 1), contract,
                preferred_element_type=jnp.float32,
            )
            parts.append(jnp.exp2(scores * SCALE).astype(jnp.bfloat16))
        expo = jnp.concatenate(parts, 1)
        value = jnp.concatenate(value, 0)
        value = jnp.concatenate([value, jnp.ones_like(value)], 1)
        total = jnp.dot(expo, value, preferred_element_type=jnp.float32)
        sums = total[:, HD:]
        store(head, tile, total[:, :HD] / sums)
        smallest = jnp.min(sums.reshape(-1, 8, HD), axis=0)
        low_sum = smallest if low_sum is None else jnp.minimum(low_sum, smallest)
    least[...] = low_sum

    @pl.when(jnp.logical_not(jnp.min(least[...]) > 2.0 ** -40))
    def _():
        for head, tile in jobs:
            query, key, bias, value = operands(head, tile)
            query = jnp.concatenate([query, hot.astype(jnp.bfloat16)], 1)
            key = jnp.concatenate(
                [jnp.concatenate(key, 0), jnp.concatenate(bias, 0)], 1)
            scores = lax.dot_general(query, key, contract, preferred_element_type=jnp.float32)
            top = jnp.max(scores, axis=1, keepdims=True)
            expo = jnp.exp2((scores - top) * SCALE).astype(jnp.bfloat16)
            value = jnp.concatenate(value, 0)
            value = jnp.concatenate([value, jnp.ones_like(value)], 1)
            total = jnp.dot(expo, value, preferred_element_type=jnp.float32)
            store(head, tile, total[:, :HD] / total[:, HD:])


def attend(info, queries, keys_values, there, got, own, low, blocks, table, part, heads_half, after):
    tokens = queries.shape[1]
    span = WINB * BLK + 2 * tokens
    count = len(part)
    wide = count * HD
    views, view_specs, pairs, pair_specs = [], [], [], []
    for head in part:
        here = lambda s, info, head=head: (0, 0, info[0] * heads_half + head)
        noisy = lambda s, info, head=head: (0, 1, 0, info[0] * heads_half + head)
        views += [queries, keys_values, there, got]
        view_specs += [
            pl.BlockSpec((2, tokens, HD), here), pl.BlockSpec((2, 1, tokens, HD), noisy)
        ] * 2
        pairs += [own, low]
        pair_specs += [
            pl.BlockSpec((2, 2, tokens, HD), lambda s, info, head=head: (0, 0, 0, head))] * 2
    out_spec = pl.BlockSpec((2, tokens, wide), lambda s, info: (0, 0, 0))
    out = jax.ShapeDtypeStruct((2, tokens, wide), jnp.bfloat16)
    work = count * 2 * 2 * tokens * span
    return pl.pallas_call(
        lambda *refs: attend_kernel(tokens, count, *refs),
        grid_spec=pltpu.PrefetchScalarGridSpec(
            num_scalar_prefetch=1,
            grid=(1,),
            in_specs=[
                *view_specs, *pair_specs,
                *[pl.BlockSpec((2, 2, tokens, wide), lambda s, info: (0, 0, 0, 0))] * 4,
                *[pl.BlockSpec(memory_space=pl.ANY)] * len(after),
                pl.BlockSpec(table.shape, lambda s, info: (0, 0, 0)),
            ],
            out_specs=[out_spec, out_spec, pl.BlockSpec((8, HD), lambda s, info: (0, 0))],
            scratch_shapes=[
                pltpu.VMEM((count, span, HD), jnp.bfloat16),
                pltpu.VMEM((count, span, HD), jnp.bfloat16),
                pltpu.VMEM((8, HD), jnp.float32),
            ],
        ),
        out_shape=[out, out, jax.ShapeDtypeStruct((8, HD), jnp.float32)],
        compiler_params=pltpu.CompilerParams(vmem_limit_bytes=VMEM),
        cost_estimate=pl.CostEstimate(
            flops=work * 8, bytes_accessed=count * 64 * 1024, transcendentals=0
        ),
    )(info, *views, *pairs, *blocks, *after, table)


def project_kernel(count, groups, add, info, *refs):
    out = refs[-1]
    acts, weights = refs[:count], refs[count:count + groups]
    act = jnp.concatenate([a[...].reshape(-1, a.shape[2]) for a in acts], 1)
    weight = jnp.concatenate([w[...] for w in weights], 0)
    total = jnp.dot(act, weight, preferred_element_type=jnp.float32)
    if add:
        total = total + refs[count + groups][...].reshape(total.shape)
    out[...] = total.astype(out.dtype).reshape(out.shape)


def project(info, pieces, weights, features, dtype, before=None):
    tokens = pieces[0][2].shape[1]
    tile = min(512, features)
    steps = features // tile
    half = weights[0].shape[0] // 2
    used, specs = [], []
    for group, first, act in pieces:
        wide = act.shape[2] if first * HD % act.shape[2] == 0 else HD
        per = half // wide
        for at in range(first * HD // wide, (first * HD + act.shape[2]) // wide):
            used.append(weights[group])
            if group == 0:
                row = lambda s, info, at=at, per=per: (info[0] * per + at, info[2] * steps + s)
            elif group == 1:
                row = lambda s, info, at=at, per=per: (
                    (1 - info[0]) * per + at, info[2] * steps + s)
            else:
                row = lambda s, info, at=at: (at, s)
            specs.append(pl.BlockSpec((wide, tile), row))
    flat = [act for _, _, act in pieces]
    spec = pl.BlockSpec((2, tokens, tile), lambda s, info: (0, 0, s))
    specs = [pl.BlockSpec(a.shape, lambda s, info: (0, 0, 0)) for a in flat] + specs
    operands = flat + used
    if before is not None:
        specs.append(spec)
        operands.append(before)
    depth = sum(a.shape[2] for a in flat)
    return pl.pallas_call(
        lambda *refs: project_kernel(len(flat), len(used), before is not None, *refs),
        grid_spec=pltpu.PrefetchScalarGridSpec(
            num_scalar_prefetch=1, grid=(steps,), in_specs=specs, out_specs=spec
        ),
        out_shape=jax.ShapeDtypeStruct((2, tokens, features), dtype),
        compiler_params=pltpu.CompilerParams(vmem_limit_bytes=40 * 1024 * 1024),
        cost_estimate=pl.CostEstimate(
            flops=2 * 2 * tokens * depth * features // 8,
            bytes_accessed=2 * depth * features // 8,
            transcendentals=0,
        ),
    )(info, *operands)


def on_device(queries, keys_values, block_mask, out_weight):
    tokens = queries.shape[1]
    n, f = lax.axis_size("ctx"), lax.axis_size("fsdp")
    index, place = lax.axis_index("ctx"), lax.axis_index("fsdp")
    core, side = index % 2, (index // 2) % 2
    info = jnp.stack([core, side, place]).astype(jnp.int32)
    width = queries.shape[2] // 2
    heads_half = width // HD
    rows = tokens // BLK
    features = out_weight.shape[1] // f
    bf16 = jnp.bfloat16
    parts = [[0,1],[2,3]] if heads_half == 4 else [[h] for h in range(heads_half)]

    pair = lambda i: i ^ 1
    ahead = lambda i: i + 4 if i + 4 < n else None
    across = lambda i: i ^ 2
    upper = lambda i: i + 2 if i & 2 == 0 else None
    lower = lambda i: i - 2 if i & 2 else None
    lanes = lambda start, size: pl.ds(pl.multiple_of(start, HD), size)

    got = moved(keys_values, n, pair, "pair_kv")
    there = moved(queries, n, pair, "pair_q")

    def cut_panels(core, place, ins, outs):
        pieces = []
        for r in range(1, f):
            column = pl.multiple_of(lax.rem(place + r, f) * features, HD)
            for p in range(cuts):
                row = pl.multiple_of(core * width + p * (width // cuts), width // cuts)
                at = pl.ds(p * (width // cuts), width // cuts)
                pieces.append((ins[0].at[pl.ds(row, width // cuts), pl.ds(column, features)],
                               [(slice(None), outs[r - 1].at[at])]))
        return pieces

    cuts = 4 if f == 2 else 1
    panels = copies(
        info, [out_weight], [jax.ShapeDtypeStruct((width, features), bf16)] * (f - 1),
        [(width // cuts, features)] * (cuts * (f - 1)), cut_panels,
    )

    def join(core, ins, outs):
        pieces = []
        for slot, source in enumerate(ins[:2]):
            for head_at, target in outs:
                wide = target.shape[-1]
                here = lanes(core * width + head_at * HD, wide)
                pieces.append((source.at[:, 0, :, here], [(slice(None), target.at[slot])]))
        return pieces

    pair_shape = lambda heads: jax.ShapeDtypeStruct((2, 2, tokens, heads * HD), bf16)
    held = lambda heads: (2, tokens, heads * HD)
    sizes = [heads_half] + [len(part) for part in parts]
    whole, *own = copies(
        info, [keys_values, got, *panels], [pair_shape(size) for size in sizes],
        [held(size) for size in sizes] * 2,
        lambda core, place, ins, outs: join(
            core, ins, [(0, outs[0])] + [(p[0], out) for p, out in zip(parts, outs[1:])]),
    )

    sames = [
        moved_both(panel, n, f, lambda i, k: (i, (k + r) % f), "panel")
        for r, panel in enumerate(panels, 1)
    ]

    blocks = []
    for k, mine in enumerate(own):
        one = moved(mine, n, ahead, f"near{k}")
        two = moved(one, n, ahead, f"far{k}")
        blocks.append((one, two, moved(one, n, across, f"nearx{k}"), moved(two, n, lower, f"farx{k}")))
    low = moved(whole, n, upper, "ownx")
    mask_there = moved(block_mask, n, pair, "pair_mask")
    table = jnp.stack([
        mask_table(index * rows, rows, block_mask),
        mask_table((index ^ 1) * rows, rows, mask_there),
    ])

    acts = [[] for _ in range(2 * f)]
    ties = []
    for k, part in enumerate(parts):
        after = []
        mine, give, tie = attend(
            info, queries, keys_values, there, got, whole, low, blocks[k], table,
            part, heads_half, after + ties[-1:],
        )
        ties.append(tie)
        acts[0].append(mine)
        for r in range(1, f):
            acts[2 * r].append(moved_both(mine, n, f, lambda i, k: (i, (k + r) % f), f"same{k}"))
            acts[2 * r + 1].append(moved_both(give, n, f, lambda i, k: (i ^ 1, (k + r) % f), f"cross{k}"))
        acts[1].append(moved(give, n, pair, f"pair{k}"))
    others = []
    for same in sames:
        same, = gated([same], ties[-1])
        others += [same, moved(same, n, pair, "panel_pair")]

    weights = [out_weight, out_weight] + others
    early, late = [], []
    for g in range(2 * f):
        for k, (part, act) in enumerate(zip(parts, acts[g])):
            (late if g and k == len(parts) - 1 else early).append((g, part[0], act))
    before = project(info, early, weights, features, jnp.float32)
    return project(info, late, weights, features, jnp.bfloat16, before)


def solution(mesh):
    in_specs = (
        P(None, "ctx", "fsdp"),
        P(None, None, "ctx", "fsdp"),
        P("ctx", None),
        P("fsdp", None),
    )
    out_specs = P(None, "ctx", "fsdp")
    return jax.shard_map(
        on_device, mesh=mesh, in_specs=in_specs, out_specs=out_specs, check_vma=False
    )
```

```python
import math

import jax
import jax.numpy as jnp
from jax import lax
from jax.experimental import pallas as pl
from jax.experimental.pallas import tpu as pltpu
from jax.sharding import PartitionSpec as P

HD = 128
BLK = 64
WINB = 32
MASKED = -1e30
SCALE = math.log2(math.e) / math.sqrt(HD)
VMEM = 60 * 1024 * 1024


def moved(array, n, go, name):
    pairs = [(i, go(i)) for i in range(n) if go(i) is not None]
    with jax.named_scope(name):
        return lax.ppermute(array, "ctx", pairs)


def moved_both(array, n, f, go, name):
    pairs = [(i * f + k, go(i, k)[0] * f + go(i, k)[1]) for i in range(n) for k in range(f)]
    with jax.named_scope(name):
        return lax.ppermute(array, ("ctx", "fsdp"), pairs)


def behind(array, *others):
    return lax.optimization_barrier((array,) + others)[0] if others else array


def gated(arrays, *ties):
    some = pl.BlockSpec(memory_space=pl.ANY)
    return pl.pallas_call(
        lambda *refs: None,
        in_specs=[some] * (len(arrays) + len(ties)),
        out_specs=[some] * len(arrays),
        out_shape=[jax.ShapeDtypeStruct(a.shape, a.dtype) for a in arrays],
        input_output_aliases={k: k for k in range(len(arrays))},
        compiler_params=pltpu.CompilerParams(vmem_limit_bytes=VMEM),
        cost_estimate=pl.CostEstimate(flops=0, bytes_accessed=0, transcendentals=0),
    )(*arrays, *ties)


def mask_table(first_block, rows, mask_rows):
    count = WINB + rows
    query = jnp.arange(rows)
    gap = WINB + query[None, :] - jnp.arange(count)[:, None]
    present = (first_block - WINB + jnp.arange(count) >= 0)[:, None]
    clean = (gap >= 0) & (gap < WINB) & present
    offsets = jnp.arange(WINB)
    picked = ((gap - 1)[:, :, None] == offsets[None, None, :]) & (mask_rows[None] == 1)
    noisy = jnp.any(picked, axis=2) & present
    own_clean = jnp.zeros((rows, rows), bool)
    own_noisy = jnp.eye(rows, dtype=bool)
    allowed = jnp.concatenate(
        [jnp.concatenate([clean, noisy], 1), jnp.concatenate([own_clean, own_noisy], 1)], 0
    )
    table = jnp.where(allowed, 0.0, MASKED).astype(jnp.float32)
    table = jnp.concatenate([table, jnp.ones((count + rows, 1), jnp.float32)], 1)
    return jnp.pad(table, ((0, 0), (0, HD - table.shape[1])))


def copies(info, sources, outs, shapes, plan):
    total = sum(math.prod(o.shape) for o in outs)

    def kernel(info, *refs):
        ins, rest = refs[:len(sources)], refs[len(sources):]
        pieces = plan(info[0], info[2], ins, rest[:len(outs)])
        room, arrive, leave = rest[len(outs):-2], rest[-2], rest[-1]
        reads = [
            pltpu.make_async_copy(source, held, arrive.at[k])
            for k, ((source, _), held) in enumerate(zip(pieces, room))
        ]
        for read in reads:
            read.start()
        writes = []
        for read, (_, targets), held in zip(reads, pieces, room):
            read.wait()
            for part, target in targets:
                write = pltpu.make_async_copy(held.at[part], target, leave.at[len(writes)])
                write.start()
                writes.append(write)
        for write in writes:
            write.wait()

    return pl.pallas_call(
        kernel,
        grid_spec=pltpu.PrefetchScalarGridSpec(
            num_scalar_prefetch=1,
            grid=(),
            in_specs=[pl.BlockSpec(memory_space=pl.ANY)] * len(sources),
            out_specs=[pl.BlockSpec(memory_space=pl.ANY)] * len(outs),
            scratch_shapes=[
                *[pltpu.VMEM(shape, jnp.bfloat16) for shape in shapes],
                pltpu.SemaphoreType.DMA((len(shapes),)),
                pltpu.SemaphoreType.DMA((32,)),
            ],
        ),
        out_shape=[jax.ShapeDtypeStruct(o.shape, o.dtype) for o in outs],
        compiler_params=pltpu.CompilerParams(vmem_limit_bytes=VMEM),
        cost_estimate=pl.CostEstimate(flops=0, bytes_accessed=total, transcendentals=0),
    )(info, *sources)


def attend_kernel(tokens, count, info, *refs):
    core, side = info[0], info[1]
    ins, refs = refs[:4 * count + 2 * count + 4], refs[-7:]
    views, pairs, blocks = ins[:4 * count], ins[4 * count:6 * count], ins[6 * count:]
    table, mine, give, tie, keys, values, least = refs
    tie[...] = jnp.zeros_like(tie)
    rows = tokens // BLK
    span = WINB * BLK + tokens
    back = WINB * BLK // (2 * tokens)

    def place(head, ref, pair, lanes):
        for slot in range(2):
            half = core if slot == 0 else 1 - core
            at = pl.multiple_of(pair * 2 * tokens + half * tokens, tokens)
            keys[head, pl.ds(at, tokens), :] = ref[slot, 0, :, lanes]
            values[head, pl.ds(at, tokens), :] = ref[slot, 1, :, lanes]

    one, two, swap, far = blocks
    for head in range(count):
        lanes = slice(head * HD, (head + 1) * HD)
        place(head, two, 0, lanes)
        place(head, one, 2, lanes)
        place(head, swap, jnp.where(side == 0, 3, 1), lanes)
        place(head, pairs[2 * head], back, slice(None))

    @pl.when(side == 0)
    def _():
        for head in range(count):
            place(head, far, 1, slice(head * HD, (head + 1) * HD))

    @pl.when(side != 0)
    def _():
        for head in range(count):
            place(head, pairs[2 * head + 1], 3, slice(None))

    spot = lax.broadcasted_iota(jnp.int32, (2 * tokens, HD), 0) // BLK
    lane = lax.broadcasted_iota(jnp.int32, (2 * tokens, HD), 1)
    hot = jnp.where(spot == lane, 1.0, 0.0)
    contract = (((1,), (1,)), ((), ()))
    step = tokens
    tiles = (span + tokens) // step

    def operands(head, tile):
        half = core if tile == 0 else 1 - core
        q_ref, n_ref = views[4 * head + 2 * tile:4 * head + 2 * tile + 2]
        query = q_ref[...].reshape(2 * tokens, HD)
        key, value = [], []
        for k in range(tiles):
            at = pl.multiple_of((half + k) * tokens, tokens)
            if k == tiles - 1:
                key.append(n_ref[0, 0])
                value.append(n_ref[1, 0])
            else:
                key.append(keys[head, pl.ds(at, step), :])
                value.append(values[head, pl.ds(at, step), :])
        bias = [
            jnp.broadcast_to(
                table[tile, k * rows:(k + 1) * rows][:, None, :], (rows, BLK, HD)
            ).reshape(step, HD).astype(jnp.bfloat16)
            for k in range(tiles)
        ]
        return query, key, bias, value

    def store(head, tile, out):
        lanes = slice(head * HD, (head + 1) * HD)
        (mine if tile == 0 else give)[:, :, lanes] = out.astype(jnp.bfloat16).reshape(
            2, tokens, HD)

    shift_lane = 2 * rows
    ones = jnp.ones((HD, HD), jnp.bfloat16)
    squares = lambda x: jnp.dot(x * x, ones, preferred_element_type=jnp.float32)
    jobs = [(head, tile) for head in range(count) for tile in range(2)]
    low_sum = None
    for head in range(count):
        longest = None
        for k in range(span // step + 1):
            size = squares(keys[head, k * step:(k + 1) * step, :])
            longest = size if longest is None else jnp.maximum(longest, size)
        for tile in range(2):
            longest = jnp.maximum(longest, squares(views[4 * head + 2 * tile + 1][0, 0]))
        longest = jnp.max(longest, axis=0, keepdims=True) * 1.03
        for tile in range(2):
            query, key, bias, value = operands(head, tile)
            bound = jnp.sqrt(squares(query) * longest)
            extra = jnp.where(lane == shift_lane, -bound, hot).astype(jnp.bfloat16)
            query = jnp.concatenate([query, extra], 1)
            parts = []
            for k in range(tiles):
                scores = lax.dot_general(
                    query, jnp.concatenate([key[k], bias[k]], 1), contract,
                    preferred_element_type=jnp.float32,
                )
                parts.append(jnp.exp2(scores * SCALE).astype(jnp.bfloat16))
            expo = jnp.concatenate(parts, 1)
            value = jnp.concatenate(value, 0)
            value = jnp.concatenate([value, jnp.ones_like(value)], 1)
            total = jnp.dot(expo, value, preferred_element_type=jnp.float32)
            sums = total[:, HD:]
            store(head, tile, total[:, :HD] / sums)
            smallest = jnp.min(sums.reshape(-1, 8, HD), axis=0)
            low_sum = smallest if low_sum is None else jnp.minimum(low_sum, smallest)
    least[...] = low_sum

    @pl.when(jnp.logical_not(jnp.min(least[...]) > 2.0 ** -40))
    def _():
        for head, tile in jobs:
            query, key, bias, value = operands(head, tile)
            query = jnp.concatenate([query, hot.astype(jnp.bfloat16)], 1)
            key = jnp.concatenate(
                [jnp.concatenate(key, 0), jnp.concatenate(bias, 0)], 1)
            scores = lax.dot_general(query, key, contract, preferred_element_type=jnp.float32)
            top = jnp.max(scores, axis=1, keepdims=True)
            expo = jnp.exp2((scores - top) * SCALE).astype(jnp.bfloat16)
            value = jnp.concatenate(value, 0)
            value = jnp.concatenate([value, jnp.ones_like(value)], 1)
            total = jnp.dot(expo, value, preferred_element_type=jnp.float32)
            store(head, tile, total[:, :HD] / total[:, HD:])


def attend(info, queries, keys_values, there, got, own, low, blocks, table, part, heads_half, after):
    tokens = queries.shape[1]
    span = WINB * BLK + 2 * tokens
    count = len(part)
    wide = count * HD
    views, view_specs, pairs, pair_specs = [], [], [], []
    for head in part:
        here = lambda s, info, head=head: (0, 0, info[0] * heads_half + head)
        noisy = lambda s, info, head=head: (0, 1, 0, info[0] * heads_half + head)
        views += [queries, keys_values, there, got]
        view_specs += [
            pl.BlockSpec((2, tokens, HD), here), pl.BlockSpec((2, 1, tokens, HD), noisy)
        ] * 2
        pairs += [own, low]
        pair_specs += [
            pl.BlockSpec((2, 2, tokens, HD), lambda s, info, head=head: (0, 0, 0, head))] * 2
    out_spec = pl.BlockSpec((2, tokens, wide), lambda s, info: (0, 0, 0))
    out = jax.ShapeDtypeStruct((2, tokens, wide), jnp.bfloat16)
    work = count * 2 * 2 * tokens * span
    return pl.pallas_call(
        lambda *refs: attend_kernel(tokens, count, *refs),
        grid_spec=pltpu.PrefetchScalarGridSpec(
            num_scalar_prefetch=1,
            grid=(1,),
            in_specs=[
                *view_specs, *pair_specs,
                *[pl.BlockSpec((2, 2, tokens, wide), lambda s, info: (0, 0, 0, 0))] * 4,
                *[pl.BlockSpec(memory_space=pl.ANY)] * len(after),
                pl.BlockSpec(table.shape, lambda s, info: (0, 0, 0)),
            ],
            out_specs=[out_spec, out_spec, pl.BlockSpec((8, HD), lambda s, info: (0, 0))],
            scratch_shapes=[
                pltpu.VMEM((count, span, HD), jnp.bfloat16),
                pltpu.VMEM((count, span, HD), jnp.bfloat16),
                pltpu.VMEM((8, HD), jnp.float32),
            ],
        ),
        out_shape=[out, out, jax.ShapeDtypeStruct((8, HD), jnp.float32)],
        compiler_params=pltpu.CompilerParams(vmem_limit_bytes=VMEM),
        cost_estimate=pl.CostEstimate(
            flops=work * 8, bytes_accessed=count * 64 * 1024, transcendentals=0
        ),
    )(info, *views, *pairs, *blocks, *after, table)


def project_kernel(count, groups, add, info, *refs):
    out = refs[-1]
    acts, weights = refs[:count], refs[count:count + groups]
    act = jnp.concatenate([a[...].reshape(-1, a.shape[2]) for a in acts], 1)
    weight = jnp.concatenate([w[...] for w in weights], 0)
    total = jnp.dot(act, weight, preferred_element_type=jnp.float32)
    if add:
        total = total + refs[count + groups][...].reshape(total.shape)
    out[...] = total.astype(out.dtype).reshape(out.shape)


def project(info, pieces, weights, features, dtype, before=None):
    tokens = pieces[0][2].shape[1]
    tile = min(512, features)
    steps = features // tile
    half = weights[0].shape[0] // 2
    used, specs = [], []
    for group, first, act in pieces:
        wide = act.shape[2] if first * HD % act.shape[2] == 0 else HD
        per = half // wide
        for at in range(first * HD // wide, (first * HD + act.shape[2]) // wide):
            used.append(weights[group])
            if group == 0:
                row = lambda s, info, at=at, per=per: (info[0] * per + at, info[2] * steps + s)
            elif group == 1:
                row = lambda s, info, at=at, per=per: (
                    (1 - info[0]) * per + at, info[2] * steps + s)
            else:
                row = lambda s, info, at=at: (at, s)
            specs.append(pl.BlockSpec((wide, tile), row))
    flat = [act for _, _, act in pieces]
    spec = pl.BlockSpec((2, tokens, tile), lambda s, info: (0, 0, s))
    specs = [pl.BlockSpec(a.shape, lambda s, info: (0, 0, 0)) for a in flat] + specs
    operands = flat + used
    if before is not None:
        specs.append(spec)
        operands.append(before)
    depth = sum(a.shape[2] for a in flat)
    return pl.pallas_call(
        lambda *refs: project_kernel(len(flat), len(used), before is not None, *refs),
        grid_spec=pltpu.PrefetchScalarGridSpec(
            num_scalar_prefetch=1, grid=(steps,), in_specs=specs, out_specs=spec
        ),
        out_shape=jax.ShapeDtypeStruct((2, tokens, features), dtype),
        compiler_params=pltpu.CompilerParams(vmem_limit_bytes=40 * 1024 * 1024),
        cost_estimate=pl.CostEstimate(
            flops=2 * 2 * tokens * depth * features // 8,
            bytes_accessed=2 * depth * features // 8,
            transcendentals=0,
        ),
    )(info, *operands)


def on_device(queries, keys_values, block_mask, out_weight):
    tokens = queries.shape[1]
    n, f = lax.axis_size("ctx"), lax.axis_size("fsdp")
    index, place = lax.axis_index("ctx"), lax.axis_index("fsdp")
    core, side = index % 2, (index // 2) % 2
    info = jnp.stack([core, side, place]).astype(jnp.int32)
    width = queries.shape[2] // 2
    heads_half = width // HD
    rows = tokens // BLK
    features = out_weight.shape[1] // f
    bf16 = jnp.bfloat16
    parts = [[0,1],[2,3]] if heads_half == 4 else [[h] for h in range(heads_half)]

    pair = lambda i: i ^ 1
    ahead = lambda i: i + 4 if i + 4 < n else None
    across = lambda i: i ^ 2
    upper = lambda i: i + 2 if i & 2 == 0 else None
    lower = lambda i: i - 2 if i & 2 else None
    lanes = lambda start, size: pl.ds(pl.multiple_of(start, HD), size)

    got = moved(keys_values, n, pair, "pair_kv")
    there = moved(queries, n, pair, "pair_q")

    def cut_panels(core, place, ins, outs):
        pieces = []
        for r in range(1, f):
            column = pl.multiple_of(lax.rem(place + r, f) * features, HD)
            for p in range(cuts):
                row = pl.multiple_of(core * width + p * (width // cuts), width // cuts)
                at = pl.ds(p * (width // cuts), width // cuts)
                pieces.append((ins[0].at[pl.ds(row, width // cuts), pl.ds(column, features)],
                               [(slice(None), outs[r - 1].at[at])]))
        return pieces

    cuts = 4 if f == 2 else 1
    panels = copies(
        info, [out_weight], [jax.ShapeDtypeStruct((width, features), bf16)] * (f - 1),
        [(width // cuts, features)] * (cuts * (f - 1)), cut_panels,
    )

    def join(core, ins, outs):
        pieces = []
        for slot, source in enumerate(ins[:2]):
            for head_at, target in outs:
                wide = target.shape[-1]
                here = lanes(core * width + head_at * HD, wide)
                pieces.append((source.at[:, 0, :, here], [(slice(None), target.at[slot])]))
        return pieces

    pair_shape = lambda heads: jax.ShapeDtypeStruct((2, 2, tokens, heads * HD), bf16)
    held = lambda heads: (2, tokens, heads * HD)
    first, = copies(
        info, [keys_values, got, *panels], [pair_shape(len(parts[0]))], [held(len(parts[0]))] * 2,
        lambda core, place, ins, outs: join(core, ins, [(0, outs[0])]),
    )
    sizes = [heads_half] + [len(part) for part in parts[1:]]
    whole, *rest = copies(
        info, [keys_values, got, first], [pair_shape(size) for size in sizes],
        [held(size) for size in sizes] * 2,
        lambda core, place, ins, outs: join(
            core, ins, [(0, outs[0])] + [(p[0], out) for p, out in zip(parts[1:], outs[1:])]),
    )
    own = [first] + rest

    sames = [
        moved_both(panel, n, f, lambda i, k: (i, (k + r) % f), "panel")
        for r, panel in enumerate(panels, 1)
    ]

    low = moved(whole, n, upper, "ownx")
    blocks = []
    for k, mine in enumerate(own):
        one = moved(mine, n, ahead, f"near{k}")
        swap = moved(one, n, across, f"nearx{k}")
        if k:
            one, = gated([one], blocks[0][2], blocks[0][1])
        two = moved(one, n, ahead, f"far{k}")
        if k:
            two, = gated([two], swap, blocks[0][3], low)
        blocks.append((one, two, swap, moved(two, n, lower, f"farx{k}")))
    mask_there = moved(block_mask, n, pair, "pair_mask")
    table = jnp.stack([
        mask_table(index * rows, rows, block_mask),
        mask_table((index ^ 1) * rows, rows, mask_there),
    ])

    acts = [[] for _ in range(2 * f)]
    ties = []
    for k, part in enumerate(parts):
        after = []
        mine, give, tie = attend(
            info, queries, keys_values, there, got, whole, low, blocks[k], table,
            part, heads_half, after + ties[-1:],
        )
        ties.append(tie)
        acts[0].append(mine)
        for r in range(1, f):
            acts[2 * r].append(moved_both(mine, n, f, lambda i, k: (i, (k + r) % f), f"same{k}"))
            acts[2 * r + 1].append(moved_both(give, n, f, lambda i, k: (i ^ 1, (k + r) % f), f"cross{k}"))
        acts[1].append(moved(give, n, pair, f"pair{k}"))
    others = []
    for same in sames:
        same, = gated([same], blocks[-1][3], ties[0])
        others += [same, moved(same, n, pair, "panel_pair")]

    weights = [out_weight, out_weight] + others
    early, late = [], []
    for g in range(2 * f):
        for k, (part, act) in enumerate(zip(parts, acts[g])):
            (late if g and k == len(parts) - 1 else early).append((g, part[0], act))
    before = project(info, early, weights, features, jnp.float32)
    return project(info, late, weights, features, jnp.bfloat16, before)


def solution(mesh):
    in_specs = (
        P(None, "ctx", "fsdp"),
        P(None, None, "ctx", "fsdp"),
        P("ctx", None),
        P("fsdp", None),
    )
    out_specs = P(None, "ctx", "fsdp")
    return jax.shard_map(
        on_device, mesh=mesh, in_specs=in_specs, out_specs=out_specs, check_vma=False
    )
```

```python
import math

import jax
import jax.numpy as jnp
from jax import lax
from jax.experimental import pallas as pl
from jax.experimental.pallas import tpu as pltpu
from jax.sharding import PartitionSpec as P

HD = 128
BLK = 64
WINB = 32
MASKED = -1e30
SCALE = math.log2(math.e) / math.sqrt(HD)
VMEM = 60 * 1024 * 1024


def moved(array, n, go, name):
    pairs = [(i, go(i)) for i in range(n) if go(i) is not None]
    with jax.named_scope(name):
        return lax.ppermute(array, "ctx", pairs)


def moved_both(array, n, f, go, name):
    pairs = [(i * f + k, go(i, k)[0] * f + go(i, k)[1]) for i in range(n) for k in range(f)]
    with jax.named_scope(name):
        return lax.ppermute(array, ("ctx", "fsdp"), pairs)


def behind(array, *others):
    return lax.optimization_barrier((array,) + others)[0] if others else array


def gated(arrays, *ties):
    some = pl.BlockSpec(memory_space=pl.ANY)
    return pl.pallas_call(
        lambda *refs: None,
        in_specs=[some] * (len(arrays) + len(ties)),
        out_specs=[some] * len(arrays),
        out_shape=[jax.ShapeDtypeStruct(a.shape, a.dtype) for a in arrays],
        input_output_aliases={k: k for k in range(len(arrays))},
        compiler_params=pltpu.CompilerParams(vmem_limit_bytes=VMEM),
        cost_estimate=pl.CostEstimate(flops=0, bytes_accessed=0, transcendentals=0),
    )(*arrays, *ties)


def mask_table(first_block, rows, mask_rows):
    count = WINB + rows
    query = jnp.arange(rows)
    gap = WINB + query[None, :] - jnp.arange(count)[:, None]
    present = (first_block - WINB + jnp.arange(count) >= 0)[:, None]
    clean = (gap >= 0) & (gap < WINB) & present
    offsets = jnp.arange(WINB)
    picked = ((gap - 1)[:, :, None] == offsets[None, None, :]) & (mask_rows[None] == 1)
    noisy = jnp.any(picked, axis=2) & present
    own_clean = jnp.zeros((rows, rows), bool)
    own_noisy = jnp.eye(rows, dtype=bool)
    allowed = jnp.concatenate(
        [jnp.concatenate([clean, noisy], 1), jnp.concatenate([own_clean, own_noisy], 1)], 0
    )
    table = jnp.where(allowed, 0.0, MASKED).astype(jnp.float32)
    table = jnp.concatenate([table, jnp.ones((count + rows, 1), jnp.float32)], 1)
    table = jnp.pad(table, ((0, 0), (0, 16 - table.shape[1]))).astype(jnp.bfloat16)
    table = jnp.repeat(table.reshape(-1, rows, 16).transpose(0, 2, 1), BLK, axis=2)
    return table


def copies(info, sources, outs, shapes, plan):
    total = sum(math.prod(o.shape) for o in outs)

    def kernel(info, *refs):
        ins, rest = refs[:len(sources)], refs[len(sources):]
        pieces = plan(info[0], info[2], ins, rest[:len(outs)])
        room, arrive, leave = rest[len(outs):-2], rest[-2], rest[-1]
        reads = [
            pltpu.make_async_copy(source, held, arrive.at[k])
            for k, ((source, _), held) in enumerate(zip(pieces, room))
        ]
        for read in reads:
            read.start()
        writes = []
        for read, (_, targets), held in zip(reads, pieces, room):
            read.wait()
            for part, target in targets:
                write = pltpu.make_async_copy(held.at[part], target, leave.at[len(writes)])
                write.start()
                writes.append(write)
        for write in writes:
            write.wait()

    return pl.pallas_call(
        kernel,
        grid_spec=pltpu.PrefetchScalarGridSpec(
            num_scalar_prefetch=1,
            grid=(),
            in_specs=[pl.BlockSpec(memory_space=pl.ANY)] * len(sources),
            out_specs=[pl.BlockSpec(memory_space=pl.ANY)] * len(outs),
            scratch_shapes=[
                *[pltpu.VMEM(shape, jnp.bfloat16) for shape in shapes],
                pltpu.SemaphoreType.DMA((len(shapes),)),
                pltpu.SemaphoreType.DMA((32,)),
            ],
        ),
        out_shape=[jax.ShapeDtypeStruct(o.shape, o.dtype) for o in outs],
        compiler_params=pltpu.CompilerParams(vmem_limit_bytes=VMEM),
        cost_estimate=pl.CostEstimate(flops=0, bytes_accessed=total, transcendentals=0),
    )(info, *sources)


def attend_kernel(tokens, info, *refs):
    core, side = info[0], info[1]
    views, pairs, blocks, refs = refs[:4], refs[4:6], refs[6:10], refs[-7:]
    own, low = pairs
    one, two, swap, far = blocks
    table, mine, give, tie, keys, values, least = refs
    tie[...] = jnp.zeros_like(tie)
    rows = tokens // BLK
    slots = WINB * BLK // tokens + 2
    back = WINB * BLK // (2 * tokens)

    def place(ref, pair):
        for slot in range(2):
            half = core if slot == 0 else 1 - core
            keys[pair * 2 + half] = ref[slot, 0].T
            values[pair * 2 + half] = ref[slot, 1]

    place(two, 0)
    place(one, 2)
    place(swap, jnp.where(side == 0, 3, 1))
    place(own, back)

    @pl.when(side == 0)
    def _():
        place(far, 1)

    @pl.when(side != 0)
    def _():
        place(low, 3)

    for tile in range(2):
        keys[slots + tile] = views[2 * tile + 1][0, 0].T

    spot = lax.broadcasted_iota(jnp.int32, (2 * tokens, HD), 0) // BLK
    lane = lax.broadcasted_iota(jnp.int32, (2 * tokens, HD), 1)
    hot = jnp.where(spot == lane, 1.0, 0.0)
    rest = jnp.zeros((HD - table.shape[2], tokens), jnp.bfloat16)

    def operands(tile, k):
        half = core if tile == 0 else 1 - core
        if k == slots - 1:
            key, value = keys[slots + tile], views[2 * tile + 1][1, 0]
        else:
            key, value = keys[half + k], values[half + k]
        return (jnp.concatenate([key, table[tile, k], rest], 0),
                jnp.concatenate([value, jnp.ones_like(value)], 1))

    def store(tile, out):
        (mine if tile == 0 else give)[...] = out.astype(jnp.bfloat16).reshape(2, tokens, HD)

    shift_lane = 2 * rows
    ones = jnp.ones((16, HD), jnp.bfloat16)
    longest = None
    for k in range(slots + 2):
        key = keys[k]
        size = jnp.dot(ones, key * key, preferred_element_type=jnp.float32)
        longest = size if longest is None else jnp.maximum(longest, size)
    longest = jnp.max(longest, axis=1, keepdims=True)[0:1] * 1.03
    low_sum = None
    for tile in range(2):
        query = views[2 * tile][...].reshape(2 * tokens, HD)
        size = jnp.dot(query * query, jnp.ones((HD, HD), jnp.bfloat16),
                       preferred_element_type=jnp.float32)
        bound = jnp.sqrt(size * longest)
        extra = jnp.where(lane == shift_lane, -bound, hot).astype(jnp.bfloat16)
        query = jnp.concatenate([query, extra], 1)
        parts, value = [], []
        for k in range(slots):
            key, val = operands(tile, k)
            scores = jnp.dot(query, key, preferred_element_type=jnp.float32)
            parts.append(jnp.exp2(scores * SCALE).astype(jnp.bfloat16))
            value.append(val)
        total = jnp.dot(jnp.concatenate(parts, 1), jnp.concatenate(value, 0),
                        preferred_element_type=jnp.float32)
        sums = total[:, HD:]
        store(tile, total[:, :HD] / sums)
        smallest = jnp.min(sums.reshape(-1, 8, HD), axis=0)
        low_sum = smallest if low_sum is None else jnp.minimum(low_sum, smallest)
    least[...] = low_sum

    @pl.when(jnp.logical_not(jnp.min(least[...]) > 2.0 ** -40))
    def _():
        for tile in range(2):
            query = views[2 * tile][...].reshape(2 * tokens, HD)
            query = jnp.concatenate([query, hot.astype(jnp.bfloat16)], 1)
            pieces = [operands(tile, k) for k in range(slots)]
            scores = jnp.concatenate(
                [jnp.dot(query, key, preferred_element_type=jnp.float32) for key, _ in pieces], 1)
            top = jnp.max(scores, axis=1, keepdims=True)
            expo = jnp.exp2((scores - top) * SCALE).astype(jnp.bfloat16)
            total = jnp.dot(expo, jnp.concatenate([value for _, value in pieces], 0),
                            preferred_element_type=jnp.float32)
            store(tile, total[:, :HD] / total[:, HD:])


def attend(info, queries, keys_values, there, got, own, low, blocks, table, part, heads_half, after):
    tokens = queries.shape[1]
    slots = WINB * BLK // tokens + 2
    count, first = len(part), part[0]
    here = lambda h, info: (0, 0, info[0] * heads_half + first + h)
    noisy = lambda h, info: (0, 1, 0, info[0] * heads_half + first + h)
    query_spec = pl.BlockSpec((2, tokens, HD), here)
    noisy_spec = pl.BlockSpec((2, 1, tokens, HD), noisy)
    whole = pl.BlockSpec((2, 2, tokens, HD), lambda h, info: (0, 0, 0, first + h))
    chunk = pl.BlockSpec((2, 2, tokens, HD), lambda h, info: (0, 0, 0, h))
    out_spec = pl.BlockSpec((2, tokens, HD), lambda h, info: (0, 0, h))
    out = jax.ShapeDtypeStruct((2, tokens, count * HD), jnp.bfloat16)
    work = count * 2 * 2 * tokens * slots * tokens
    return pl.pallas_call(
        lambda *refs: attend_kernel(tokens, *refs),
        grid_spec=pltpu.PrefetchScalarGridSpec(
            num_scalar_prefetch=1,
            grid=(count,),
            in_specs=[
                query_spec, noisy_spec, query_spec, noisy_spec, whole, whole, *[chunk] * 4,
                *[pl.BlockSpec(memory_space=pl.ANY)] * len(after),
                pl.BlockSpec(table.shape, lambda h, info: (0, 0, 0, 0)),
            ],
            out_specs=[out_spec, out_spec, pl.BlockSpec((8, HD), lambda h, info: (0, 0))],
            scratch_shapes=[
                pltpu.VMEM((slots + 2, HD, tokens), jnp.bfloat16),
                pltpu.VMEM((slots, tokens, HD), jnp.bfloat16),
                pltpu.VMEM((8, HD), jnp.float32),
            ],
        ),
        out_shape=[out, out, jax.ShapeDtypeStruct((8, HD), jnp.float32)],
        compiler_params=pltpu.CompilerParams(vmem_limit_bytes=VMEM),
        cost_estimate=pl.CostEstimate(
            flops=work * 8, bytes_accessed=count * 64 * 1024, transcendentals=0
        ),
    )(info, queries, keys_values, there, got, own, low, *blocks, *after, table)


def project_kernel(count, groups, add, info, *refs):
    out = refs[-1]
    acts, weights = refs[:count], refs[count:count + groups]
    act = jnp.concatenate([a[...].reshape(-1, a.shape[2]) for a in acts], 1)
    weight = jnp.concatenate([w[...] for w in weights], 0)
    total = jnp.dot(act, weight, preferred_element_type=jnp.float32)
    if add:
        total = total + refs[count + groups][...].reshape(total.shape)
    out[...] = total.astype(out.dtype).reshape(out.shape)


def project(info, pieces, weights, features, dtype, before=None):
    tokens = pieces[0][2].shape[1]
    tile = min(512, features)
    steps = features // tile
    half = weights[0].shape[0] // 2
    used, specs = [], []
    for group, first, act in pieces:
        wide = act.shape[2] if first * HD % act.shape[2] == 0 else HD
        per = half // wide
        for at in range(first * HD // wide, (first * HD + act.shape[2]) // wide):
            used.append(weights[group])
            if group == 0:
                row = lambda s, info, at=at, per=per: (info[0] * per + at, info[2] * steps + s)
            elif group == 1:
                row = lambda s, info, at=at, per=per: (
                    (1 - info[0]) * per + at, info[2] * steps + s)
            else:
                row = lambda s, info, at=at: (at, s)
            specs.append(pl.BlockSpec((wide, tile), row))
    flat = [act for _, _, act in pieces]
    spec = pl.BlockSpec((2, tokens, tile), lambda s, info: (0, 0, s))
    specs = [pl.BlockSpec(a.shape, lambda s, info: (0, 0, 0)) for a in flat] + specs
    operands = flat + used
    if before is not None:
        specs.append(spec)
        operands.append(before)
    depth = sum(a.shape[2] for a in flat)
    return pl.pallas_call(
        lambda *refs: project_kernel(len(flat), len(used), before is not None, *refs),
        grid_spec=pltpu.PrefetchScalarGridSpec(
            num_scalar_prefetch=1, grid=(steps,), in_specs=specs, out_specs=spec
        ),
        out_shape=jax.ShapeDtypeStruct((2, tokens, features), dtype),
        compiler_params=pltpu.CompilerParams(vmem_limit_bytes=40 * 1024 * 1024),
        cost_estimate=pl.CostEstimate(
            flops=2 * 2 * tokens * depth * features // 8,
            bytes_accessed=2 * depth * features // 8,
            transcendentals=0,
        ),
    )(info, *operands)


def on_device(queries, keys_values, block_mask, out_weight):
    tokens = queries.shape[1]
    n, f = lax.axis_size("ctx"), lax.axis_size("fsdp")
    index, place = lax.axis_index("ctx"), lax.axis_index("fsdp")
    core, side = index % 2, (index // 2) % 2
    info = jnp.stack([core, side, place]).astype(jnp.int32)
    width = queries.shape[2] // 2
    heads_half = width // HD
    rows = tokens // BLK
    features = out_weight.shape[1] // f
    bf16 = jnp.bfloat16
    parts = [[0,1],[2,3]] if heads_half == 4 else [[h] for h in range(heads_half)]

    pair = lambda i: i ^ 1
    ahead = lambda i: i + 4 if i + 4 < n else None
    across = lambda i: i ^ 2
    upper = lambda i: i + 2 if i & 2 == 0 else None
    lower = lambda i: i - 2 if i & 2 else None
    lanes = lambda start, size: pl.ds(pl.multiple_of(start, HD), size)

    got = moved(keys_values, n, pair, "pair_kv")
    there = moved(queries, n, pair, "pair_q")

    def cut_panels(core, place, ins, outs):
        pieces = []
        for r in range(1, f):
            column = pl.multiple_of(lax.rem(place + r, f) * features, HD)
            for p in range(cuts):
                row = pl.multiple_of(core * width + p * (width // cuts), width // cuts)
                at = pl.ds(p * (width // cuts), width // cuts)
                pieces.append((ins[0].at[pl.ds(row, width // cuts), pl.ds(column, features)],
                               [(slice(None), outs[r - 1].at[at])]))
        return pieces

    cuts = 4 if f == 2 else 1
    panels = copies(
        info, [out_weight], [jax.ShapeDtypeStruct((width, features), bf16)] * (f - 1),
        [(width // cuts, features)] * (cuts * (f - 1)), cut_panels,
    )

    def join(core, ins, outs):
        pieces = []
        for slot, source in enumerate(ins[:2]):
            for head_at, target in outs:
                wide = target.shape[-1]
                here = lanes(core * width + head_at * HD, wide)
                pieces.append((source.at[:, 0, :, here], [(slice(None), target.at[slot])]))
        return pieces

    pair_shape = lambda heads: jax.ShapeDtypeStruct((2, 2, tokens, heads * HD), bf16)
    held = lambda heads: (2, tokens, heads * HD)
    first, = copies(
        info, [keys_values, got, *panels], [pair_shape(len(parts[0]))], [held(len(parts[0]))] * 2,
        lambda core, place, ins, outs: join(core, ins, [(0, outs[0])]),
    )
    sizes = [heads_half] + [len(part) for part in parts[1:]]
    whole, *rest = copies(
        info, [keys_values, got, first], [pair_shape(size) for size in sizes],
        [held(size) for size in sizes] * 2,
        lambda core, place, ins, outs: join(
            core, ins, [(0, outs[0])] + [(p[0], out) for p, out in zip(parts[1:], outs[1:])]),
    )
    own = [first] + rest

    sames = [
        moved_both(panel, n, f, lambda i, k: (i, (k + r) % f), "panel")
        for r, panel in enumerate(panels, 1)
    ]


    blocks = []
    for k, mine in enumerate(own):
        one = moved(mine, n, ahead, f"near{k}")
        swap = moved(one, n, across, f"nearx{k}")
        if k:
            one, = gated([one], blocks[0][2], blocks[0][1])
        two = moved(one, n, ahead, f"far{k}")
        if k:
            two, = gated([two], swap, blocks[0][3])
        blocks.append((one, two, swap, moved(two, n, lower, f"farx{k}")))
        if k == 0:
            spare, = gated([whole], swap)
            low = moved(spare, n, upper, "ownx")
    mask_there = moved(block_mask, n, pair, "pair_mask")
    table = jnp.stack([
        mask_table(index * rows, rows, block_mask),
        mask_table((index ^ 1) * rows, rows, mask_there),
    ])

    acts = [[] for _ in range(2 * f)]
    ties = []
    for k, part in enumerate(parts):
        after = []
        mine, give, tie = attend(
            info, queries, keys_values, there, got, spare, low, blocks[k], table,
            part, heads_half, after + ties[-1:],
        )
        ties.append(tie)
        acts[0].append(mine)
        for r in range(1, f):
            acts[2 * r].append(moved_both(mine, n, f, lambda i, k: (i, (k + r) % f), f"same{k}"))
            acts[2 * r + 1].append(moved_both(give, n, f, lambda i, k: (i ^ 1, (k + r) % f), f"cross{k}"))
        acts[1].append(moved(give, n, pair, f"pair{k}"))
    others = []
    for same in sames:
        same, = gated([same], blocks[-1][3], ties[0])
        others += [same, moved(same, n, pair, "panel_pair")]

    weights = [out_weight, out_weight] + others
    early, late = [], []
    for g in range(2 * f):
        for k, (part, act) in enumerate(zip(parts, acts[g])):
            (late if g and k == len(parts) - 1 else early).append((g, part[0], act))
    before = project(info, early, weights, features, jnp.float32)
    return project(info, late, weights, features, jnp.bfloat16, before)


def solution(mesh):
    in_specs = (
        P(None, "ctx", "fsdp"),
        P(None, None, "ctx", "fsdp"),
        P("ctx", None),
        P("fsdp", None),
    )
    out_specs = P(None, "ctx", "fsdp")
    return jax.shard_map(
        on_device, mesh=mesh, in_specs=in_specs, out_specs=out_specs, check_vma=False
    )
```

```python
import math

import jax
import jax.numpy as jnp
from jax import lax
from jax.experimental import pallas as pl
from jax.experimental.pallas import tpu as pltpu
from jax.sharding import PartitionSpec as P

HD = 128
BLK = 64
WINB = 32
MASKED = -1e30
SCALE = math.log2(math.e) / math.sqrt(HD)
VMEM = 60 * 1024 * 1024


def moved(array, n, go, name):
    pairs = [(i, go(i)) for i in range(n) if go(i) is not None]
    with jax.named_scope(name):
        return lax.ppermute(array, "ctx", pairs)


def moved_both(array, n, f, go, name):
    pairs = [(i * f + k, go(i, k)[0] * f + go(i, k)[1]) for i in range(n) for k in range(f)]
    with jax.named_scope(name):
        return lax.ppermute(array, ("ctx", "fsdp"), pairs)


def behind(array, *others):
    return lax.optimization_barrier((array,) + others)[0] if others else array


def gated(arrays, *ties):
    some = pl.BlockSpec(memory_space=pl.ANY)
    return pl.pallas_call(
        lambda *refs: None,
        in_specs=[some] * (len(arrays) + len(ties)),
        out_specs=[some] * len(arrays),
        out_shape=[jax.ShapeDtypeStruct(a.shape, a.dtype) for a in arrays],
        input_output_aliases={k: k for k in range(len(arrays))},
        compiler_params=pltpu.CompilerParams(vmem_limit_bytes=VMEM),
        cost_estimate=pl.CostEstimate(flops=0, bytes_accessed=0, transcendentals=0),
    )(*arrays, *ties)


def mask_table(first_block, rows, mask_rows):
    count = WINB + rows
    query = jnp.arange(rows)
    gap = WINB + query[None, :] - jnp.arange(count)[:, None]
    present = (first_block - WINB + jnp.arange(count) >= 0)[:, None]
    clean = (gap >= 0) & (gap < WINB) & present
    offsets = jnp.arange(WINB)
    picked = ((gap - 1)[:, :, None] == offsets[None, None, :]) & (mask_rows[None] == 1)
    noisy = jnp.any(picked, axis=2) & present
    own_clean = jnp.zeros((rows, rows), bool)
    own_noisy = jnp.eye(rows, dtype=bool)
    allowed = jnp.concatenate(
        [jnp.concatenate([clean, noisy], 1), jnp.concatenate([own_clean, own_noisy], 1)], 0
    )
    table = jnp.where(allowed, 0.0, MASKED).astype(jnp.float32)
    table = jnp.concatenate([table, jnp.ones((count + rows, 1), jnp.float32)], 1)
    table = jnp.pad(table, ((0, 0), (0, 16 - table.shape[1]))).astype(jnp.bfloat16)
    table = jnp.repeat(table.reshape(-1, rows, 16).transpose(0, 2, 1), BLK, axis=2)
    return table


def copies(info, sources, outs, shapes, plan):
    total = sum(math.prod(o.shape) for o in outs)

    def kernel(info, *refs):
        ins, rest = refs[:len(sources)], refs[len(sources):]
        pieces = plan(info[0], info[2], ins, rest[:len(outs)])
        room, arrive, leave = rest[len(outs):-2], rest[-2], rest[-1]
        reads = [
            pltpu.make_async_copy(source, held, arrive.at[k])
            for k, ((source, _), held) in enumerate(zip(pieces, room))
        ]
        for read in reads:
            read.start()
        writes = []
        for read, (_, targets), held in zip(reads, pieces, room):
            read.wait()
            for part, target in targets:
                write = pltpu.make_async_copy(held.at[part], target, leave.at[len(writes)])
                write.start()
                writes.append(write)
        for write in writes:
            write.wait()

    return pl.pallas_call(
        kernel,
        grid_spec=pltpu.PrefetchScalarGridSpec(
            num_scalar_prefetch=1,
            grid=(),
            in_specs=[pl.BlockSpec(memory_space=pl.ANY)] * len(sources),
            out_specs=[pl.BlockSpec(memory_space=pl.ANY)] * len(outs),
            scratch_shapes=[
                *[pltpu.VMEM(shape, jnp.bfloat16) for shape in shapes],
                pltpu.SemaphoreType.DMA((len(shapes),)),
                pltpu.SemaphoreType.DMA((32,)),
            ],
        ),
        out_shape=[jax.ShapeDtypeStruct(o.shape, o.dtype) for o in outs],
        compiler_params=pltpu.CompilerParams(vmem_limit_bytes=VMEM),
        cost_estimate=pl.CostEstimate(flops=0, bytes_accessed=total, transcendentals=0),
    )(info, *sources)


def attend_kernel(tokens, info, *refs):
    core, side = info[0], info[1]
    views, pairs, blocks, refs = refs[:4], refs[4:6], refs[6:10], refs[-7:]
    own, low = pairs
    one, two, swap, far = blocks
    table, mine, give, tie, keys, values, least = refs
    tie[...] = jnp.zeros_like(tie)
    rows = tokens // BLK
    slots = WINB * BLK // tokens + 2
    back = WINB * BLK // (2 * tokens)

    def place(ref, pair):
        for slot in range(2):
            half = core if slot == 0 else 1 - core
            keys[pair * 2 + half] = ref[slot, 0].T
            values[pair * 2 + half] = ref[slot, 1]

    place(two, 0)
    place(one, 2)
    place(swap, jnp.where(side == 0, 3, 1))
    place(own, back)

    @pl.when(side == 0)
    def _():
        place(far, 1)

    @pl.when(side != 0)
    def _():
        place(low, 3)

    for tile in range(2):
        keys[slots + tile] = views[2 * tile + 1][0, 0].T

    spot = lax.broadcasted_iota(jnp.int32, (2 * tokens, HD), 0) // BLK
    lane = lax.broadcasted_iota(jnp.int32, (2 * tokens, HD), 1)
    hot = jnp.where(spot == lane, 1.0, 0.0)
    rest = jnp.zeros((HD - table.shape[2], tokens), jnp.bfloat16)

    def operands(tile, k):
        half = core if tile == 0 else 1 - core
        if k == slots - 1:
            key, value = keys[slots + tile], views[2 * tile + 1][1, 0]
        else:
            key, value = keys[half + k], values[half + k]
        return (jnp.concatenate([key, table[tile, k], rest], 0),
                jnp.concatenate([value, jnp.ones_like(value)], 1))

    def store(tile, out):
        (mine if tile == 0 else give)[...] = out.astype(jnp.bfloat16).reshape(2, tokens, HD)

    shift_lane = 2 * rows
    ones = jnp.ones((16, HD), jnp.bfloat16)
    longest = None
    for k in range(slots + 2):
        key = keys[k]
        size = jnp.dot(ones, key * key, preferred_element_type=jnp.float32)
        longest = size if longest is None else jnp.maximum(longest, size)
    longest = jnp.max(longest, axis=1, keepdims=True)[0:1] * 1.03
    queries = []
    for tile in range(2):
        query = views[2 * tile][...].reshape(2 * tokens, HD)
        size = jnp.dot(query * query, jnp.ones((HD, HD), jnp.bfloat16),
                       preferred_element_type=jnp.float32)
        bound = jnp.sqrt(size * longest)
        extra = jnp.where(lane == shift_lane, -bound, hot).astype(jnp.bfloat16)
        queries.append(jnp.concatenate([query, extra], 1))

    steps = [(tile, k) for tile in range(2) for k in range(0, slots, 2)]
    totals = [None, None]

    def scores_of(tile, k):
        key = jnp.concatenate([operands(tile, j)[0] for j in range(k, min(k + 2, slots))], 1)
        return jnp.dot(queries[tile], key, preferred_element_type=jnp.float32)

    def add(tile, k, expo):
        value = jnp.concatenate([operands(tile, j)[1] for j in range(k, min(k + 2, slots))], 0)
        part = jnp.dot(expo, value, preferred_element_type=jnp.float32)
        totals[tile] = part if totals[tile] is None else totals[tile] + part

    scores, last = scores_of(*steps[0]), None
    for at, step in enumerate(steps):
        upcoming = scores_of(*steps[at + 1]) if at + 1 < len(steps) else None
        if last is not None:
            add(*last)
        last = (*step, jnp.exp2(scores * SCALE).astype(jnp.bfloat16))
        scores = upcoming
    add(*last)
    low_sum = None
    for tile, total in enumerate(totals):
        sums = total[:, HD:]
        store(tile, total[:, :HD] / sums)
        smallest = jnp.min(sums.reshape(-1, 8, HD), axis=0)
        low_sum = smallest if low_sum is None else jnp.minimum(low_sum, smallest)
    least[...] = low_sum

    @pl.when(jnp.logical_not(jnp.min(least[...]) > 2.0 ** -40))
    def _():
        for tile in range(2):
            query = views[2 * tile][...].reshape(2 * tokens, HD)
            query = jnp.concatenate([query, hot.astype(jnp.bfloat16)], 1)
            pieces = [operands(tile, k) for k in range(slots)]
            scores = jnp.concatenate(
                [jnp.dot(query, key, preferred_element_type=jnp.float32) for key, _ in pieces], 1)
            top = jnp.max(scores, axis=1, keepdims=True)
            expo = jnp.exp2((scores - top) * SCALE).astype(jnp.bfloat16)
            total = jnp.dot(expo, jnp.concatenate([value for _, value in pieces], 0),
                            preferred_element_type=jnp.float32)
            store(tile, total[:, :HD] / total[:, HD:])


def attend(info, queries, keys_values, there, got, own, low, blocks, table, part, heads_half, after):
    tokens = queries.shape[1]
    slots = WINB * BLK // tokens + 2
    count, first = len(part), part[0]
    here = lambda h, info: (0, 0, info[0] * heads_half + first + h)
    noisy = lambda h, info: (0, 1, 0, info[0] * heads_half + first + h)
    query_spec = pl.BlockSpec((2, tokens, HD), here)
    noisy_spec = pl.BlockSpec((2, 1, tokens, HD), noisy)
    chunk = pl.BlockSpec((2, 2, tokens, HD), lambda h, info: (0, 0, 0, h))
    out_spec = pl.BlockSpec((2, tokens, HD), lambda h, info: (0, 0, h))
    out = jax.ShapeDtypeStruct((2, tokens, count * HD), jnp.bfloat16)
    work = count * 2 * 2 * tokens * slots * tokens
    return pl.pallas_call(
        lambda *refs: attend_kernel(tokens, *refs),
        grid_spec=pltpu.PrefetchScalarGridSpec(
            num_scalar_prefetch=1,
            grid=(count,),
            in_specs=[
                query_spec, noisy_spec, query_spec, noisy_spec, *[chunk] * 6,
                *[pl.BlockSpec(memory_space=pl.ANY)] * len(after),
                pl.BlockSpec(table.shape, lambda h, info: (0, 0, 0, 0)),
            ],
            out_specs=[out_spec, out_spec, pl.BlockSpec((8, HD), lambda h, info: (0, 0))],
            scratch_shapes=[
                pltpu.VMEM((slots + 2, HD, tokens), jnp.bfloat16),
                pltpu.VMEM((slots, tokens, HD), jnp.bfloat16),
                pltpu.VMEM((8, HD), jnp.float32),
            ],
        ),
        out_shape=[out, out, jax.ShapeDtypeStruct((8, HD), jnp.float32)],
        compiler_params=pltpu.CompilerParams(vmem_limit_bytes=VMEM),
        cost_estimate=pl.CostEstimate(
            flops=work * 8, bytes_accessed=count * 64 * 1024, transcendentals=0
        ),
    )(info, queries, keys_values, there, got, own, low, *blocks, *after, table)


def project_kernel(count, groups, add, info, *refs):
    out = refs[-1]
    acts, weights = refs[:count], refs[count:count + groups]
    act = jnp.concatenate([a[...].reshape(-1, a.shape[2]) for a in acts], 1)
    weight = jnp.concatenate([w[...] for w in weights], 0)
    total = jnp.dot(act, weight, preferred_element_type=jnp.float32)
    if add:
        total = total + refs[count + groups][...].reshape(total.shape)
    out[...] = total.astype(out.dtype).reshape(out.shape)


def project(info, pieces, weights, features, dtype, before=None):
    tokens = pieces[0][2].shape[1]
    tile = min(512, features)
    steps = features // tile
    half = weights[0].shape[0] // 2
    used, specs = [], []
    for group, first, act in pieces:
        wide = act.shape[2] if first * HD % act.shape[2] == 0 else HD
        per = half // wide
        for at in range(first * HD // wide, (first * HD + act.shape[2]) // wide):
            used.append(weights[group])
            if group == 0:
                row = lambda s, info, at=at, per=per: (info[0] * per + at, info[2] * steps + s)
            elif group == 1:
                row = lambda s, info, at=at, per=per: (
                    (1 - info[0]) * per + at, info[2] * steps + s)
            else:
                row = lambda s, info, at=at: (at, s)
            specs.append(pl.BlockSpec((wide, tile), row))
    flat = [act for _, _, act in pieces]
    spec = pl.BlockSpec((2, tokens, tile), lambda s, info: (0, 0, s))
    specs = [pl.BlockSpec(a.shape, lambda s, info: (0, 0, 0)) for a in flat] + specs
    operands = flat + used
    if before is not None:
        specs.append(spec)
        operands.append(before)
    depth = sum(a.shape[2] for a in flat)
    return pl.pallas_call(
        lambda *refs: project_kernel(len(flat), len(used), before is not None, *refs),
        grid_spec=pltpu.PrefetchScalarGridSpec(
            num_scalar_prefetch=1, grid=(steps,), in_specs=specs, out_specs=spec
        ),
        out_shape=jax.ShapeDtypeStruct((2, tokens, features), dtype),
        compiler_params=pltpu.CompilerParams(vmem_limit_bytes=VMEM),
        cost_estimate=pl.CostEstimate(
            flops=2 * 2 * tokens * depth * features // 8,
            bytes_accessed=2 * depth * features // 8,
            transcendentals=0,
        ),
    )(info, *operands)


def on_device(queries, keys_values, block_mask, out_weight):
    tokens = queries.shape[1]
    n, f = lax.axis_size("ctx"), lax.axis_size("fsdp")
    index, place = lax.axis_index("ctx"), lax.axis_index("fsdp")
    core, side = index % 2, (index // 2) % 2
    info = jnp.stack([core, side, place]).astype(jnp.int32)
    width = queries.shape[2] // 2
    heads_half = width // HD
    rows = tokens // BLK
    features = out_weight.shape[1] // f
    bf16 = jnp.bfloat16
    parts = [[0,1],[2,3]] if heads_half == 4 else [[h] for h in range(heads_half)]

    pair = lambda i: i ^ 1
    ahead = lambda i: i + 4 if i + 4 < n else None
    across = lambda i: i ^ 2
    upper = lambda i: i + 2 if i & 2 == 0 else None
    lower = lambda i: i - 2 if i & 2 else None
    lanes = lambda start, size: pl.ds(pl.multiple_of(start, HD), size)

    got = moved(keys_values, n, pair, "pair_kv")
    there = moved(queries, n, pair, "pair_q")

    def cut_panels(core, place, ins, outs):
        pieces = []
        for r in range(1, f):
            column = pl.multiple_of(lax.rem(place + r, f) * features, HD)
            for p in range(cuts):
                row = pl.multiple_of(core * width + p * (width // cuts), width // cuts)
                at = pl.ds(p * (width // cuts), width // cuts)
                pieces.append((ins[0].at[pl.ds(row, width // cuts), pl.ds(column, features)],
                               [(slice(None), outs[r - 1].at[at])]))
        return pieces

    cuts = 4 if f == 2 else 1
    panels = copies(
        info, [out_weight], [jax.ShapeDtypeStruct((width, features), bf16)] * (f - 1),
        [(width // cuts, features)] * (cuts * (f - 1)), cut_panels,
    )

    def join(core, ins, outs):
        pieces = []
        for slot, source in enumerate(ins[:2]):
            for head_at, target in outs:
                wide = target.shape[-1]
                here = lanes(core * width + head_at * HD, wide)
                pieces.append((source.at[:, 0, :, here], [(slice(None), target.at[slot])]))
        return pieces

    pair_shape = lambda heads: jax.ShapeDtypeStruct((2, 2, tokens, heads * HD), bf16)
    held = lambda heads: (2, tokens, heads * HD)
    first, = copies(
        info, [keys_values, got, *panels], [pair_shape(len(parts[0]))], [held(len(parts[0]))] * 2,
        lambda core, place, ins, outs: join(core, ins, [(0, outs[0])]),
    )
    rest = []
    if len(parts) > 1:
        sizes = [len(part) for part in parts[1:]]
        rest = copies(
            info, [keys_values, got, first], [pair_shape(size) for size in sizes],
            [held(size) for size in sizes] * 2,
            lambda core, place, ins, outs: join(
                core, ins, [(p[0], out) for p, out in zip(parts[1:], outs)]),
        )
    own = [first] + list(rest)

    sames = [
        moved_both(panel, n, f, lambda i, k: (i, (k + r) % f), "panel")
        for r, panel in enumerate(panels, 1)
    ]

    blocks = []
    lows = []
    for k, mine in enumerate(own):
        one = moved(mine, n, ahead, f"near{k}")
        swap = moved(one, n, across, f"nearx{k}")
        if k:
            one, = gated([one], *blocks[-1][1:3])
        two = moved(one, n, ahead, f"far{k}")
        if k:
            own[k - 1], = gated([own[k - 1]], swap)
            lows.append(moved(own[k - 1], n, upper, f"ownx{k - 1}"))
            two, = gated([two], swap, blocks[-1][3], lows[-1])
        blocks.append((one, two, swap, moved(two, n, lower, f"farx{k}")))
    if lows:
        own[-1], = gated([own[-1]], lows[-1])
    lows.append(moved(own[-1], n, upper, f"ownx{len(own) - 1}"))

    mask_there = moved(block_mask, n, pair, "pair_mask")
    table = jnp.stack([
        mask_table(index * rows, rows, block_mask),
        mask_table((index ^ 1) * rows, rows, mask_there),
    ])

    acts = [[] for _ in range(2 * f)]
    ties = []
    for k, part in enumerate(parts):
        after = []
        mine, give, tie = attend(
            info, queries, keys_values, there, got, own[k], lows[k], blocks[k], table,
            part, heads_half, after + ties[-1:],
        )
        ties.append(tie)
        acts[0].append(mine)
        for r in range(1, f):
            acts[2 * r].append(moved_both(mine, n, f, lambda i, k: (i, (k + r) % f), f"same{k}"))
            acts[2 * r + 1].append(moved_both(give, n, f, lambda i, k: (i ^ 1, (k + r) % f), f"cross{k}"))
        acts[1].append(moved(give, n, pair, f"pair{k}"))
    others = []
    for same in sames:
        same, = gated([same], blocks[-1][3], ties[0], lows[-1])
        others += [same, moved(same, n, pair, "panel_pair")]

    weights = [out_weight, out_weight] + others
    early, late = [], []
    for g in range(2 * f):
        for k, (part, act) in enumerate(zip(parts, acts[g])):
            (late if g and k == len(parts) - 1 else early).append((g, part[0], act))
    before = project(info, early, weights, features, jnp.float32)
    return project(info, late, weights, features, jnp.bfloat16, before)


def solution(mesh):
    in_specs = (
        P(None, "ctx", "fsdp"),
        P(None, None, "ctx", "fsdp"),
        P("ctx", None),
        P("fsdp", None),
    )
    out_specs = P(None, "ctx", "fsdp")
    return jax.shard_map(
        on_device, mesh=mesh, in_specs=in_specs, out_specs=out_specs, check_vma=False
    )
```

```python
import math

import jax
import jax.numpy as jnp
from jax import lax
from jax.experimental import pallas as pl
from jax.experimental.pallas import tpu as pltpu
from jax.sharding import PartitionSpec as P

HD = 128
BLK = 64
WINB = 32
MASKED = -1e30
SCALE = 1.0 / math.sqrt(HD)
VMEM = 60 * 1024 * 1024


def moved(array, n, go, name):
    pairs = [(i, go(i)) for i in range(n) if go(i) is not None]
    with jax.named_scope(name):
        return lax.ppermute(array, "ctx", pairs)


def moved_both(array, n, f, go, name):
    pairs = [(i * f + k, go(i, k)[0] * f + go(i, k)[1]) for i in range(n) for k in range(f)]
    with jax.named_scope(name):
        return lax.ppermute(array, ("ctx", "fsdp"), pairs)


def behind(array, *others):
    return lax.optimization_barrier((array,) + others)[0] if others else array


def gated(arrays, *ties):
    ties = [t[(0,) * (t.ndim - 2)][:8] for t in ties]
    some = pl.BlockSpec(memory_space=pl.ANY)
    return pl.pallas_call(
        lambda *refs: None,
        in_specs=[some] * (len(arrays) + len(ties)),
        out_specs=[some] * len(arrays),
        out_shape=[jax.ShapeDtypeStruct(a.shape, a.dtype) for a in arrays],
        input_output_aliases={k: k for k in range(len(arrays))},
        compiler_params=pltpu.CompilerParams(vmem_limit_bytes=1024 * 1024),
        cost_estimate=pl.CostEstimate(flops=0, bytes_accessed=0, transcendentals=0),
    )(*arrays, *ties)


def mask_table(first_block, rows, mask_rows):
    count = WINB + rows
    query = jnp.arange(rows)
    gap = WINB + query[None, :] - jnp.arange(count)[:, None]
    present = (first_block - WINB + jnp.arange(count) >= 0)[:, None]
    clean = (gap >= 0) & (gap < WINB) & present
    offsets = jnp.arange(WINB)
    picked = ((gap - 1)[:, :, None] == offsets[None, None, :]) & (mask_rows[None] == 1)
    noisy = jnp.any(picked, axis=2) & present
    own_clean = jnp.zeros((rows, rows), bool)
    own_noisy = jnp.eye(rows, dtype=bool)
    allowed = jnp.concatenate(
        [jnp.concatenate([clean, noisy], 1), jnp.concatenate([own_clean, own_noisy], 1)], 0
    )
    table = jnp.where(allowed, 0.0, MASKED).astype(jnp.float32)
    table = jnp.concatenate([table, jnp.ones((count + rows, 1), jnp.float32)], 1)
    table = jnp.pad(table, ((0, 0), (0, 16 - table.shape[1]))).astype(jnp.bfloat16)
    table = jnp.repeat(table.reshape(-1, rows, 16).transpose(0, 2, 1), BLK, axis=2)
    return table


def copies(info, sources, outs, shapes, plan):
    total = sum(math.prod(o.shape) for o in outs)

    def kernel(info, *refs):
        ins, rest = refs[:len(sources)], refs[len(sources):]
        pieces = plan(info[0], info[2], ins, rest[:len(outs)])
        room, arrive, leave = rest[len(outs):-2], rest[-2], rest[-1]
        reads = [
            pltpu.make_async_copy(source, held, arrive.at[k])
            for k, ((source, _), held) in enumerate(zip(pieces, room))
        ]
        for read in reads:
            read.start()
        writes = []
        for read, (_, targets), held in zip(reads, pieces, room):
            read.wait()
            for part, target in targets:
                write = pltpu.make_async_copy(held.at[part], target, leave.at[len(writes)])
                write.start()
                writes.append(write)
        for write in writes:
            write.wait()

    return pl.pallas_call(
        kernel,
        grid_spec=pltpu.PrefetchScalarGridSpec(
            num_scalar_prefetch=1,
            grid=(),
            in_specs=[pl.BlockSpec(memory_space=pl.ANY)] * len(sources),
            out_specs=[pl.BlockSpec(memory_space=pl.ANY)] * len(outs),
            scratch_shapes=[
                *[pltpu.VMEM(shape, jnp.bfloat16) for shape in shapes],
                pltpu.SemaphoreType.DMA((len(shapes),)),
                pltpu.SemaphoreType.DMA((32,)),
            ],
        ),
        out_shape=[jax.ShapeDtypeStruct(o.shape, o.dtype) for o in outs],
        compiler_params=pltpu.CompilerParams(vmem_limit_bytes=VMEM),
        cost_estimate=pl.CostEstimate(flops=0, bytes_accessed=total, transcendentals=0),
    )(info, *sources)


def attend_kernel(tokens, info, *refs):
    core, side = info[0], info[1]
    views, (own, one, two, swap, extra), refs = refs[:4], refs[4:9], refs[-7:]
    table, mine, give, tie, keys, values, least = refs
    tie[...] = jnp.zeros_like(tie)
    rows = tokens // BLK
    slots = WINB * BLK // tokens + 2
    back = WINB * BLK // (2 * tokens)

    def place(ref, pair):
        for slot in range(2):
            half = core if slot == 0 else 1 - core
            keys[pair * 2 + half] = ref[0, slot, 0].T
            values[pair * 2 + half] = ref[0, slot, 1]

    place(two, 0)
    place(one, 2)
    place(swap, jnp.where(side == 0, 3, 1))
    place(own, back)

    place(extra, jnp.where(side == 0, 1, 3))
    for tile in range(2):
        keys[slots + tile] = views[2 * tile + 1][0, 0].T

    spot = lax.broadcasted_iota(jnp.int32, (2 * tokens, HD), 0) // BLK
    lane = lax.broadcasted_iota(jnp.int32, (2 * tokens, HD), 1)
    hot = jnp.where(spot == lane, 1.0, 0.0)
    rest = jnp.zeros((HD - table.shape[2], tokens), jnp.bfloat16)

    def operands(tile, k):
        half = core if tile == 0 else 1 - core
        if k == slots - 1:
            key, value = keys[slots + tile], views[2 * tile + 1][1, 0]
        else:
            key, value = keys[half + k], values[half + k]
        return (jnp.concatenate([key, table[tile, k], rest], 0),
                jnp.concatenate([value, jnp.ones_like(value)], 1))

    def store(tile, out):
        (mine if tile == 0 else give)[...] = out.astype(jnp.bfloat16).reshape(2, tokens, HD)

    shift_lane = 2 * rows
    ones = jnp.ones((16, HD), jnp.bfloat16)
    longest = None
    for k in range(slots + 2):
        key = keys[k]
        size = jnp.dot(ones, key * key, preferred_element_type=jnp.float32)
        longest = size if longest is None else jnp.maximum(longest, size)
    longest = jnp.max(longest, axis=1, keepdims=True)[0:1] * 1.03
    queries = []
    for tile in range(2):
        query = views[2 * tile][...].reshape(2 * tokens, HD)
        size = jnp.dot(query * query, jnp.ones((HD, HD), jnp.bfloat16),
                       preferred_element_type=jnp.float32)
        bound = jnp.sqrt(size * longest)
        extra = jnp.where(lane == shift_lane, -bound, hot).astype(jnp.bfloat16)
        queries.append(jnp.concatenate([query, extra], 1))

    steps = [(tile, k) for tile in range(2) for k in range(0, slots, 2)]
    totals = [None, None]

    def scores_of(tile, k):
        key = jnp.concatenate([operands(tile, j)[0] for j in range(k, min(k + 2, slots))], 1)
        return jnp.dot(queries[tile], key, preferred_element_type=jnp.float32)

    def add(tile, k, expo):
        value = jnp.concatenate([operands(tile, j)[1] for j in range(k, min(k + 2, slots))], 0)
        part = jnp.dot(expo, value, preferred_element_type=jnp.float32)
        totals[tile] = part if totals[tile] is None else totals[tile] + part

    scores, last = scores_of(*steps[0]), None
    for at, step in enumerate(steps):
        upcoming = scores_of(*steps[at + 1]) if at + 1 < len(steps) else None
        if last is not None:
            add(*last)
        last = (*step, jnp.exp(scores * SCALE).astype(jnp.bfloat16))
        scores = upcoming
    add(*last)
    low_sum = None
    for tile, total in enumerate(totals):
        sums = total[:, HD:]
        store(tile, total[:, :HD] / sums)
        smallest = jnp.min(sums.reshape(-1, 8, HD), axis=0)
        low_sum = smallest if low_sum is None else jnp.minimum(low_sum, smallest)
    least[...] = low_sum

    @pl.when(jnp.logical_not(jnp.min(least[...]) > 2.0 ** -40))
    def _():
        for tile in range(2):
            query = views[2 * tile][...].reshape(2 * tokens, HD)
            query = jnp.concatenate([query, hot.astype(jnp.bfloat16)], 1)
            pieces = [operands(tile, k) for k in range(slots)]
            scores = jnp.concatenate(
                [jnp.dot(query, key, preferred_element_type=jnp.float32) for key, _ in pieces], 1)
            top = jnp.max(scores, axis=1, keepdims=True)
            expo = jnp.exp((scores - top) * SCALE).astype(jnp.bfloat16)
            total = jnp.dot(expo, jnp.concatenate([value for _, value in pieces], 0),
                            preferred_element_type=jnp.float32)
            store(tile, total[:, :HD] / total[:, HD:])


def attend(info, queries, keys_values, there, got, own, blocks, table, part, heads_half, after):
    tokens = queries.shape[1]
    slots = WINB * BLK // tokens + 2
    count, first = len(part), part[0]
    here = lambda h, info: (0, 0, info[0] * heads_half + first + h)
    noisy = lambda h, info: (0, 1, 0, info[0] * heads_half + first + h)
    query_spec = pl.BlockSpec((2, tokens, HD), here)
    noisy_spec = pl.BlockSpec((2, 1, tokens, HD), noisy)
    chunk = pl.BlockSpec((1, 2, 2, tokens, HD), lambda h, info: (h, 0, 0, 0, 0))
    out_spec = pl.BlockSpec((2, tokens, HD), lambda h, info: (0, 0, h))
    out = jax.ShapeDtypeStruct((2, tokens, count * HD), jnp.bfloat16)
    work = count * 2 * 2 * tokens * slots * tokens
    return pl.pallas_call(
        lambda *refs: attend_kernel(tokens, *refs),
        grid_spec=pltpu.PrefetchScalarGridSpec(
            num_scalar_prefetch=1,
            grid=(count,),
            in_specs=[
                query_spec, noisy_spec, query_spec, noisy_spec, *[chunk] * 5,
                *[pl.BlockSpec(memory_space=pl.ANY)] * len(after),
                pl.BlockSpec(table.shape, lambda h, info: (0, 0, 0, 0)),
            ],
            out_specs=[out_spec, out_spec, pl.BlockSpec((8, HD), lambda h, info: (0, 0))],
            scratch_shapes=[
                pltpu.VMEM((slots + 2, HD, tokens), jnp.bfloat16),
                pltpu.VMEM((slots, tokens, HD), jnp.bfloat16),
                pltpu.VMEM((8, HD), jnp.float32),
            ],
        ),
        out_shape=[out, out, jax.ShapeDtypeStruct((8, HD), jnp.float32)],
        compiler_params=pltpu.CompilerParams(vmem_limit_bytes=VMEM),
        cost_estimate=pl.CostEstimate(
            flops=work * 8, bytes_accessed=count * 64 * 1024, transcendentals=0
        ),
    )(info, queries, keys_values, there, got, own, *blocks, *after, table)


def project_kernel(count, groups, add, info, *refs):
    out = refs[-1]
    acts, weights = refs[:count], refs[count:count + groups]
    act = jnp.concatenate([a[...].reshape(-1, a.shape[2]) for a in acts], 1)
    weight = jnp.concatenate([w[...] for w in weights], 0)
    total = jnp.dot(act, weight, preferred_element_type=jnp.float32)
    if add:
        total = total + refs[count + groups][...].reshape(total.shape)
    out[...] = total.astype(out.dtype).reshape(out.shape)


def project(info, pieces, weights, features, dtype, before=None):
    tokens = pieces[0][2].shape[1]
    tile = min(512, features)
    steps = features // tile
    half = weights[0].shape[0] // 2
    used, specs = [], []
    for group, first, act in pieces:
        wide = act.shape[2] if first * HD % act.shape[2] == 0 else HD
        per = half // wide
        for at in range(first * HD // wide, (first * HD + act.shape[2]) // wide):
            used.append(weights[group])
            if group == 0:
                row = lambda s, info, at=at, per=per: (info[0] * per + at, info[2] * steps + s)
            elif group == 1:
                row = lambda s, info, at=at, per=per: (
                    (1 - info[0]) * per + at, info[2] * steps + s)
            else:
                row = lambda s, info, at=at: (at, s)
            specs.append(pl.BlockSpec((wide, tile), row))
    flat = [act for _, _, act in pieces]
    spec = pl.BlockSpec((2, tokens, tile), lambda s, info: (0, 0, s))
    specs = [pl.BlockSpec(a.shape, lambda s, info: (0, 0, 0)) for a in flat] + specs
    operands = flat + used
    if before is not None:
        specs.append(spec)
        operands.append(before)
    depth = sum(a.shape[2] for a in flat)
    return pl.pallas_call(
        lambda *refs: project_kernel(len(flat), len(used), before is not None, *refs),
        grid_spec=pltpu.PrefetchScalarGridSpec(
            num_scalar_prefetch=1, grid=(steps,), in_specs=specs, out_specs=spec
        ),
        out_shape=jax.ShapeDtypeStruct((2, tokens, features), dtype),
        compiler_params=pltpu.CompilerParams(vmem_limit_bytes=40 * 1024 * 1024),
        cost_estimate=pl.CostEstimate(
            flops=2 * 2 * tokens * depth * features // 8,
            bytes_accessed=2 * depth * features // 8,
            transcendentals=0,
        ),
    )(info, *operands)


def on_device(queries, keys_values, block_mask, out_weight):
    tokens = queries.shape[1]
    n, f = lax.axis_size("ctx"), lax.axis_size("fsdp")
    index, place = lax.axis_index("ctx"), lax.axis_index("fsdp")
    core, side = index % 2, (index // 2) % 2
    info = jnp.stack([core, side, place]).astype(jnp.int32)
    width = queries.shape[2] // 2
    heads_half = width // HD
    rows = tokens // BLK
    features = out_weight.shape[1] // f
    bf16 = jnp.bfloat16
    parts = [[0,1],[2,3]] if heads_half == 4 else [[h] for h in range(heads_half)]

    pair = lambda i: i ^ 1
    ahead = lambda i: i + 4 if i + 4 < n else None
    across = lambda i: i ^ 2
    upper = lambda i: i + 2 if i & 2 == 0 else None
    lower = lambda i: i - 2 if i & 2 else None
    lanes = lambda start, size: pl.ds(pl.multiple_of(start, HD), size)

    got = moved(keys_values, n, pair, "pair_kv")
    there = moved(queries, n, pair, "pair_q")

    def cut_panels(core, place, ins, outs):
        pieces = []
        for r in range(1, f):
            column = pl.multiple_of(lax.rem(place + r, f) * features, HD)
            for p in range(cuts):
                row = pl.multiple_of(core * width + p * (width // cuts), width // cuts)
                at = pl.ds(p * (width // cuts), width // cuts)
                pieces.append((ins[0].at[pl.ds(row, width // cuts), pl.ds(column, features)],
                               [(slice(None), outs[r - 1].at[at])]))
        return pieces

    cuts = 4 if f == 2 else 1
    panels = copies(
        info, [out_weight], [jax.ShapeDtypeStruct((width, features), bf16)] * (f - 1),
        [(width // cuts, features)] * (cuts * (f - 1)), cut_panels,
    )

    def join(core, ins, outs):
        pieces = []
        for slot, source in enumerate(ins[:2]):
            for head_at, target in outs:
                heads = target.shape[0]
                here = lanes(core * width + head_at * HD, heads * HD)
                pieces.append((source.at[:, 0, :, here], [
                    ((slice(None), slice(None), slice(h * HD, (h + 1) * HD)), target.at[h, slot])
                    for h in range(heads)
                ]))
        return pieces

    pair_shape = lambda heads: jax.ShapeDtypeStruct((heads, 2, 2, tokens, HD), bf16)
    held = lambda heads: (2, tokens, heads * HD)
    first, = copies(
        info, [keys_values, got, *panels], [pair_shape(len(parts[0]))], [held(len(parts[0]))] * 2,
        lambda core, place, ins, outs: join(core, ins, [(0, outs[0])]),
    )
    rest = []
    if len(parts) > 1:
        sizes = [len(part) for part in parts[1:]]
        rest = copies(
            info, [keys_values, got, first], [pair_shape(size) for size in sizes],
            [held(size) for size in sizes] * 2,
            lambda core, place, ins, outs: join(
                core, ins, [(p[0], out) for p, out in zip(parts[1:], outs)]),
        )
    own = [first] + list(rest)

    sames = [
        moved_both(panel, n, f, lambda i, k: (i, (k + r) % f), "panel")
        for r, panel in enumerate(panels, 1)
    ]


    blocks = []
    for k, mine in enumerate(own):
        one = moved(mine, n, ahead, f"near{k}")
        swap = moved(one, n, across, f"nearx{k}")
        if k:
            one, = gated([one], *blocks[-1][1:3])
        two = moved(one, n, ahead, f"far{k}")
        if k:
            two, = gated([two], swap, blocks[-1][3])
        extra = moved(jnp.where(side == 0, mine, two), n, across, f"extra{k}")
        blocks.append((one, two, swap, extra))

    mask_there = moved(block_mask, n, pair, "pair_mask")
    table = jnp.stack([
        mask_table(index * rows, rows, block_mask),
        mask_table((index ^ 1) * rows, rows, mask_there),
    ])

    acts = [[] for _ in range(2 * f)]
    ties = []
    for k, part in enumerate(parts):
        after = []
        mine, give, tie = attend(
            info, queries, keys_values, there, got, own[k], blocks[k], table,
            part, heads_half, after + ties[-1:],
        )
        ties.append(tie)
        acts[0].append(mine)
        for r in range(1, f):
            acts[2 * r].append(moved_both(mine, n, f, lambda i, k: (i, (k + r) % f), f"same{k}"))
            acts[2 * r + 1].append(moved_both(give, n, f, lambda i, k: (i ^ 1, (k + r) % f), f"cross{k}"))
        acts[1].append(moved(give, n, pair, f"pair{k}"))
    others = []
    for same in sames:
        same, = gated([same], blocks[-1][3], ties[0])
        others += [same, moved(same, n, pair, "panel_pair")]

    weights = [out_weight, out_weight] + others
    early, late = [], []
    for g in range(2 * f):
        for k, (part, act) in enumerate(zip(parts, acts[g])):
            (late if g and k == len(parts) - 1 else early).append((g, part[0], act))
    before = project(info, early, weights, features, jnp.float32)
    return project(info, late, weights, features, jnp.bfloat16, before)


def solution(mesh):
    in_specs = (
        P(None, "ctx", "fsdp"),
        P(None, None, "ctx", "fsdp"),
        P("ctx", None),
        P("fsdp", None),
    )
    out_specs = P(None, "ctx", "fsdp")
    return jax.shard_map(
        on_device, mesh=mesh, in_specs=in_specs, out_specs=out_specs, check_vma=False
    )
```

```python
import math

import jax
import jax.numpy as jnp
from jax import lax
from jax.experimental import pallas as pl
from jax.experimental.pallas import tpu as pltpu
from jax.sharding import PartitionSpec as P

HD = 128
BLK = 64
WINB = 32
MASKED = -1e30
SCALE = 1.0 / math.sqrt(HD)
VMEM = 60 * 1024 * 1024


def moved(array, n, go, name):
    pairs = [(i, go(i)) for i in range(n) if go(i) is not None]
    with jax.named_scope(name):
        return lax.ppermute(array, "ctx", pairs)


def moved_both(array, n, f, go, name):
    pairs = [(i * f + k, go(i, k)[0] * f + go(i, k)[1]) for i in range(n) for k in range(f)]
    with jax.named_scope(name):
        return lax.ppermute(array, ("ctx", "fsdp"), pairs)


def behind(array, *others):
    return lax.optimization_barrier((array,) + others)[0] if others else array


def gated(arrays, *ties):
    ties = [t[(0,) * (t.ndim - 2)][:8] for t in ties]
    some = pl.BlockSpec(memory_space=pl.ANY)
    return pl.pallas_call(
        lambda *refs: None,
        in_specs=[some] * (len(arrays) + len(ties)),
        out_specs=[some] * len(arrays),
        out_shape=[jax.ShapeDtypeStruct(a.shape, a.dtype) for a in arrays],
        input_output_aliases={k: k for k in range(len(arrays))},
        compiler_params=pltpu.CompilerParams(vmem_limit_bytes=1024 * 1024),
        cost_estimate=pl.CostEstimate(flops=0, bytes_accessed=0, transcendentals=0),
    )(*arrays, *ties)


def mask_table(first_block, rows, mask_rows):
    count = WINB + rows
    query = jnp.arange(rows)
    gap = WINB + query[None, :] - jnp.arange(count)[:, None]
    present = (first_block - WINB + jnp.arange(count) >= 0)[:, None]
    clean = (gap >= 0) & (gap < WINB) & present
    offsets = jnp.arange(WINB)
    picked = ((gap - 1)[:, :, None] == offsets[None, None, :]) & (mask_rows[None] == 1)
    noisy = jnp.any(picked, axis=2) & present
    own_clean = jnp.zeros((rows, rows), bool)
    own_noisy = jnp.eye(rows, dtype=bool)
    allowed = jnp.concatenate(
        [jnp.concatenate([clean, noisy], 1), jnp.concatenate([own_clean, own_noisy], 1)], 0
    )
    table = jnp.where(allowed, 0.0, MASKED).astype(jnp.float32)
    return jnp.repeat(table.reshape(-1, rows, 2 * rows).transpose(0, 2, 1), BLK, axis=2)


def copies(info, sources, outs, shapes, plan):
    total = sum(math.prod(o.shape) for o in outs)

    def kernel(info, *refs):
        ins, rest = refs[:len(sources)], refs[len(sources):]
        pieces = plan(info[0], info[2], ins, rest[:len(outs)])
        room, arrive, leave = rest[len(outs):-2], rest[-2], rest[-1]
        reads = [
            pltpu.make_async_copy(source, held, arrive.at[k])
            for k, ((source, _), held) in enumerate(zip(pieces, room))
        ]
        for read in reads:
            read.start()
        writes = []
        for read, (_, targets), held in zip(reads, pieces, room):
            read.wait()
            for part, target in targets:
                write = pltpu.make_async_copy(held.at[part], target, leave.at[len(writes)])
                write.start()
                writes.append(write)
        for write in writes:
            write.wait()

    return pl.pallas_call(
        kernel,
        grid_spec=pltpu.PrefetchScalarGridSpec(
            num_scalar_prefetch=1,
            grid=(),
            in_specs=[pl.BlockSpec(memory_space=pl.ANY)] * len(sources),
            out_specs=[pl.BlockSpec(memory_space=pl.ANY)] * len(outs),
            scratch_shapes=[
                *[pltpu.VMEM(shape, jnp.bfloat16) for shape in shapes],
                pltpu.SemaphoreType.DMA((len(shapes),)),
                pltpu.SemaphoreType.DMA((32,)),
            ],
        ),
        out_shape=[jax.ShapeDtypeStruct(o.shape, o.dtype) for o in outs],
        compiler_params=pltpu.CompilerParams(vmem_limit_bytes=VMEM),
        cost_estimate=pl.CostEstimate(flops=0, bytes_accessed=total, transcendentals=0),
    )(info, *sources)


def attend_kernel(tokens, info, *refs):
    core, side = info[0], info[1]
    views, (own, one, two, swap, extra), refs = refs[:4], refs[4:9], refs[-7:]
    table, mine, give, tie, keys, values, least = refs
    tie[...] = jnp.zeros_like(tie)
    rows = tokens // BLK
    slots = WINB * BLK // tokens + 2
    back = WINB * BLK // (2 * tokens)

    def place(ref, pair):
        for slot in range(2):
            half = core if slot == 0 else 1 - core
            keys[pair * 2 + half] = ref[0, slot, 0].T
            values[pair * 2 + half] = ref[0, slot, 1]

    place(two, 0)
    place(one, 2)
    place(swap, jnp.where(side == 0, 3, 1))
    place(own, back)

    place(extra, jnp.where(side == 0, 1, 3))
    for tile in range(2):
        keys[slots + tile] = views[2 * tile + 1][0, 0].T

    def operands(tile, k):
        half = core if tile == 0 else 1 - core
        if k == slots - 1:
            return keys[slots + tile], views[2 * tile + 1][1, 0]
        return keys[half + k], values[half + k]

    def store(tile, out):
        (mine if tile == 0 else give)[...] = out.astype(jnp.bfloat16).reshape(2, tokens, HD)

    ones = jnp.ones((16, HD), jnp.bfloat16)
    longest = None
    for k in range(slots + 2):
        key = keys[k]
        size = jnp.dot(ones, key * key, preferred_element_type=jnp.float32)
        longest = size if longest is None else jnp.maximum(longest, size)
    longest = jnp.max(longest, axis=1, keepdims=True)[0:1] * 1.03
    queries, shifts = [], []
    for tile in range(2):
        query = views[2 * tile][...].reshape(2 * tokens, HD)
        size = jnp.dot(query * query, jnp.ones((HD, HD), jnp.bfloat16),
                       preferred_element_type=jnp.float32)
        queries.append(query)
        shifts.append((jnp.sqrt(size * longest) * SCALE)[:, 0:1])

    steps = [(tile, k) for tile in range(2) for k in range(0, slots, 2)]
    totals, sums = [None, None], [None, None]

    def scores_of(tile, k):
        key = jnp.concatenate([operands(tile, j)[0] for j in range(k, min(k + 2, slots))], 1)
        scores = jnp.dot(queries[tile], key, preferred_element_type=jnp.float32)
        bias = jnp.concatenate([table[tile, j] for j in range(k, min(k + 2, slots))], 1)
        return scores, bias

    def weights_of(tile, scores, bias, shift):
        wide = scores.shape[1]
        shifted = scores * SCALE - shift
        shifted = shifted.reshape(2 * rows, BLK, wide) + bias[:, None, :]
        return jnp.exp(shifted.reshape(2 * tokens, wide))

    def add(tile, k, expo):
        value = jnp.concatenate([operands(tile, j)[1] for j in range(k, min(k + 2, slots))], 0)
        part = jnp.dot(expo, value, preferred_element_type=jnp.float32)
        totals[tile] = part if totals[tile] is None else totals[tile] + part

    scores, last = scores_of(*steps[0]), None
    for at, step in enumerate(steps):
        upcoming = scores_of(*steps[at + 1]) if at + 1 < len(steps) else None
        if last is not None:
            add(*last)
        tile = step[0]
        expo = weights_of(tile, *scores, shifts[tile])
        for lanes in range(0, expo.shape[1], HD):
            part = expo[:, lanes:lanes + HD]
            sums[tile] = part if sums[tile] is None else sums[tile] + part
        last = (*step, expo.astype(jnp.bfloat16))
        scores = upcoming
    add(*last)
    low_sum = None
    for tile, total in enumerate(totals):
        whole = jnp.sum(sums[tile], axis=1, keepdims=True)
        store(tile, total / whole)
        smallest = jnp.min(whole, axis=0, keepdims=True)
        low_sum = smallest if low_sum is None else jnp.minimum(low_sum, smallest)
    least[...] = jnp.broadcast_to(low_sum, least.shape)

    @pl.when(jnp.logical_not(jnp.min(least[...]) > 2.0 ** -40))
    def _():
        for tile in range(2):
            runs = [scores_of(tile, k) for k in range(0, slots, 2)]
            scores = jnp.concatenate([score for score, _ in runs], 1) * SCALE
            bias = jnp.concatenate([bias for _, bias in runs], 1)
            wide = scores.shape[1]
            scores = (scores.reshape(2 * rows, BLK, wide) + bias[:, None, :]).reshape(
                2 * tokens, wide)
            expo = jnp.exp(scores - jnp.max(scores, axis=1, keepdims=True))
            value = jnp.concatenate([operands(tile, k)[1] for k in range(slots)], 0)
            total = jnp.dot(expo.astype(jnp.bfloat16), value, preferred_element_type=jnp.float32)
            store(tile, total / jnp.sum(expo, axis=1, keepdims=True))


def attend(info, queries, keys_values, there, got, own, blocks, table, part, heads_half, after):
    tokens = queries.shape[1]
    slots = WINB * BLK // tokens + 2
    count, first = len(part), part[0]
    here = lambda h, info: (0, 0, info[0] * heads_half + first + h)
    noisy = lambda h, info: (0, 1, 0, info[0] * heads_half + first + h)
    query_spec = pl.BlockSpec((2, tokens, HD), here)
    noisy_spec = pl.BlockSpec((2, 1, tokens, HD), noisy)
    chunk = pl.BlockSpec((1, 2, 2, tokens, HD), lambda h, info: (h, 0, 0, 0, 0))
    out_spec = pl.BlockSpec((2, tokens, HD), lambda h, info: (0, 0, h))
    out = jax.ShapeDtypeStruct((2, tokens, count * HD), jnp.bfloat16)
    work = count * 2 * 2 * tokens * slots * tokens
    return pl.pallas_call(
        lambda *refs: attend_kernel(tokens, *refs),
        grid_spec=pltpu.PrefetchScalarGridSpec(
            num_scalar_prefetch=1,
            grid=(count,),
            in_specs=[
                query_spec, noisy_spec, query_spec, noisy_spec, *[chunk] * 5,
                *[pl.BlockSpec(memory_space=pl.ANY)] * len(after),
                pl.BlockSpec(table.shape, lambda h, info: (0, 0, 0, 0)),
            ],
            out_specs=[out_spec, out_spec, pl.BlockSpec((8, HD), lambda h, info: (0, 0))],
            scratch_shapes=[
                pltpu.VMEM((slots + 2, HD, tokens), jnp.bfloat16),
                pltpu.VMEM((slots, tokens, HD), jnp.bfloat16),
                pltpu.VMEM((8, HD), jnp.float32),
            ],
        ),
        out_shape=[out, out, jax.ShapeDtypeStruct((8, HD), jnp.float32)],
        compiler_params=pltpu.CompilerParams(vmem_limit_bytes=VMEM),
        cost_estimate=pl.CostEstimate(
            flops=work * 8, bytes_accessed=count * 64 * 1024, transcendentals=0
        ),
    )(info, queries, keys_values, there, got, own, *blocks, *after, table)


def project_kernel(count, groups, add, info, *refs):
    out = refs[-1]
    acts, weights = refs[:count], refs[count:count + groups]
    act = jnp.concatenate([a[...].reshape(-1, a.shape[2]) for a in acts], 1)
    weight = jnp.concatenate([w[...] for w in weights], 0)
    total = jnp.dot(act, weight, preferred_element_type=jnp.float32)
    if add:
        total = total + refs[count + groups][...].reshape(total.shape)
    out[...] = total.astype(out.dtype).reshape(out.shape)


def project(info, pieces, weights, features, dtype, before=None):
    tokens = pieces[0][2].shape[1]
    tile = min(512, features)
    steps = features // tile
    half = weights[0].shape[0] // 2
    used, specs = [], []
    for group, first, act in pieces:
        wide = act.shape[2] if first * HD % act.shape[2] == 0 else HD
        per = half // wide
        for at in range(first * HD // wide, (first * HD + act.shape[2]) // wide):
            used.append(weights[group])
            if group == 0:
                row = lambda s, info, at=at, per=per: (info[0] * per + at, info[2] * steps + s)
            elif group == 1:
                row = lambda s, info, at=at, per=per: (
                    (1 - info[0]) * per + at, info[2] * steps + s)
            else:
                row = lambda s, info, at=at: (at, s)
            specs.append(pl.BlockSpec((wide, tile), row))
    flat = [act for _, _, act in pieces]
    spec = pl.BlockSpec((2, tokens, tile), lambda s, info: (0, 0, s))
    specs = [pl.BlockSpec(a.shape, lambda s, info: (0, 0, 0)) for a in flat] + specs
    operands = flat + used
    if before is not None:
        specs.append(spec)
        operands.append(before)
    depth = sum(a.shape[2] for a in flat)
    return pl.pallas_call(
        lambda *refs: project_kernel(len(flat), len(used), before is not None, *refs),
        grid_spec=pltpu.PrefetchScalarGridSpec(
            num_scalar_prefetch=1, grid=(steps,), in_specs=specs, out_specs=spec
        ),
        out_shape=jax.ShapeDtypeStruct((2, tokens, features), dtype),
        compiler_params=pltpu.CompilerParams(vmem_limit_bytes=40 * 1024 * 1024),
        cost_estimate=pl.CostEstimate(
            flops=2 * 2 * tokens * depth * features // 8,
            bytes_accessed=2 * depth * features // 8,
            transcendentals=0,
        ),
    )(info, *operands)


def on_device(queries, keys_values, block_mask, out_weight):
    tokens = queries.shape[1]
    n, f = lax.axis_size("ctx"), lax.axis_size("fsdp")
    index, place = lax.axis_index("ctx"), lax.axis_index("fsdp")
    core, side = index % 2, (index // 2) % 2
    info = jnp.stack([core, side, place]).astype(jnp.int32)
    width = queries.shape[2] // 2
    heads_half = width // HD
    rows = tokens // BLK
    features = out_weight.shape[1] // f
    bf16 = jnp.bfloat16
    parts = [[0,1],[2,3]] if heads_half == 4 else [[h] for h in range(heads_half)]

    pair = lambda i: i ^ 1
    ahead = lambda i: i + 4 if i + 4 < n else None
    across = lambda i: i ^ 2
    upper = lambda i: i + 2 if i & 2 == 0 else None
    lower = lambda i: i - 2 if i & 2 else None
    lanes = lambda start, size: pl.ds(pl.multiple_of(start, HD), size)

    got = moved(keys_values, n, pair, "pair_kv")
    there = moved(queries, n, pair, "pair_q")

    def cut_panels(core, place, ins, outs):
        pieces = []
        for r in range(1, f):
            column = pl.multiple_of(lax.rem(place + r, f) * features, HD)
            for p in range(cuts):
                row = pl.multiple_of(core * width + p * (width // cuts), width // cuts)
                at = pl.ds(p * (width // cuts), width // cuts)
                pieces.append((ins[0].at[pl.ds(row, width // cuts), pl.ds(column, features)],
                               [(slice(None), outs[r - 1].at[at])]))
        return pieces

    cuts = 4 if f == 2 else 1
    panels = copies(
        info, [out_weight], [jax.ShapeDtypeStruct((width, features), bf16)] * (f - 1),
        [(width // cuts, features)] * (cuts * (f - 1)), cut_panels,
    )

    def join(core, ins, outs):
        pieces = []
        for slot, source in enumerate(ins[:2]):
            for head_at, target in outs:
                heads = target.shape[0]
                here = lanes(core * width + head_at * HD, heads * HD)
                pieces.append((source.at[:, 0, :, here], [
                    ((slice(None), slice(None), slice(h * HD, (h + 1) * HD)), target.at[h, slot])
                    for h in range(heads)
                ]))
        return pieces

    pair_shape = lambda heads: jax.ShapeDtypeStruct((heads, 2, 2, tokens, HD), bf16)
    held = lambda heads: (2, tokens, heads * HD)
    first, = copies(
        info, [keys_values, got, *panels], [pair_shape(len(parts[0]))], [held(len(parts[0]))] * 2,
        lambda core, place, ins, outs: join(core, ins, [(0, outs[0])]),
    )
    rest = []
    if len(parts) > 1:
        sizes = [len(part) for part in parts[1:]]
        rest = copies(
            info, [keys_values, got, first], [pair_shape(size) for size in sizes],
            [held(size) for size in sizes] * 2,
            lambda core, place, ins, outs: join(
                core, ins, [(p[0], out) for p, out in zip(parts[1:], outs)]),
        )
    own = [first] + list(rest)

    sames = [
        moved_both(panel, n, f, lambda i, k: (i, (k + r) % f), "panel")
        for r, panel in enumerate(panels, 1)
    ]


    blocks = []
    for k, mine in enumerate(own):
        one = moved(mine, n, ahead, f"near{k}")
        swap = moved(one, n, across, f"nearx{k}")
        if k:
            one, = gated([one], *blocks[-1][1:3])
        two = moved(one, n, ahead, f"far{k}")
        if k:
            two, = gated([two], swap, blocks[-1][3])
        extra = moved(jnp.where(side == 0, mine, two), n, across, f"extra{k}")
        blocks.append((one, two, swap, extra))

    mask_there = moved(block_mask, n, pair, "pair_mask")
    table = jnp.stack([
        mask_table(index * rows, rows, block_mask),
        mask_table((index ^ 1) * rows, rows, mask_there),
    ])

    acts = [[] for _ in range(2 * f)]
    ties = []
    for k, part in enumerate(parts):
        after = []
        mine, give, tie = attend(
            info, queries, keys_values, there, got, own[k], blocks[k], table,
            part, heads_half, after + ties[-1:],
        )
        ties.append(tie)
        acts[0].append(mine)
        for r in range(1, f):
            acts[2 * r].append(moved_both(mine, n, f, lambda i, k: (i, (k + r) % f), f"same{k}"))
            acts[2 * r + 1].append(moved_both(give, n, f, lambda i, k: (i ^ 1, (k + r) % f), f"cross{k}"))
        acts[1].append(moved(give, n, pair, f"pair{k}"))
    others = []
    for same in sames:
        same, = gated([same], blocks[-1][3], ties[0])
        others += [same, moved(same, n, pair, "panel_pair")]

    weights = [out_weight, out_weight] + others
    early, late = [], []
    for g in range(2 * f):
        for k, (part, act) in enumerate(zip(parts, acts[g])):
            (late if g and k == len(parts) - 1 else early).append((g, part[0], act))
    before = project(info, early, weights, features, jnp.float32)
    return project(info, late, weights, features, jnp.bfloat16, before)


def solution(mesh):
    in_specs = (
        P(None, "ctx", "fsdp"),
        P(None, None, "ctx", "fsdp"),
        P("ctx", None),
        P("fsdp", None),
    )
    out_specs = P(None, "ctx", "fsdp")
    return jax.shard_map(
        on_device, mesh=mesh, in_specs=in_specs, out_specs=out_specs, check_vma=False
    )
```

```python
import math

import jax
import jax.numpy as jnp
from jax import lax
from jax.experimental import pallas as pl
from jax.experimental.pallas import tpu as pltpu
from jax.sharding import PartitionSpec as P

HD = 128
BLK = 64
WINB = 32
MASKED = -1e30
SCALE = 1.0 / math.sqrt(HD)
VMEM = 60 * 1024 * 1024
GRID = 1.5 * 2.0 ** 21


def moved(array, n, go, name):
    pairs = [(i, go(i)) for i in range(n) if go(i) is not None]
    with jax.named_scope(name):
        return lax.ppermute(array, "ctx", pairs)


def moved_both(array, n, f, go, name):
    pairs = [(i * f + k, go(i, k)[0] * f + go(i, k)[1]) for i in range(n) for k in range(f)]
    with jax.named_scope(name):
        return lax.ppermute(array, ("ctx", "fsdp"), pairs)


def behind(array, *others):
    return lax.optimization_barrier((array,) + others)[0] if others else array


def gated(arrays, *ties):
    ties = [t[(0,) * (t.ndim - 2)][:8] for t in ties]
    some = pl.BlockSpec(memory_space=pl.ANY)
    return pl.pallas_call(
        lambda *refs: None,
        in_specs=[some] * (len(arrays) + len(ties)),
        out_specs=[some] * len(arrays),
        out_shape=[jax.ShapeDtypeStruct(a.shape, a.dtype) for a in arrays],
        input_output_aliases={k: k for k in range(len(arrays))},
        compiler_params=pltpu.CompilerParams(vmem_limit_bytes=1024 * 1024),
        cost_estimate=pl.CostEstimate(flops=0, bytes_accessed=0, transcendentals=0),
    )(*arrays, *ties)


def mask_table(first_block, rows, mask_rows):
    count = WINB + rows
    query = jnp.arange(rows)
    gap = WINB + query[None, :] - jnp.arange(count)[:, None]
    present = (first_block - WINB + jnp.arange(count) >= 0)[:, None]
    clean = (gap >= 0) & (gap < WINB) & present
    offsets = jnp.arange(WINB)
    picked = ((gap - 1)[:, :, None] == offsets[None, None, :]) & (mask_rows[None] == 1)
    noisy = jnp.any(picked, axis=2) & present
    own_clean = jnp.zeros((rows, rows), bool)
    own_noisy = jnp.eye(rows, dtype=bool)
    allowed = jnp.concatenate(
        [jnp.concatenate([clean, noisy], 1), jnp.concatenate([own_clean, own_noisy], 1)], 0
    )
    table = jnp.where(allowed, 0.0, MASKED).astype(jnp.float32)
    table = jnp.concatenate([table, jnp.ones((count + rows, 1), jnp.float32)], 1)
    table = jnp.pad(table, ((0, 0), (0, 16 - table.shape[1]))).astype(jnp.bfloat16)
    table = jnp.repeat(table.reshape(-1, rows, 16).transpose(0, 2, 1), BLK, axis=2)
    return table


def copies(info, sources, outs, shapes, plan):
    total = sum(math.prod(o.shape) for o in outs)

    def kernel(info, *refs):
        ins, rest = refs[:len(sources)], refs[len(sources):]
        pieces = plan(info[0], info[2], ins, rest[:len(outs)])
        room, arrive, leave = rest[len(outs):-2], rest[-2], rest[-1]
        reads = [
            pltpu.make_async_copy(source, held, arrive.at[k])
            for k, ((source, _), held) in enumerate(zip(pieces, room))
        ]
        for read in reads:
            read.start()
        writes = []
        for read, (_, targets), held in zip(reads, pieces, room):
            read.wait()
            for part, target in targets:
                write = pltpu.make_async_copy(held.at[part], target, leave.at[len(writes)])
                write.start()
                writes.append(write)
        for write in writes:
            write.wait()

    return pl.pallas_call(
        kernel,
        grid_spec=pltpu.PrefetchScalarGridSpec(
            num_scalar_prefetch=1,
            grid=(),
            in_specs=[pl.BlockSpec(memory_space=pl.ANY)] * len(sources),
            out_specs=[pl.BlockSpec(memory_space=pl.ANY)] * len(outs),
            scratch_shapes=[
                *[pltpu.VMEM(shape, jnp.bfloat16) for shape in shapes],
                pltpu.SemaphoreType.DMA((len(shapes),)),
                pltpu.SemaphoreType.DMA((32,)),
            ],
        ),
        out_shape=[jax.ShapeDtypeStruct(o.shape, o.dtype) for o in outs],
        compiler_params=pltpu.CompilerParams(vmem_limit_bytes=VMEM),
        cost_estimate=pl.CostEstimate(flops=0, bytes_accessed=total, transcendentals=0),
    )(info, *sources)


def exponentials(x):
    high = (x + GRID) - GRID
    low = ((x - high) * math.log(2.0)).astype(jnp.bfloat16)
    low = low + low * low * jnp.bfloat16(0.5)
    expo = jnp.exp2(high.astype(jnp.bfloat16))
    return expo + expo * low


def attend_kernel(tokens, info, *refs):
    core, side = info[0], info[1]
    views, (own, one, two, swap, extra), refs = refs[:4], refs[4:9], refs[-7:]
    table, mine, give, tie, keys, values, least = refs
    tie[...] = jnp.zeros_like(tie)
    rows = tokens // BLK
    slots = WINB * BLK // tokens + 2
    back = WINB * BLK // (2 * tokens)

    def place(ref, pair):
        for slot in range(2):
            half = core if slot == 0 else 1 - core
            keys[pair * 2 + half] = ref[0, slot, 0].T
            values[pair * 2 + half] = ref[0, slot, 1]

    place(two, 0)
    place(one, 2)
    place(swap, jnp.where(side == 0, 3, 1))
    place(own, back)

    place(extra, jnp.where(side == 0, 1, 3))
    for tile in range(2):
        keys[slots + tile] = views[2 * tile + 1][0, 0].T

    spot = lax.broadcasted_iota(jnp.int32, (2 * tokens, HD), 0) // BLK
    lane = lax.broadcasted_iota(jnp.int32, (2 * tokens, HD), 1)
    hot = jnp.where(spot == lane, 1.0, 0.0)
    rest = jnp.zeros((HD - table.shape[2], tokens), jnp.bfloat16)

    def operands(tile, k):
        half = core if tile == 0 else 1 - core
        if k == slots - 1:
            key, value = keys[slots + tile], views[2 * tile + 1][1, 0]
        else:
            key, value = keys[half + k], values[half + k]
        return (jnp.concatenate([key, table[tile, k], rest], 0),
                jnp.concatenate([value, jnp.ones_like(value)], 1))

    def store(tile, out):
        (mine if tile == 0 else give)[...] = out.astype(jnp.bfloat16).reshape(2, tokens, HD)

    shift_lane = 2 * rows
    ones = jnp.ones((16, HD), jnp.bfloat16)
    longest = None
    for k in range(slots + 2):
        key = keys[k]
        size = jnp.dot(ones, key * key, preferred_element_type=jnp.float32)
        longest = size if longest is None else jnp.maximum(longest, size)
    longest = jnp.max(longest, axis=1, keepdims=True)[0:1] * 1.03
    queries = []
    for tile in range(2):
        query = views[2 * tile][...].reshape(2 * tokens, HD)
        size = jnp.dot(query * query, jnp.ones((HD, HD), jnp.bfloat16),
                       preferred_element_type=jnp.float32)
        bound = jnp.sqrt(size * longest)
        extra = jnp.where(lane == shift_lane, -bound, hot).astype(jnp.bfloat16)
        queries.append(jnp.concatenate([query, extra], 1))

    steps = [(tile, k) for tile in range(2) for k in range(0, slots, 2)]
    totals = [None, None]

    def scores_of(tile, k):
        key = jnp.concatenate([operands(tile, j)[0] for j in range(k, min(k + 2, slots))], 1)
        return jnp.dot(queries[tile], key, preferred_element_type=jnp.float32)

    def add(tile, k, expo):
        value = jnp.concatenate([operands(tile, j)[1] for j in range(k, min(k + 2, slots))], 0)
        part = jnp.dot(expo, value, preferred_element_type=jnp.float32)
        totals[tile] = part if totals[tile] is None else totals[tile] + part

    scores, last = scores_of(*steps[0]), None
    for at, step in enumerate(steps):
        upcoming = scores_of(*steps[at + 1]) if at + 1 < len(steps) else None
        if last is not None:
            add(*last)
        last = (*step, exponentials(scores * (SCALE * math.log2(math.e))))
        scores = upcoming
    add(*last)
    low_sum = None
    for tile, total in enumerate(totals):
        sums = total[:, HD:]
        store(tile, total[:, :HD] / sums)
        smallest = jnp.min(sums.reshape(-1, 8, HD), axis=0)
        low_sum = smallest if low_sum is None else jnp.minimum(low_sum, smallest)
    least[...] = low_sum

    @pl.when(jnp.logical_not(jnp.min(least[...]) > 2.0 ** -40))
    def _():
        for tile in range(2):
            query = views[2 * tile][...].reshape(2 * tokens, HD)
            query = jnp.concatenate([query, hot.astype(jnp.bfloat16)], 1)
            pieces = [operands(tile, k) for k in range(slots)]
            scores = jnp.concatenate(
                [jnp.dot(query, key, preferred_element_type=jnp.float32) for key, _ in pieces], 1)
            top = jnp.max(scores, axis=1, keepdims=True)
            expo = jnp.exp((scores - top) * SCALE).astype(jnp.bfloat16)
            total = jnp.dot(expo, jnp.concatenate([value for _, value in pieces], 0),
                            preferred_element_type=jnp.float32)
            store(tile, total[:, :HD] / total[:, HD:])


def attend(info, queries, keys_values, there, got, own, blocks, table, part, heads_half, after):
    tokens = queries.shape[1]
    slots = WINB * BLK // tokens + 2
    count, first = len(part), part[0]
    here = lambda h, info: (0, 0, info[0] * heads_half + first + h)
    noisy = lambda h, info: (0, 1, 0, info[0] * heads_half + first + h)
    query_spec = pl.BlockSpec((2, tokens, HD), here)
    noisy_spec = pl.BlockSpec((2, 1, tokens, HD), noisy)
    chunk = pl.BlockSpec((1, 2, 2, tokens, HD), lambda h, info: (h, 0, 0, 0, 0))
    out_spec = pl.BlockSpec((2, tokens, HD), lambda h, info: (0, 0, h))
    out = jax.ShapeDtypeStruct((2, tokens, count * HD), jnp.bfloat16)
    work = count * 2 * 2 * tokens * slots * tokens
    return pl.pallas_call(
        lambda *refs: attend_kernel(tokens, *refs),
        grid_spec=pltpu.PrefetchScalarGridSpec(
            num_scalar_prefetch=1,
            grid=(count,),
            in_specs=[
                query_spec, noisy_spec, query_spec, noisy_spec, *[chunk] * 5,
                *[pl.BlockSpec(memory_space=pl.ANY)] * len(after),
                pl.BlockSpec(table.shape, lambda h, info: (0, 0, 0, 0)),
            ],
            out_specs=[out_spec, out_spec, pl.BlockSpec((8, HD), lambda h, info: (0, 0))],
            scratch_shapes=[
                pltpu.VMEM((slots + 2, HD, tokens), jnp.bfloat16),
                pltpu.VMEM((slots, tokens, HD), jnp.bfloat16),
                pltpu.VMEM((8, HD), jnp.float32),
            ],
        ),
        out_shape=[out, out, jax.ShapeDtypeStruct((8, HD), jnp.float32)],
        compiler_params=pltpu.CompilerParams(vmem_limit_bytes=VMEM),
        cost_estimate=pl.CostEstimate(
            flops=work * 8, bytes_accessed=count * 64 * 1024, transcendentals=0
        ),
    )(info, queries, keys_values, there, got, own, *blocks, *after, table)


def project_kernel(count, groups, add, info, *refs):
    out = refs[-1]
    acts, weights = refs[:count], refs[count:count + groups]
    act = jnp.concatenate([a[...].reshape(-1, a.shape[2]) for a in acts], 1)
    weight = jnp.concatenate([w[...] for w in weights], 0)
    total = jnp.dot(act, weight, preferred_element_type=jnp.float32)
    if add:
        total = total + refs[count + groups][...].reshape(total.shape)
    out[...] = total.astype(out.dtype).reshape(out.shape)


def project(info, pieces, weights, features, dtype, before=None):
    tokens = pieces[0][2].shape[1]
    tile = min(512, features)
    steps = features // tile
    half = weights[0].shape[0] // 2
    used, specs = [], []
    for group, first, act in pieces:
        wide = act.shape[2] if first * HD % act.shape[2] == 0 else HD
        per = half // wide
        for at in range(first * HD // wide, (first * HD + act.shape[2]) // wide):
            used.append(weights[group])
            if group == 0:
                row = lambda s, info, at=at, per=per: (info[0] * per + at, info[2] * steps + s)
            elif group == 1:
                row = lambda s, info, at=at, per=per: (
                    (1 - info[0]) * per + at, info[2] * steps + s)
            else:
                row = lambda s, info, at=at: (at, s)
            specs.append(pl.BlockSpec((wide, tile), row))
    flat = [act for _, _, act in pieces]
    spec = pl.BlockSpec((2, tokens, tile), lambda s, info: (0, 0, s))
    specs = [pl.BlockSpec(a.shape, lambda s, info: (0, 0, 0)) for a in flat] + specs
    operands = flat + used
    if before is not None:
        specs.append(spec)
        operands.append(before)
    depth = sum(a.shape[2] for a in flat)
    return pl.pallas_call(
        lambda *refs: project_kernel(len(flat), len(used), before is not None, *refs),
        grid_spec=pltpu.PrefetchScalarGridSpec(
            num_scalar_prefetch=1, grid=(steps,), in_specs=specs, out_specs=spec
        ),
        out_shape=jax.ShapeDtypeStruct((2, tokens, features), dtype),
        compiler_params=pltpu.CompilerParams(vmem_limit_bytes=40 * 1024 * 1024),
        cost_estimate=pl.CostEstimate(
            flops=2 * 2 * tokens * depth * features // 8,
            bytes_accessed=2 * depth * features // 8,
            transcendentals=0,
        ),
    )(info, *operands)


def on_device(queries, keys_values, block_mask, out_weight):
    tokens = queries.shape[1]
    n, f = lax.axis_size("ctx"), lax.axis_size("fsdp")
    index, place = lax.axis_index("ctx"), lax.axis_index("fsdp")
    core, side = index % 2, (index // 2) % 2
    info = jnp.stack([core, side, place]).astype(jnp.int32)
    width = queries.shape[2] // 2
    heads_half = width // HD
    rows = tokens // BLK
    features = out_weight.shape[1] // f
    bf16 = jnp.bfloat16
    parts = [[0,1],[2,3]] if heads_half == 4 else [[h] for h in range(heads_half)]

    pair = lambda i: i ^ 1
    ahead = lambda i: i + 4 if i + 4 < n else None
    across = lambda i: i ^ 2
    upper = lambda i: i + 2 if i & 2 == 0 else None
    lower = lambda i: i - 2 if i & 2 else None
    lanes = lambda start, size: pl.ds(pl.multiple_of(start, HD), size)

    got = moved(keys_values, n, pair, "pair_kv")
    there = moved(queries, n, pair, "pair_q")

    def cut_panels(core, place, ins, outs):
        pieces = []
        for r in range(1, f):
            column = pl.multiple_of(lax.rem(place + r, f) * features, HD)
            for p in range(cuts):
                row = pl.multiple_of(core * width + p * (width // cuts), width // cuts)
                at = pl.ds(p * (width // cuts), width // cuts)
                pieces.append((ins[0].at[pl.ds(row, width // cuts), pl.ds(column, features)],
                               [(slice(None), outs[r - 1].at[at])]))
        return pieces

    cuts = 4 if f == 2 else 1
    panels = copies(
        info, [out_weight], [jax.ShapeDtypeStruct((width, features), bf16)] * (f - 1),
        [(width // cuts, features)] * (cuts * (f - 1)), cut_panels,
    )

    def join(core, ins, outs):
        pieces = []
        for slot, source in enumerate(ins[:2]):
            for head_at, target in outs:
                heads = target.shape[0]
                here = lanes(core * width + head_at * HD, heads * HD)
                pieces.append((source.at[:, 0, :, here], [
                    ((slice(None), slice(None), slice(h * HD, (h + 1) * HD)), target.at[h, slot])
                    for h in range(heads)
                ]))
        return pieces

    pair_shape = lambda heads: jax.ShapeDtypeStruct((heads, 2, 2, tokens, HD), bf16)
    held = lambda heads: (2, tokens, heads * HD)
    first, = copies(
        info, [keys_values, got, *panels], [pair_shape(len(parts[0]))], [held(len(parts[0]))] * 2,
        lambda core, place, ins, outs: join(core, ins, [(0, outs[0])]),
    )
    rest = []
    if len(parts) > 1:
        sizes = [len(part) for part in parts[1:]]
        rest = copies(
            info, [keys_values, got, first], [pair_shape(size) for size in sizes],
            [held(size) for size in sizes] * 2,
            lambda core, place, ins, outs: join(
                core, ins, [(p[0], out) for p, out in zip(parts[1:], outs)]),
        )
    own = [first] + list(rest)

    sames = [
        moved_both(panel, n, f, lambda i, k: (i, (k + r) % f), "panel")
        for r, panel in enumerate(panels, 1)
    ]


    blocks = []
    for k, mine in enumerate(own):
        one = moved(mine, n, ahead, f"near{k}")
        swap = moved(one, n, across, f"nearx{k}")
        if k:
            one, = gated([one], *blocks[-1][1:3])
        two = moved(one, n, ahead, f"far{k}")
        if k:
            two, = gated([two], swap, blocks[-1][3])
        extra = moved(jnp.where(side == 0, mine, two), n, across, f"extra{k}")
        blocks.append((one, two, swap, extra))

    mask_there = moved(block_mask, n, pair, "pair_mask")
    table = jnp.stack([
        mask_table(index * rows, rows, block_mask),
        mask_table((index ^ 1) * rows, rows, mask_there),
    ])

    acts = [[] for _ in range(2 * f)]
    ties = []
    for k, part in enumerate(parts):
        after = []
        mine, give, tie = attend(
            info, queries, keys_values, there, got, own[k], blocks[k], table,
            part, heads_half, after + ties[-1:],
        )
        ties.append(tie)
        acts[0].append(mine)
        for r in range(1, f):
            acts[2 * r].append(moved_both(mine, n, f, lambda i, k: (i, (k + r) % f), f"same{k}"))
            acts[2 * r + 1].append(moved_both(give, n, f, lambda i, k: (i ^ 1, (k + r) % f), f"cross{k}"))
        acts[1].append(moved(give, n, pair, f"pair{k}"))
    others = []
    for same in sames:
        same, = gated([same], blocks[-1][3], ties[0])
        others += [same, moved(same, n, pair, "panel_pair")]

    weights = [out_weight, out_weight] + others
    early, late = [], []
    for g in range(2 * f):
        for k, (part, act) in enumerate(zip(parts, acts[g])):
            (late if g and k == len(parts) - 1 else early).append((g, part[0], act))
    before = project(info, early, weights, features, jnp.float32)
    return project(info, late, weights, features, jnp.bfloat16, before)


def solution(mesh):
    in_specs = (
        P(None, "ctx", "fsdp"),
        P(None, None, "ctx", "fsdp"),
        P("ctx", None),
        P("fsdp", None),
    )
    out_specs = P(None, "ctx", "fsdp")
    return jax.shard_map(
        on_device, mesh=mesh, in_specs=in_specs, out_specs=out_specs, check_vma=False
    )
```

```python
import math

import jax
import jax.numpy as jnp
from jax import lax
from jax.experimental import pallas as pl
from jax.experimental.pallas import tpu as pltpu
from jax.sharding import PartitionSpec as P

HD = 128
BLK = 64
WINB = 32
MASKED = -1e30
SCALE = 1.0 / math.sqrt(HD)
VMEM = 60 * 1024 * 1024


def moved(array, n, go, name):
    pairs = [(i, go(i)) for i in range(n) if go(i) is not None]
    with jax.named_scope(name):
        return lax.ppermute(array, "ctx", pairs)


def moved_both(array, n, f, go, name):
    pairs = [(i * f + k, go(i, k)[0] * f + go(i, k)[1]) for i in range(n) for k in range(f)]
    with jax.named_scope(name):
        return lax.ppermute(array, ("ctx", "fsdp"), pairs)


def behind(array, *others):
    return lax.optimization_barrier((array,) + others)[0] if others else array


def gated(arrays, *ties):
    ties = [t[(0,) * (t.ndim - 2)][:8] for t in ties]
    some = pl.BlockSpec(memory_space=pl.ANY)
    return pl.pallas_call(
        lambda *refs: None,
        in_specs=[some] * (len(arrays) + len(ties)),
        out_specs=[some] * len(arrays),
        out_shape=[jax.ShapeDtypeStruct(a.shape, a.dtype) for a in arrays],
        input_output_aliases={k: k for k in range(len(arrays))},
        compiler_params=pltpu.CompilerParams(vmem_limit_bytes=1024 * 1024),
        cost_estimate=pl.CostEstimate(flops=0, bytes_accessed=0, transcendentals=0),
    )(*arrays, *ties)


def mask_table(first_block, rows, mask_rows):
    count = WINB + rows
    query = jnp.arange(rows)
    gap = WINB + query[None, :] - jnp.arange(count)[:, None]
    present = (first_block - WINB + jnp.arange(count) >= 0)[:, None]
    clean = (gap >= 0) & (gap < WINB) & present
    offsets = jnp.arange(WINB)
    picked = ((gap - 1)[:, :, None] == offsets[None, None, :]) & (mask_rows[None] == 1)
    noisy = jnp.any(picked, axis=2) & present
    own_clean = jnp.zeros((rows, rows), bool)
    own_noisy = jnp.eye(rows, dtype=bool)
    allowed = jnp.concatenate(
        [jnp.concatenate([clean, noisy], 1), jnp.concatenate([own_clean, own_noisy], 1)], 0
    )
    table = jnp.where(allowed, 0.0, MASKED).astype(jnp.float32)
    return jnp.repeat(table.reshape(-1, rows, 2 * rows).transpose(0, 2, 1), BLK, axis=2)


def copies(info, sources, outs, shapes, plan, limit=8 * 1024 * 1024):
    total = sum(math.prod(o.shape) for o in outs)

    def kernel(info, *refs):
        ins, rest = refs[:len(sources)], refs[len(sources):]
        pieces = plan(info[0], info[2], ins, rest[:len(outs)])
        room, arrive, leave = rest[len(outs):-2], rest[-2], rest[-1]
        reads = [
            pltpu.make_async_copy(source, held, arrive.at[k])
            for k, ((source, _), held) in enumerate(zip(pieces, room))
        ]
        for read in reads:
            read.start()
        writes = []
        for read, (_, targets), held in zip(reads, pieces, room):
            read.wait()
            for part, target in targets:
                write = pltpu.make_async_copy(held.at[part], target, leave.at[len(writes)])
                write.start()
                writes.append(write)
        for write in writes:
            write.wait()

    return pl.pallas_call(
        kernel,
        grid_spec=pltpu.PrefetchScalarGridSpec(
            num_scalar_prefetch=1,
            grid=(),
            in_specs=[pl.BlockSpec(memory_space=pl.ANY)] * len(sources),
            out_specs=[pl.BlockSpec(memory_space=pl.ANY)] * len(outs),
            scratch_shapes=[
                *[pltpu.VMEM(shape, jnp.bfloat16) for shape in shapes],
                pltpu.SemaphoreType.DMA((len(shapes),)),
                pltpu.SemaphoreType.DMA((32,)),
            ],
        ),
        out_shape=[jax.ShapeDtypeStruct(o.shape, o.dtype) for o in outs],
        compiler_params=pltpu.CompilerParams(vmem_limit_bytes=limit),
        cost_estimate=pl.CostEstimate(flops=0, bytes_accessed=total, transcendentals=0),
    )(info, *sources)


def attend_kernel(tokens, info, *refs):
    core, side = info[0], info[1]
    views, (own, one, two, swap, extra), refs = refs[:4], refs[4:9], refs[-7:]
    table, mine, give, tie, keys, values, least = refs
    tie[...] = jnp.zeros_like(tie)
    rows = tokens // BLK
    slots = WINB * BLK // tokens + 2
    back = WINB * BLK // (2 * tokens)

    def place(ref, pair):
        for slot in range(2):
            half = core if slot == 0 else 1 - core
            keys[pair * 2 + half] = ref[0, slot, 0].T
            values[pair * 2 + half] = ref[0, slot, 1]

    place(two, 0)
    place(one, 2)
    place(swap, jnp.where(side == 0, 3, 1))
    place(own, back)

    place(extra, jnp.where(side == 0, 1, 3))
    for tile in range(2):
        keys[slots + tile] = views[2 * tile + 1][0, 0].T

    def operands(tile, k):
        half = core if tile == 0 else 1 - core
        if k == slots - 1:
            return keys[slots + tile], views[2 * tile + 1][1, 0]
        return keys[half + k], values[half + k]

    def store(tile, out):
        (mine if tile == 0 else give)[...] = out.astype(jnp.bfloat16).reshape(2, tokens, HD)

    ones = jnp.ones((16, HD), jnp.bfloat16)
    longest = None
    for k in range(slots + 2):
        key = keys[k]
        size = jnp.dot(ones, key * key, preferred_element_type=jnp.float32)
        longest = size if longest is None else jnp.maximum(longest, size)
    longest = jnp.max(longest, axis=1, keepdims=True)[0:1] * 1.03
    queries, shifts = [], []
    for tile in range(2):
        query = views[2 * tile][...].reshape(2 * tokens, HD)
        size = jnp.dot(query * query, jnp.ones((HD, HD), jnp.bfloat16),
                       preferred_element_type=jnp.float32)
        queries.append(query)
        shifts.append((jnp.sqrt(size * longest) * SCALE)[:, 0:1])

    steps = [(tile, k) for tile in range(2) for k in (*range(0, slots - 1, 2), slots - 1)]
    totals, sums = [None, None], [None, None]

    def runs_of(k):
        return range(k, k + 1 if k == slots - 1 else min(k + 2, slots - 1))

    def scores_of(tile, k, everyone=False):
        key = jnp.concatenate([operands(tile, j)[0] for j in runs_of(k)], 1)
        bias = jnp.concatenate([table[tile, j] for j in runs_of(k)], 1)
        query = queries[tile]
        if k == slots - 1 and not everyone:
            query, bias = query[tokens:], bias[rows:]
        return jnp.dot(query, key, preferred_element_type=jnp.float32), bias

    def weights_of(scores, bias, shift):
        count, wide = scores.shape
        shifted = scores * SCALE - shift[2 * tokens - count:]
        shifted = shifted.reshape(count // BLK, BLK, wide) + bias[:, None, :]
        return jnp.exp(shifted.reshape(count, wide))

    def plus(total, part):
        if total is None or total.shape == part.shape:
            return part if total is None else total + part
        half = part.shape[0]
        return jnp.concatenate([total[:-half], total[-half:] + part], 0)

    def add(tile, k, expo):
        value = jnp.concatenate([operands(tile, j)[1] for j in runs_of(k)], 0)
        totals[tile] = plus(
            totals[tile], jnp.dot(expo, value, preferred_element_type=jnp.float32))

    scores, last = scores_of(*steps[0]), None
    for at, step in enumerate(steps):
        upcoming = scores_of(*steps[at + 1]) if at + 1 < len(steps) else None
        if last is not None:
            add(*last)
        tile = step[0]
        expo = weights_of(*scores, shifts[tile])
        for lanes in range(0, expo.shape[1], HD):
            sums[tile] = plus(sums[tile], expo[:, lanes:lanes + HD])
        last = (*step, expo.astype(jnp.bfloat16))
        scores = upcoming
    add(*last)
    low_sum = None
    for tile, total in enumerate(totals):
        whole = jnp.sum(sums[tile], axis=1, keepdims=True)
        store(tile, total / whole)
        smallest = jnp.min(whole, axis=0, keepdims=True)
        low_sum = smallest if low_sum is None else jnp.minimum(low_sum, smallest)
    least[...] = jnp.broadcast_to(low_sum, least.shape)

    @pl.when(jnp.logical_not(jnp.min(least[...]) > 2.0 ** -40))
    def _():
        for tile in range(2):
            runs = [scores_of(tile, k, True) for t, k in steps if t == tile]
            scores = jnp.concatenate([score for score, _ in runs], 1) * SCALE
            bias = jnp.concatenate([bias for _, bias in runs], 1)
            wide = scores.shape[1]
            scores = (scores.reshape(2 * rows, BLK, wide) + bias[:, None, :]).reshape(
                2 * tokens, wide)
            expo = jnp.exp(scores - jnp.max(scores, axis=1, keepdims=True))
            value = jnp.concatenate([operands(tile, k)[1] for k in range(slots)], 0)
            total = jnp.dot(expo.astype(jnp.bfloat16), value, preferred_element_type=jnp.float32)
            store(tile, total / jnp.sum(expo, axis=1, keepdims=True))


def attend(info, queries, keys_values, there, got, own, blocks, table, part, heads_half, after):
    tokens = queries.shape[1]
    slots = WINB * BLK // tokens + 2
    count, first = len(part), part[0]
    here = lambda h, info: (0, 0, info[0] * heads_half + first + h)
    noisy = lambda h, info: (0, 1, 0, info[0] * heads_half + first + h)
    query_spec = pl.BlockSpec((2, tokens, HD), here)
    noisy_spec = pl.BlockSpec((2, 1, tokens, HD), noisy)
    chunk = pl.BlockSpec((1, 2, 2, tokens, HD), lambda h, info: (h, 0, 0, 0, 0))
    out_spec = pl.BlockSpec((2, tokens, HD), lambda h, info: (0, 0, h))
    out = jax.ShapeDtypeStruct((2, tokens, count * HD), jnp.bfloat16)
    work = count * 2 * 2 * tokens * slots * tokens
    return pl.pallas_call(
        lambda *refs: attend_kernel(tokens, *refs),
        grid_spec=pltpu.PrefetchScalarGridSpec(
            num_scalar_prefetch=1,
            grid=(count,),
            in_specs=[
                query_spec, noisy_spec, query_spec, noisy_spec, *[chunk] * 5,
                *[pl.BlockSpec(memory_space=pl.ANY)] * len(after),
                pl.BlockSpec(table.shape, lambda h, info: (0, 0, 0, 0)),
            ],
            out_specs=[out_spec, out_spec, pl.BlockSpec((8, HD), lambda h, info: (0, 0))],
            scratch_shapes=[
                pltpu.VMEM((slots + 2, HD, tokens), jnp.bfloat16),
                pltpu.VMEM((slots, tokens, HD), jnp.bfloat16),
                pltpu.VMEM((8, HD), jnp.float32),
            ],
        ),
        out_shape=[out, out, jax.ShapeDtypeStruct((8, HD), jnp.float32)],
        compiler_params=pltpu.CompilerParams(vmem_limit_bytes=VMEM),
        cost_estimate=pl.CostEstimate(
            flops=work * 8, bytes_accessed=count * 64 * 1024, transcendentals=0
        ),
    )(info, queries, keys_values, there, got, own, *blocks, *after, table)


def project_kernel(count, groups, add, info, *refs):
    out = refs[-1]
    acts, weights = refs[:count], refs[count:count + groups]
    act = jnp.concatenate([a[...].reshape(-1, a.shape[2]) for a in acts], 1)
    weight = jnp.concatenate([w[...] for w in weights], 0)
    total = jnp.dot(act, weight, preferred_element_type=jnp.float32)
    if add:
        total = total + refs[count + groups][...].reshape(total.shape)
    out[...] = total.astype(out.dtype).reshape(out.shape)


def project(info, pieces, weights, features, dtype, before=None):
    tokens = pieces[0][2].shape[1]
    tile = min(512, features)
    steps = features // tile
    half = weights[0].shape[0] // 2
    used, specs = [], []
    for group, first, act in pieces:
        wide = act.shape[2] if first * HD % act.shape[2] == 0 else HD
        per = half // wide
        for at in range(first * HD // wide, (first * HD + act.shape[2]) // wide):
            used.append(weights[group])
            if group == 0:
                row = lambda s, info, at=at, per=per: (info[0] * per + at, info[2] * steps + s)
            elif group == 1:
                row = lambda s, info, at=at, per=per: (
                    (1 - info[0]) * per + at, info[2] * steps + s)
            else:
                row = lambda s, info, at=at: (at, s)
            specs.append(pl.BlockSpec((wide, tile), row))
    flat = [act for _, _, act in pieces]
    spec = pl.BlockSpec((2, tokens, tile), lambda s, info: (0, 0, s))
    specs = [pl.BlockSpec(a.shape, lambda s, info: (0, 0, 0)) for a in flat] + specs
    operands = flat + used
    if before is not None:
        specs.append(spec)
        operands.append(before)
    depth = sum(a.shape[2] for a in flat)
    return pl.pallas_call(
        lambda *refs: project_kernel(len(flat), len(used), before is not None, *refs),
        grid_spec=pltpu.PrefetchScalarGridSpec(
            num_scalar_prefetch=1, grid=(steps,), in_specs=specs, out_specs=spec
        ),
        out_shape=jax.ShapeDtypeStruct((2, tokens, features), dtype),
        compiler_params=pltpu.CompilerParams(vmem_limit_bytes=40 * 1024 * 1024),
        cost_estimate=pl.CostEstimate(
            flops=2 * 2 * tokens * depth * features // 8,
            bytes_accessed=2 * depth * features // 8,
            transcendentals=0,
        ),
    )(info, *operands)


def on_device(queries, keys_values, block_mask, out_weight):
    tokens = queries.shape[1]
    n, f = lax.axis_size("ctx"), lax.axis_size("fsdp")
    index, place = lax.axis_index("ctx"), lax.axis_index("fsdp")
    core, side = index % 2, (index // 2) % 2
    info = jnp.stack([core, side, place]).astype(jnp.int32)
    width = queries.shape[2] // 2
    heads_half = width // HD
    rows = tokens // BLK
    features = out_weight.shape[1] // f
    bf16 = jnp.bfloat16
    parts = [[0,1],[2,3]] if heads_half == 4 else [[h] for h in range(heads_half)]

    pair = lambda i: i ^ 1
    ahead = lambda i: i + 4 if i + 4 < n else None
    across = lambda i: i ^ 2
    upper = lambda i: i + 2 if i & 2 == 0 else None
    lower = lambda i: i - 2 if i & 2 else None
    lanes = lambda start, size: pl.ds(pl.multiple_of(start, HD), size)

    got = moved(keys_values, n, pair, "pair_kv")
    there = moved(queries, n, pair, "pair_q")

    def cut_panels(core, place, ins, outs):
        pieces = []
        for r in range(1, f):
            column = pl.multiple_of(lax.rem(place + r, f) * features, HD)
            for p in range(cuts):
                row = pl.multiple_of(core * width + p * (width // cuts), width // cuts)
                at = pl.ds(p * (width // cuts), width // cuts)
                pieces.append((ins[0].at[pl.ds(row, width // cuts), pl.ds(column, features)],
                               [(slice(None), outs[r - 1].at[at])]))
        return pieces

    cuts = 4 if f == 2 else 1
    panels = copies(
        info, [out_weight], [jax.ShapeDtypeStruct((width, features), bf16)] * (f - 1),
        [(width // cuts, features)] * (cuts * (f - 1)), cut_panels, VMEM,
    )

    def join(core, ins, outs):
        pieces = []
        for slot, source in enumerate(ins[:2]):
            for head_at, target in outs:
                heads = target.shape[0]
                here = lanes(core * width + head_at * HD, heads * HD)
                pieces.append((source.at[:, 0, :, here], [
                    ((slice(None), slice(None), slice(h * HD, (h + 1) * HD)), target.at[h, slot])
                    for h in range(heads)
                ]))
        return pieces

    pair_shape = lambda heads: jax.ShapeDtypeStruct((heads, 2, 2, tokens, HD), bf16)
    held = lambda heads: (2, tokens, heads * HD)
    first, = copies(
        info, [keys_values, got, *panels], [pair_shape(len(parts[0]))], [held(len(parts[0]))] * 2,
        lambda core, place, ins, outs: join(core, ins, [(0, outs[0])]),
    )
    rest = []
    if len(parts) > 1:
        sizes = [len(part) for part in parts[1:]]
        rest = copies(
            info, [keys_values, got, first], [pair_shape(size) for size in sizes],
            [held(size) for size in sizes] * 2,
            lambda core, place, ins, outs: join(
                core, ins, [(p[0], out) for p, out in zip(parts[1:], outs)]),
        )
    own = [first] + list(rest)

    sames = [
        moved_both(panel, n, f, lambda i, k: (i, (k + r) % f), "panel")
        for r, panel in enumerate(panels, 1)
    ]


    blocks = []
    for k, mine in enumerate(own):
        one = moved(mine, n, ahead, f"near{k}")
        swap = moved(one, n, across, f"nearx{k}")
        if k:
            one, = gated([one], *blocks[-1][1:3])
        two = moved(one, n, ahead, f"far{k}")
        if k:
            two, = gated([two], swap, blocks[-1][3])
        extra = moved(jnp.where(side == 0, mine, two), n, across, f"extra{k}")
        blocks.append((one, two, swap, extra))

    mask_there = moved(block_mask, n, pair, "pair_mask")
    table = jnp.stack([
        mask_table(index * rows, rows, block_mask),
        mask_table((index ^ 1) * rows, rows, mask_there),
    ])

    acts = [[] for _ in range(2 * f)]
    ties = []
    for k, part in enumerate(parts):
        after = []
        mine, give, tie = attend(
            info, queries, keys_values, there, got, own[k], blocks[k], table,
            part, heads_half, after + ties[-1:],
        )
        ties.append(tie)
        acts[0].append(mine)
        for r in range(1, f):
            acts[2 * r].append(moved_both(mine, n, f, lambda i, k: (i, (k + r) % f), f"same{k}"))
            acts[2 * r + 1].append(moved_both(give, n, f, lambda i, k: (i ^ 1, (k + r) % f), f"cross{k}"))
        acts[1].append(moved(give, n, pair, f"pair{k}"))
    others = []
    for same in sames:
        same, = gated([same], blocks[-1][3], ties[0])
        others += [same, moved(same, n, pair, "panel_pair")]

    weights = [out_weight, out_weight] + others
    stages = [[], [], []]
    for g in range(2 * f):
        for k, (part, act) in enumerate(zip(parts, acts[g])):
            late = k == len(parts) - 1 and g > 0
            stages[(1 if g % 2 else 2) if late else 0].append((g, part[0], act))
    total = None
    stages = [stage for stage in stages if stage]
    for k, stage in enumerate(stages):
        dtype = jnp.bfloat16 if k == len(stages) - 1 else jnp.float32
        total = project(info, stage, weights, features, dtype, total)
    return total


def solution(mesh):
    in_specs = (
        P(None, "ctx", "fsdp"),
        P(None, None, "ctx", "fsdp"),
        P("ctx", None),
        P("fsdp", None),
    )
    out_specs = P(None, "ctx", "fsdp")
    return jax.shard_map(
        on_device, mesh=mesh, in_specs=in_specs, out_specs=out_specs, check_vma=False
    )
```

```python
import math

import jax
import jax.numpy as jnp
from jax import lax
from jax.experimental import pallas as pl
from jax.experimental.pallas import tpu as pltpu
from jax.sharding import PartitionSpec as P

HD = 128
BLK = 64
WINB = 32
MASKED = -1e30
SCALE = 1.0 / math.sqrt(HD)
VMEM = 60 * 1024 * 1024


def moved(array, n, go, name):
    pairs = [(i, go(i)) for i in range(n) if go(i) is not None]
    with jax.named_scope(name):
        return lax.ppermute(array, "ctx", pairs)


def moved_both(array, n, f, go, name):
    pairs = [(i * f + k, go(i, k)[0] * f + go(i, k)[1]) for i in range(n) for k in range(f)]
    with jax.named_scope(name):
        return lax.ppermute(array, ("ctx", "fsdp"), pairs)


def behind(array, *others):
    return lax.optimization_barrier((array,) + others)[0] if others else array


def gated(arrays, *ties):
    ties = [t[(0,) * (t.ndim - 2)][:8] for t in ties]
    some = pl.BlockSpec(memory_space=pl.ANY)
    return pl.pallas_call(
        lambda *refs: None,
        in_specs=[some] * (len(arrays) + len(ties)),
        out_specs=[some] * len(arrays),
        out_shape=[jax.ShapeDtypeStruct(a.shape, a.dtype) for a in arrays],
        input_output_aliases={k: k for k in range(len(arrays))},
        compiler_params=pltpu.CompilerParams(vmem_limit_bytes=1024 * 1024),
        cost_estimate=pl.CostEstimate(flops=0, bytes_accessed=0, transcendentals=0),
    )(*arrays, *ties)


def mask_table(first_block, rows, mask_rows):
    count = WINB + rows
    query = jnp.arange(rows)
    gap = WINB + query[None, :] - jnp.arange(count)[:, None]
    present = (first_block - WINB + jnp.arange(count) >= 0)[:, None]
    clean = (gap >= 0) & (gap < WINB) & present
    offsets = jnp.arange(WINB)
    picked = ((gap - 1)[:, :, None] == offsets[None, None, :]) & (mask_rows[None] == 1)
    noisy = jnp.any(picked, axis=2) & present
    own_clean = jnp.zeros((rows, rows), bool)
    own_noisy = jnp.eye(rows, dtype=bool)
    allowed = jnp.concatenate(
        [jnp.concatenate([clean, noisy], 1), jnp.concatenate([own_clean, own_noisy], 1)], 0
    )
    table = jnp.where(allowed, 0.0, MASKED).astype(jnp.float32)
    return jnp.repeat(table.reshape(-1, rows, 2 * rows).transpose(0, 2, 1), BLK, axis=2)


def copies(info, sources, outs, shapes, plan, limit=8 * 1024 * 1024):
    total = sum(math.prod(o.shape) for o in outs)

    def kernel(info, *refs):
        ins, rest = refs[:len(sources)], refs[len(sources):]
        pieces = plan(info[0], info[2], ins, rest[:len(outs)])
        room, arrive, leave = rest[len(outs):-2], rest[-2], rest[-1]
        reads = [
            pltpu.make_async_copy(source, held, arrive.at[k])
            for k, ((source, _), held) in enumerate(zip(pieces, room))
        ]
        for read in reads:
            read.start()
        writes = []
        for read, (_, targets), held in zip(reads, pieces, room):
            read.wait()
            for part, target in targets:
                write = pltpu.make_async_copy(held.at[part], target, leave.at[len(writes)])
                write.start()
                writes.append(write)
        for write in writes:
            write.wait()

    return pl.pallas_call(
        kernel,
        grid_spec=pltpu.PrefetchScalarGridSpec(
            num_scalar_prefetch=1,
            grid=(),
            in_specs=[pl.BlockSpec(memory_space=pl.ANY)] * len(sources),
            out_specs=[pl.BlockSpec(memory_space=pl.ANY)] * len(outs),
            scratch_shapes=[
                *[pltpu.VMEM(shape, jnp.bfloat16) for shape in shapes],
                pltpu.SemaphoreType.DMA((len(shapes),)),
                pltpu.SemaphoreType.DMA((32,)),
            ],
        ),
        out_shape=[jax.ShapeDtypeStruct(o.shape, o.dtype) for o in outs],
        compiler_params=pltpu.CompilerParams(vmem_limit_bytes=limit),
        cost_estimate=pl.CostEstimate(flops=0, bytes_accessed=total, transcendentals=0),
    )(info, *sources)


def attend_kernel(tokens, info, *refs):
    core, side = info[0], info[1]
    views, (own, one, two, swap, extra), refs = refs[:4], refs[4:9], refs[-7:]
    table, mine, give, tie, keys, values, least = refs
    tie[...] = jnp.zeros_like(tie)
    rows = tokens // BLK
    slots = WINB * BLK // tokens + 2
    back = WINB * BLK // (2 * tokens)

    def place(ref, pair):
        for slot in range(2):
            half = core if slot == 0 else 1 - core
            keys[pair * 2 + half] = ref[0, slot, 0].T
            values[pair * 2 + half] = ref[0, slot, 1]

    place(two, 0)
    place(one, 2)
    place(swap, jnp.where(side == 0, 3, 1))
    place(own, back)

    place(extra, jnp.where(side == 0, 1, 3))
    for tile in range(2):
        keys[slots + tile] = views[2 * tile + 1][0, 0].T

    def operands(tile, k):
        half = core if tile == 0 else 1 - core
        if k == slots - 1:
            return keys[slots + tile], views[2 * tile + 1][1, 0]
        return keys[half + k], values[half + k]

    def store(tile, out):
        (mine if tile == 0 else give)[...] = out.astype(jnp.bfloat16).reshape(2, tokens, HD)

    ones = jnp.ones((16, HD), jnp.bfloat16)
    longest = None
    for k in range(slots + 2):
        key = keys[k]
        size = jnp.dot(ones, key * key, preferred_element_type=jnp.float32)
        longest = size if longest is None else jnp.maximum(longest, size)
    longest = jnp.max(longest, axis=1, keepdims=True)[0:1] * 1.03
    queries, shifts = [], []
    for tile in range(2):
        query = views[2 * tile][...].reshape(2 * tokens, HD)
        size = jnp.dot(query * query, jnp.ones((HD, HD), jnp.bfloat16),
                       preferred_element_type=jnp.float32)
        queries.append(query)
        shifts.append((jnp.sqrt(size * longest) * SCALE)[:, 0:1])

    steps = [(tile, k) for tile in range(2) for k in range(0, slots, 2)]
    totals, sums = [None, None], [None, None]

    def scores_of(tile, k):
        key = jnp.concatenate([operands(tile, j)[0] for j in range(k, min(k + 2, slots))], 1)
        scores = jnp.dot(queries[tile], key, preferred_element_type=jnp.float32)
        bias = jnp.concatenate([table[tile, j] for j in range(k, min(k + 2, slots))], 1)
        return scores, bias

    def weights_of(tile, scores, bias, shift):
        wide = scores.shape[1]
        shifted = scores * SCALE - shift
        shifted = shifted.reshape(2 * rows, BLK, wide) + bias[:, None, :]
        return jnp.exp(shifted.reshape(2 * tokens, wide))

    def add(tile, k, expo):
        value = jnp.concatenate([operands(tile, j)[1] for j in range(k, min(k + 2, slots))], 0)
        part = jnp.dot(expo, value, preferred_element_type=jnp.float32)
        totals[tile] = part if totals[tile] is None else totals[tile] + part

    scores, last = scores_of(*steps[0]), None
    for at, step in enumerate(steps):
        upcoming = scores_of(*steps[at + 1]) if at + 1 < len(steps) else None
        if last is not None:
            add(*last)
        tile = step[0]
        expo = weights_of(tile, *scores, shifts[tile])
        for lanes in range(0, expo.shape[1], HD):
            part = expo[:, lanes:lanes + HD]
            sums[tile] = part if sums[tile] is None else sums[tile] + part
        last = (*step, expo.astype(jnp.bfloat16))
        scores = upcoming
    add(*last)
    low_sum = None
    for tile, total in enumerate(totals):
        whole = jnp.sum(sums[tile], axis=1, keepdims=True)
        store(tile, total / whole)
        smallest = jnp.min(whole, axis=0, keepdims=True)
        low_sum = smallest if low_sum is None else jnp.minimum(low_sum, smallest)
    least[...] = jnp.broadcast_to(low_sum, least.shape)

    @pl.when(jnp.logical_not(jnp.min(least[...]) > 2.0 ** -40))
    def _():
        for tile in range(2):
            runs = [scores_of(tile, k) for k in range(0, slots, 2)]
            scores = jnp.concatenate([score for score, _ in runs], 1) * SCALE
            bias = jnp.concatenate([bias for _, bias in runs], 1)
            wide = scores.shape[1]
            scores = (scores.reshape(2 * rows, BLK, wide) + bias[:, None, :]).reshape(
                2 * tokens, wide)
            expo = jnp.exp(scores - jnp.max(scores, axis=1, keepdims=True))
            value = jnp.concatenate([operands(tile, k)[1] for k in range(slots)], 0)
            total = jnp.dot(expo.astype(jnp.bfloat16), value, preferred_element_type=jnp.float32)
            store(tile, total / jnp.sum(expo, axis=1, keepdims=True))


def attend(info, queries, keys_values, there, got, own, blocks, table, part, heads_half, after):
    tokens = queries.shape[1]
    slots = WINB * BLK // tokens + 2
    count, first = len(part), part[0]
    here = lambda h, info: (0, 0, info[0] * heads_half + first + h)
    noisy = lambda h, info: (0, 1, 0, info[0] * heads_half + first + h)
    query_spec = pl.BlockSpec((2, tokens, HD), here)
    noisy_spec = pl.BlockSpec((2, 1, tokens, HD), noisy)
    chunk = pl.BlockSpec((1, 2, 2, tokens, HD), lambda h, info: (h, 0, 0, 0, 0))
    out_spec = pl.BlockSpec((2, tokens, HD), lambda h, info: (0, 0, h))
    out = jax.ShapeDtypeStruct((2, tokens, count * HD), jnp.bfloat16)
    work = count * 2 * 2 * tokens * slots * tokens
    return pl.pallas_call(
        lambda *refs: attend_kernel(tokens, *refs),
        grid_spec=pltpu.PrefetchScalarGridSpec(
            num_scalar_prefetch=1,
            grid=(count,),
            in_specs=[
                query_spec, noisy_spec, query_spec, noisy_spec, *[chunk] * 5,
                *[pl.BlockSpec(memory_space=pl.ANY)] * len(after),
                pl.BlockSpec(table.shape, lambda h, info: (0, 0, 0, 0)),
            ],
            out_specs=[out_spec, out_spec, pl.BlockSpec((8, HD), lambda h, info: (0, 0))],
            scratch_shapes=[
                pltpu.VMEM((slots + 2, HD, tokens), jnp.bfloat16),
                pltpu.VMEM((slots, tokens, HD), jnp.bfloat16),
                pltpu.VMEM((8, HD), jnp.float32),
            ],
        ),
        out_shape=[out, out, jax.ShapeDtypeStruct((8, HD), jnp.float32)],
        compiler_params=pltpu.CompilerParams(vmem_limit_bytes=VMEM),
        cost_estimate=pl.CostEstimate(
            flops=work * 8, bytes_accessed=count * 64 * 1024, transcendentals=0
        ),
    )(info, queries, keys_values, there, got, own, *blocks, *after, table)


def project_kernel(count, groups, add, info, *refs):
    out = refs[-1]
    acts, weights = refs[:count], refs[count:count + groups]
    act = jnp.concatenate([a[...].reshape(-1, a.shape[2]) for a in acts], 1)
    weight = jnp.concatenate([w[...] for w in weights], 0)
    total = jnp.dot(act, weight, preferred_element_type=jnp.float32)
    if add:
        total = total + refs[count + groups][...].reshape(total.shape)
    out[...] = total.astype(out.dtype).reshape(out.shape)


def project(info, pieces, weights, features, dtype, before=None):
    tokens = pieces[0][2].shape[1]
    tile = min(512 if before is None else 256, features)
    steps = features // tile
    half = weights[0].shape[0] // 2
    used, specs = [], []
    for group, first, act in pieces:
        wide = act.shape[2] if first * HD % act.shape[2] == 0 else HD
        per = half // wide
        for at in range(first * HD // wide, (first * HD + act.shape[2]) // wide):
            used.append(weights[group])
            if group == 0:
                row = lambda s, info, at=at, per=per: (info[0] * per + at, info[2] * steps + s)
            elif group == 1:
                row = lambda s, info, at=at, per=per: (
                    (1 - info[0]) * per + at, info[2] * steps + s)
            else:
                row = lambda s, info, at=at: (at, s)
            specs.append(pl.BlockSpec((wide, tile), row))
    flat = [act for _, _, act in pieces]
    spec = pl.BlockSpec((2, tokens, tile), lambda s, info: (0, 0, s))
    specs = [pl.BlockSpec(a.shape, lambda s, info: (0, 0, 0)) for a in flat] + specs
    operands = flat + used
    if before is not None:
        specs.append(spec)
        operands.append(before)
    depth = sum(a.shape[2] for a in flat)
    return pl.pallas_call(
        lambda *refs: project_kernel(len(flat), len(used), before is not None, *refs),
        grid_spec=pltpu.PrefetchScalarGridSpec(
            num_scalar_prefetch=1, grid=(steps,), in_specs=specs, out_specs=spec
        ),
        out_shape=jax.ShapeDtypeStruct((2, tokens, features), dtype),
        compiler_params=pltpu.CompilerParams(vmem_limit_bytes=40 * 1024 * 1024),
        cost_estimate=pl.CostEstimate(
            flops=2 * 2 * tokens * depth * features // 8,
            bytes_accessed=2 * depth * features // 8,
            transcendentals=0,
        ),
    )(info, *operands)


def on_device(queries, keys_values, block_mask, out_weight):
    tokens = queries.shape[1]
    n, f = lax.axis_size("ctx"), lax.axis_size("fsdp")
    index, place = lax.axis_index("ctx"), lax.axis_index("fsdp")
    core, side = index % 2, (index // 2) % 2
    info = jnp.stack([core, side, place]).astype(jnp.int32)
    width = queries.shape[2] // 2
    heads_half = width // HD
    rows = tokens // BLK
    features = out_weight.shape[1] // f
    bf16 = jnp.bfloat16
    parts = [[0,1],[2,3]] if heads_half == 4 else [[h] for h in range(heads_half)]

    pair = lambda i: i ^ 1
    ahead = lambda i: i + 4 if i + 4 < n else None
    across = lambda i: i ^ 2
    upper = lambda i: i + 2 if i & 2 == 0 else None
    lower = lambda i: i - 2 if i & 2 else None
    lanes = lambda start, size: pl.ds(pl.multiple_of(start, HD), size)

    got = moved(keys_values, n, pair, "pair_kv")
    there = moved(queries, n, pair, "pair_q")

    def cut_panels(core, place, ins, outs):
        pieces = []
        for r in range(1, f):
            column = pl.multiple_of(lax.rem(place + r, f) * features, HD)
            for p in range(cuts):
                row = pl.multiple_of(core * width + p * (width // cuts), width // cuts)
                at = pl.ds(p * (width // cuts), width // cuts)
                pieces.append((ins[0].at[pl.ds(row, width // cuts), pl.ds(column, features)],
                               [(slice(None), outs[r - 1].at[at])]))
        return pieces

    cuts = 4 if f == 2 else 1
    panels = copies(
        info, [out_weight], [jax.ShapeDtypeStruct((width, features), bf16)] * (f - 1),
        [(width // cuts, features)] * (cuts * (f - 1)), cut_panels, VMEM,
    )

    def join(core, ins, outs):
        pieces = []
        for slot, source in enumerate(ins[:2]):
            for head_at, target in outs:
                heads = target.shape[0]
                here = lanes(core * width + head_at * HD, heads * HD)
                pieces.append((source.at[:, 0, :, here], [
                    ((slice(None), slice(None), slice(h * HD, (h + 1) * HD)), target.at[h, slot])
                    for h in range(heads)
                ]))
        return pieces

    pair_shape = lambda heads: jax.ShapeDtypeStruct((heads, 2, 2, tokens, HD), bf16)
    held = lambda heads: (2, tokens, heads * HD)
    first, = copies(
        info, [keys_values, got, *panels], [pair_shape(len(parts[0]))], [held(len(parts[0]))] * 2,
        lambda core, place, ins, outs: join(core, ins, [(0, outs[0])]),
    )
    rest = []
    if len(parts) > 1:
        sizes = [len(part) for part in parts[1:]]
        rest = copies(
            info, [keys_values, got, first], [pair_shape(size) for size in sizes],
            [held(size) for size in sizes] * 2,
            lambda core, place, ins, outs: join(
                core, ins, [(p[0], out) for p, out in zip(parts[1:], outs)]),
        )
    own = [first] + list(rest)

    sames = [
        moved_both(panel, n, f, lambda i, k: (i, (k + r) % f), "panel")
        for r, panel in enumerate(panels, 1)
    ]


    blocks = []
    for k, mine in enumerate(own):
        one = moved(mine, n, ahead, f"near{k}")
        swap = moved(one, n, across, f"nearx{k}")
        two = moved(one, n, ahead, f"far{k}")
        two, = gated([two], swap, *[block[3] for block in blocks])
        extra = moved(jnp.where(side == 0, mine, two), n, across, f"extra{k}")
        blocks.append((one, two, swap, extra))

    mask_there = moved(block_mask, n, pair, "pair_mask")
    table = jnp.stack([
        mask_table(index * rows, rows, block_mask),
        mask_table((index ^ 1) * rows, rows, mask_there),
    ])

    acts = [[] for _ in range(2 * f)]
    ties = []
    for k, part in enumerate(parts):
        after = []
        mine, give, tie = attend(
            info, queries, keys_values, there, got, own[k], blocks[k], table,
            part, heads_half, after + ties[-1:],
        )
        ties.append(tie)
        acts[0].append(mine)
        for r in range(1, f):
            acts[2 * r].append(moved_both(mine, n, f, lambda i, k: (i, (k + r) % f), f"same{k}"))
            acts[2 * r + 1].append(moved_both(give, n, f, lambda i, k: (i ^ 1, (k + r) % f), f"cross{k}"))
        acts[1].append(moved(give, n, pair, f"pair{k}"))
    others = []
    for same in sames:
        same, = gated([same], blocks[-1][3], ties[0])
        others += [same, moved(same, n, pair, "panel_pair")]

    weights = [out_weight, out_weight] + others
    stages = [[], [], []]
    for g in range(2 * f):
        for k, (part, act) in enumerate(zip(parts, acts[g])):
            late = k == len(parts) - 1 and g > 0
            stages[(1 if g % 2 else 2) if late else 0].append((g, part[0], act))
    total = None
    stages = [stage for stage in stages if stage]
    for k, stage in enumerate(stages):
        dtype = jnp.bfloat16 if k == len(stages) - 1 else jnp.float32
        total = project(info, stage, weights, features, dtype, total)
    return total


def solution(mesh):
    in_specs = (
        P(None, "ctx", "fsdp"),
        P(None, None, "ctx", "fsdp"),
        P("ctx", None),
        P("fsdp", None),
    )
    out_specs = P(None, "ctx", "fsdp")
    return jax.shard_map(
        on_device, mesh=mesh, in_specs=in_specs, out_specs=out_specs, check_vma=False
    )
```

```python
import math

import jax
import jax.numpy as jnp
from jax import lax
from jax.experimental import pallas as pl
from jax.experimental.pallas import tpu as pltpu
from jax.sharding import PartitionSpec as P

HD = 128
BLK = 64
WINB = 32
MASKED = -1e30
SCALE = 1.0 / math.sqrt(HD)
VMEM = 60 * 1024 * 1024


def moved(array, n, go, name):
    pairs = [(i, go(i)) for i in range(n) if go(i) is not None]
    with jax.named_scope(name):
        return lax.ppermute(array, "ctx", pairs)


def moved_both(array, n, f, go, name):
    pairs = [(i * f + k, go(i, k)[0] * f + go(i, k)[1]) for i in range(n) for k in range(f)]
    with jax.named_scope(name):
        return lax.ppermute(array, ("ctx", "fsdp"), pairs)


def behind(array, *others):
    return lax.optimization_barrier((array,) + others)[0] if others else array


def gated(arrays, *ties):
    ties = [t[(0,) * (t.ndim - 2)][:8] for t in ties]
    some = pl.BlockSpec(memory_space=pl.ANY)
    return pl.pallas_call(
        lambda *refs: None,
        in_specs=[some] * (len(arrays) + len(ties)),
        out_specs=[some] * len(arrays),
        out_shape=[jax.ShapeDtypeStruct(a.shape, a.dtype) for a in arrays],
        input_output_aliases={k: k for k in range(len(arrays))},
        compiler_params=pltpu.CompilerParams(vmem_limit_bytes=1024 * 1024),
        cost_estimate=pl.CostEstimate(flops=0, bytes_accessed=0, transcendentals=0),
    )(*arrays, *ties)


def mask_table(first_block, rows, mask_rows):
    count = WINB + rows
    query = jnp.arange(rows)
    gap = WINB + query[None, :] - jnp.arange(count)[:, None]
    present = (first_block - WINB + jnp.arange(count) >= 0)[:, None]
    clean = (gap >= 0) & (gap < WINB) & present
    offsets = jnp.arange(WINB)
    picked = ((gap - 1)[:, :, None] == offsets[None, None, :]) & (mask_rows[None] == 1)
    noisy = jnp.any(picked, axis=2) & present
    own_clean = jnp.zeros((rows, rows), bool)
    own_noisy = jnp.eye(rows, dtype=bool)
    allowed = jnp.concatenate(
        [jnp.concatenate([clean, noisy], 1), jnp.concatenate([own_clean, own_noisy], 1)], 0
    )
    table = jnp.where(allowed, 0.0, MASKED).astype(jnp.float32)
    return jnp.repeat(table.reshape(-1, rows, 2 * rows).transpose(0, 2, 1), BLK, axis=2)


def copies(info, sources, outs, shapes, plan, limit=8 * 1024 * 1024):
    total = sum(math.prod(o.shape) for o in outs)

    def kernel(info, *refs):
        ins, rest = refs[:len(sources)], refs[len(sources):]
        pieces = plan(info[0], info[2], ins, rest[:len(outs)])
        room, arrive, leave = rest[len(outs):-2], rest[-2], rest[-1]
        reads = [
            pltpu.make_async_copy(source, held, arrive.at[k])
            for k, ((source, _), held) in enumerate(zip(pieces, room))
        ]
        for read in reads:
            read.start()
        writes = []
        for read, (_, targets), held in zip(reads, pieces, room):
            read.wait()
            for part, target in targets:
                write = pltpu.make_async_copy(held.at[part], target, leave.at[len(writes)])
                write.start()
                writes.append(write)
        for write in writes:
            write.wait()

    return pl.pallas_call(
        kernel,
        grid_spec=pltpu.PrefetchScalarGridSpec(
            num_scalar_prefetch=1,
            grid=(),
            in_specs=[pl.BlockSpec(memory_space=pl.ANY)] * len(sources),
            out_specs=[pl.BlockSpec(memory_space=pl.ANY)] * len(outs),
            scratch_shapes=[
                *[pltpu.VMEM(shape, jnp.bfloat16) for shape in shapes],
                pltpu.SemaphoreType.DMA((len(shapes),)),
                pltpu.SemaphoreType.DMA((32,)),
            ],
        ),
        out_shape=[jax.ShapeDtypeStruct(o.shape, o.dtype) for o in outs],
        compiler_params=pltpu.CompilerParams(vmem_limit_bytes=limit),
        cost_estimate=pl.CostEstimate(flops=0, bytes_accessed=total, transcendentals=0),
    )(info, *sources)


def attend_kernel(tokens, info, *refs):
    core, side = info[0], info[1]
    views, (own, one, two, swap, extra), refs = refs[:4], refs[4:9], refs[-7:]
    table, mine, give, tie, keys, values, least = refs
    tie[...] = jnp.zeros_like(tie)
    rows = tokens // BLK
    slots = WINB * BLK // tokens + 2
    back = WINB * BLK // (2 * tokens)

    def place(ref, pair):
        for slot in range(2):
            half = core if slot == 0 else 1 - core
            keys[pair * 2 + half] = ref[0, slot, 0].T
            values[pair * 2 + half] = ref[0, slot, 1]

    place(two, 0)
    place(one, 2)
    place(swap, jnp.where(side == 0, 3, 1))
    place(own, back)

    place(extra, jnp.where(side == 0, 1, 3))
    for tile in range(2):
        keys[slots + tile] = views[2 * tile + 1][0, 0].T

    def operands(tile, k):
        half = core if tile == 0 else 1 - core
        if k == slots - 1:
            return keys[slots + tile], views[2 * tile + 1][1, 0]
        return keys[half + k], values[half + k]

    def store(tile, out):
        (mine if tile == 0 else give)[...] = out.astype(jnp.bfloat16).reshape(2, tokens, HD)

    ones = jnp.ones((16, HD), jnp.bfloat16)
    longest = None
    for k in range(slots + 2):
        key = keys[k]
        size = jnp.dot(ones, key * key, preferred_element_type=jnp.float32)
        longest = size if longest is None else jnp.maximum(longest, size)
    longest = jnp.max(longest, axis=1, keepdims=True)[0:1] * 1.03
    queries, shifts = [], []
    for tile in range(2):
        query = views[2 * tile][...].reshape(2 * tokens, HD)
        size = jnp.dot(query * query, jnp.ones((HD, HD), jnp.bfloat16),
                       preferred_element_type=jnp.float32)
        queries.append(query)
        shifts.append((jnp.sqrt(size * longest) * SCALE)[:, 0:1])

    steps = [(tile, k) for tile in range(2) for k in range(0, slots, 2)]
    totals, sums = [None, None], [None, None]

    def scores_of(tile, k):
        key = jnp.concatenate([operands(tile, j)[0] for j in range(k, min(k + 2, slots))], 1)
        scores = jnp.dot(queries[tile], key, preferred_element_type=jnp.float32)
        bias = jnp.concatenate([table[tile, j] for j in range(k, min(k + 2, slots))], 1)
        return scores, bias

    def weights_of(tile, scores, bias, shift):
        wide = scores.shape[1]
        shifted = scores * SCALE - shift
        shifted = shifted.reshape(2 * rows, BLK, wide) + bias[:, None, :]
        return jnp.exp(shifted.reshape(2 * tokens, wide))

    def add(tile, k, expo):
        value = jnp.concatenate([operands(tile, j)[1] for j in range(k, min(k + 2, slots))], 0)
        part = jnp.dot(expo, value, preferred_element_type=jnp.float32)
        totals[tile] = part if totals[tile] is None else totals[tile] + part

    scores, last = scores_of(*steps[0]), None
    for at, step in enumerate(steps):
        upcoming = scores_of(*steps[at + 1]) if at + 1 < len(steps) else None
        if last is not None:
            add(*last)
        tile = step[0]
        expo = weights_of(tile, *scores, shifts[tile])
        for lanes in range(0, expo.shape[1], HD):
            part = expo[:, lanes:lanes + HD]
            sums[tile] = part if sums[tile] is None else sums[tile] + part
        last = (*step, expo.astype(jnp.bfloat16))
        scores = upcoming
    add(*last)
    low_sum = None
    for tile, total in enumerate(totals):
        whole = jnp.sum(sums[tile], axis=1, keepdims=True)
        store(tile, total / whole)
        smallest = jnp.min(whole, axis=0, keepdims=True)
        low_sum = smallest if low_sum is None else jnp.minimum(low_sum, smallest)
    least[...] = jnp.broadcast_to(low_sum, least.shape)

    @pl.when(jnp.logical_not(jnp.min(least[...]) > 2.0 ** -40))
    def _():
        for tile in range(2):
            runs = [scores_of(tile, k) for k in range(0, slots, 2)]
            scores = jnp.concatenate([score for score, _ in runs], 1) * SCALE
            bias = jnp.concatenate([bias for _, bias in runs], 1)
            wide = scores.shape[1]
            scores = (scores.reshape(2 * rows, BLK, wide) + bias[:, None, :]).reshape(
                2 * tokens, wide)
            expo = jnp.exp(scores - jnp.max(scores, axis=1, keepdims=True))
            value = jnp.concatenate([operands(tile, k)[1] for k in range(slots)], 0)
            total = jnp.dot(expo.astype(jnp.bfloat16), value, preferred_element_type=jnp.float32)
            store(tile, total / jnp.sum(expo, axis=1, keepdims=True))


def attend(info, queries, keys_values, there, got, own, blocks, table, part, heads_half, after):
    tokens = queries.shape[1]
    slots = WINB * BLK // tokens + 2
    count, first = len(part), part[0]
    here = lambda h, info: (0, 0, info[0] * heads_half + first + h)
    noisy = lambda h, info: (0, 1, 0, info[0] * heads_half + first + h)
    query_spec = pl.BlockSpec((2, tokens, HD), here)
    noisy_spec = pl.BlockSpec((2, 1, tokens, HD), noisy)
    chunk = pl.BlockSpec((1, 2, 2, tokens, HD), lambda h, info: (h, 0, 0, 0, 0))
    out_spec = pl.BlockSpec((2, tokens, HD), lambda h, info: (0, 0, h))
    out = jax.ShapeDtypeStruct((2, tokens, count * HD), jnp.bfloat16)
    work = count * 2 * 2 * tokens * slots * tokens
    return pl.pallas_call(
        lambda *refs: attend_kernel(tokens, *refs),
        grid_spec=pltpu.PrefetchScalarGridSpec(
            num_scalar_prefetch=1,
            grid=(count,),
            in_specs=[
                query_spec, noisy_spec, query_spec, noisy_spec, *[chunk] * 5,
                *[pl.BlockSpec(memory_space=pl.ANY)] * len(after),
                pl.BlockSpec(table.shape, lambda h, info: (0, 0, 0, 0)),
            ],
            out_specs=[out_spec, out_spec, pl.BlockSpec((8, HD), lambda h, info: (0, 0))],
            scratch_shapes=[
                pltpu.VMEM((slots + 2, HD, tokens), jnp.bfloat16),
                pltpu.VMEM((slots, tokens, HD), jnp.bfloat16),
                pltpu.VMEM((8, HD), jnp.float32),
            ],
        ),
        out_shape=[out, out, jax.ShapeDtypeStruct((8, HD), jnp.float32)],
        compiler_params=pltpu.CompilerParams(vmem_limit_bytes=24 * 1024 * 1024),
        cost_estimate=pl.CostEstimate(
            flops=work * 8, bytes_accessed=count * 64 * 1024, transcendentals=0
        ),
    )(info, queries, keys_values, there, got, own, *blocks, *after, table)


def project_kernel(count, groups, add, info, *refs):
    out = refs[-1]
    acts, weights = refs[:count], refs[count:count + groups]
    act = jnp.concatenate([a[...].reshape(-1, a.shape[2]) for a in acts], 1)
    weight = jnp.concatenate([w[...] for w in weights], 0)
    total = jnp.dot(act, weight, preferred_element_type=jnp.float32)
    if add:
        total = total + refs[count + groups][...].reshape(total.shape)
    out[...] = total.astype(out.dtype).reshape(out.shape)


def project(info, pieces, weights, features, dtype, before=None):
    tokens = pieces[0][2].shape[1]
    tile = min(512 if before is None else 1024, features)
    steps = features // tile
    half = weights[0].shape[0] // 2
    used, specs = [], []
    for group, first, act in pieces:
        wide = act.shape[2] if first * HD % act.shape[2] == 0 else HD
        per = half // wide
        for at in range(first * HD // wide, (first * HD + act.shape[2]) // wide):
            used.append(weights[group])
            if group == 0:
                row = lambda s, info, at=at, per=per: (info[0] * per + at, info[2] * steps + s)
            elif group == 1:
                row = lambda s, info, at=at, per=per: (
                    (1 - info[0]) * per + at, info[2] * steps + s)
            else:
                row = lambda s, info, at=at: (at, s)
            specs.append(pl.BlockSpec((wide, tile), row))
    flat = [act for _, _, act in pieces]
    spec = pl.BlockSpec((2, tokens, tile), lambda s, info: (0, 0, s))
    specs = [pl.BlockSpec(a.shape, lambda s, info: (0, 0, 0)) for a in flat] + specs
    operands = flat + used
    if before is not None:
        specs.append(spec)
        operands.append(before)
    depth = sum(a.shape[2] for a in flat)
    return pl.pallas_call(
        lambda *refs: project_kernel(len(flat), len(used), before is not None, *refs),
        grid_spec=pltpu.PrefetchScalarGridSpec(
            num_scalar_prefetch=1, grid=(steps,), in_specs=specs, out_specs=spec
        ),
        out_shape=jax.ShapeDtypeStruct((2, tokens, features), dtype),
        compiler_params=pltpu.CompilerParams(vmem_limit_bytes=40 * 1024 * 1024),
        cost_estimate=pl.CostEstimate(
            flops=2 * 2 * tokens * depth * features // 8,
            bytes_accessed=2 * depth * features // 8,
            transcendentals=0,
        ),
    )(info, *operands)


def on_device(queries, keys_values, block_mask, out_weight):
    tokens = queries.shape[1]
    n, f = lax.axis_size("ctx"), lax.axis_size("fsdp")
    index, place = lax.axis_index("ctx"), lax.axis_index("fsdp")
    core, side = index % 2, (index // 2) % 2
    info = jnp.stack([core, side, place]).astype(jnp.int32)
    width = queries.shape[2] // 2
    heads_half = width // HD
    rows = tokens // BLK
    features = out_weight.shape[1] // f
    bf16 = jnp.bfloat16
    parts = [[0,1],[2,3]] if heads_half == 4 else [[h] for h in range(heads_half)]

    pair = lambda i: i ^ 1
    ahead = lambda i: i + 4 if i + 4 < n else None
    across = lambda i: i ^ 2
    upper = lambda i: i + 2 if i & 2 == 0 else None
    lower = lambda i: i - 2 if i & 2 else None
    lanes = lambda start, size: pl.ds(pl.multiple_of(start, HD), size)

    got = moved(keys_values, n, pair, "pair_kv")
    there = moved(queries, n, pair, "pair_q")

    def cut_panels(core, place, ins, outs):
        pieces = []
        for r in range(1, f):
            column = pl.multiple_of(lax.rem(place + r, f) * features, HD)
            for p in range(cuts):
                row = pl.multiple_of(core * width + p * (width // cuts), width // cuts)
                at = pl.ds(p * (width // cuts), width // cuts)
                pieces.append((ins[0].at[pl.ds(row, width // cuts), pl.ds(column, features)],
                               [(slice(None), outs[r - 1].at[at])]))
        return pieces

    cuts = 4 if f == 2 else 1
    panels = copies(
        info, [out_weight], [jax.ShapeDtypeStruct((width, features), bf16)] * (f - 1),
        [(width // cuts, features)] * (cuts * (f - 1)), cut_panels, VMEM,
    )

    def join(core, ins, outs):
        pieces = []
        for slot, source in enumerate(ins[:2]):
            for head_at, target in outs:
                heads = target.shape[0]
                here = lanes(core * width + head_at * HD, heads * HD)
                pieces.append((source.at[:, 0, :, here], [
                    ((slice(None), slice(None), slice(h * HD, (h + 1) * HD)), target.at[h, slot])
                    for h in range(heads)
                ]))
        return pieces

    pair_shape = lambda heads: jax.ShapeDtypeStruct((heads, 2, 2, tokens, HD), bf16)
    held = lambda heads: (2, tokens, heads * HD)
    first, = copies(
        info, [keys_values, got, *panels], [pair_shape(len(parts[0]))], [held(len(parts[0]))] * 2,
        lambda core, place, ins, outs: join(core, ins, [(0, outs[0])]),
    )
    rest = []
    if len(parts) > 1:
        sizes = [len(part) for part in parts[1:]]
        rest = copies(
            info, [keys_values, got, first], [pair_shape(size) for size in sizes],
            [held(size) for size in sizes] * 2,
            lambda core, place, ins, outs: join(
                core, ins, [(p[0], out) for p, out in zip(parts[1:], outs)]),
        )
    own = [first] + list(rest)

    sames = [
        moved_both(panel, n, f, lambda i, k: (i, (k + r) % f), "panel")
        for r, panel in enumerate(panels, 1)
    ]


    blocks = []
    for k, mine in enumerate(own):
        one = moved(mine, n, ahead, f"near{k}")
        swap = moved(one, n, across, f"nearx{k}")
        two = moved(one, n, ahead, f"far{k}")
        two, = gated([two], swap, *[block[3] for block in blocks])
        extra = moved(jnp.where(side == 0, mine, two), n, across, f"extra{k}")
        blocks.append((one, two, swap, extra))

    mask_there = moved(block_mask, n, pair, "pair_mask")
    table = jnp.stack([
        mask_table(index * rows, rows, block_mask),
        mask_table((index ^ 1) * rows, rows, mask_there),
    ])

    acts = [[] for _ in range(2 * f)]
    ties = []
    for k, part in enumerate(parts):
        after = []
        mine, give, tie = attend(
            info, queries, keys_values, there, got, own[k], blocks[k], table,
            part, heads_half, after + ties[-1:],
        )
        ties.append(tie)
        acts[0].append(mine)
        for r in range(1, f):
            acts[2 * r].append(moved_both(mine, n, f, lambda i, k: (i, (k + r) % f), f"same{k}"))
            acts[2 * r + 1].append(moved_both(give, n, f, lambda i, k: (i ^ 1, (k + r) % f), f"cross{k}"))
        acts[1].append(moved(give, n, pair, f"pair{k}"))
    others = []
    for same in sames:
        same, = gated([same], blocks[-1][3], ties[0])
        others += [same, moved(same, n, pair, "panel_pair")]

    weights = [out_weight, out_weight] + others
    stages = [[], [], []]
    for g in range(2 * f):
        for k, (part, act) in enumerate(zip(parts, acts[g])):
            late = k == len(parts) - 1 and g > 0
            stages[(1 if g % 2 else 2) if late else 0].append((g, part[0], act))
    total = None
    stages = [stage for stage in stages if stage]
    for k, stage in enumerate(stages):
        dtype = jnp.bfloat16 if k == len(stages) - 1 else jnp.float32
        total = project(info, stage, weights, features, dtype, total)
    return total


def solution(mesh):
    in_specs = (
        P(None, "ctx", "fsdp"),
        P(None, None, "ctx", "fsdp"),
        P("ctx", None),
        P("fsdp", None),
    )
    out_specs = P(None, "ctx", "fsdp")
    return jax.shard_map(
        on_device, mesh=mesh, in_specs=in_specs, out_specs=out_specs, check_vma=False
    )
```

```python
import math

import jax
import jax.numpy as jnp
from jax import lax
from jax.experimental import pallas as pl
from jax.experimental.pallas import tpu as pltpu
from jax.sharding import PartitionSpec as P

HD = 128
BLK = 64
WINB = 32
MASKED = -1e30
SCALE = 1.0 / math.sqrt(HD)
VMEM = 60 * 1024 * 1024


def moved(array, n, go, name):
    pairs = [(i, go(i)) for i in range(n) if go(i) is not None]
    with jax.named_scope(name):
        return lax.ppermute(array, "ctx", pairs)


def moved_both(array, n, f, go, name):
    pairs = [(i * f + k, go(i, k)[0] * f + go(i, k)[1]) for i in range(n) for k in range(f)]
    with jax.named_scope(name):
        return lax.ppermute(array, ("ctx", "fsdp"), pairs)


def behind(array, *others):
    return lax.optimization_barrier((array,) + others)[0] if others else array


def gated(arrays, *ties):
    ties = [t[(0,) * (t.ndim - 2)][:8] for t in ties]
    some = pl.BlockSpec(memory_space=pl.ANY)
    return pl.pallas_call(
        lambda *refs: None,
        in_specs=[some] * (len(arrays) + len(ties)),
        out_specs=[some] * len(arrays),
        out_shape=[jax.ShapeDtypeStruct(a.shape, a.dtype) for a in arrays],
        input_output_aliases={k: k for k in range(len(arrays))},
        compiler_params=pltpu.CompilerParams(vmem_limit_bytes=1024 * 1024),
        cost_estimate=pl.CostEstimate(flops=0, bytes_accessed=0, transcendentals=0),
    )(*arrays, *ties)


def mask_table(first_block, rows, mask_rows):
    count = WINB + rows
    query = jnp.arange(rows)
    gap = WINB + query[None, :] - jnp.arange(count)[:, None]
    present = (first_block - WINB + jnp.arange(count) >= 0)[:, None]
    clean = (gap >= 0) & (gap < WINB) & present
    offsets = jnp.arange(WINB)
    picked = ((gap - 1)[:, :, None] == offsets[None, None, :]) & (mask_rows[None] == 1)
    noisy = jnp.any(picked, axis=2) & present
    own_clean = jnp.zeros((rows, rows), bool)
    own_noisy = jnp.eye(rows, dtype=bool)
    allowed = jnp.concatenate(
        [jnp.concatenate([clean, noisy], 1), jnp.concatenate([own_clean, own_noisy], 1)], 0
    )
    table = jnp.where(allowed, 0.0, MASKED).astype(jnp.float32)
    return jnp.repeat(table.reshape(-1, rows, 2 * rows).transpose(0, 2, 1), BLK, axis=2)


def copies(info, sources, outs, shapes, plan, limit=8 * 1024 * 1024):
    total = sum(math.prod(o.shape) for o in outs)

    def kernel(info, *refs):
        ins, rest = refs[:len(sources)], refs[len(sources):]
        pieces = plan(info[0], info[2], ins, rest[:len(outs)])
        room, arrive, leave = rest[len(outs):-2], rest[-2], rest[-1]
        reads = [
            pltpu.make_async_copy(source, held, arrive.at[k])
            for k, ((source, _), held) in enumerate(zip(pieces, room))
        ]
        for read in reads:
            read.start()
        writes = []
        for read, (_, targets), held in zip(reads, pieces, room):
            read.wait()
            for part, target in targets:
                write = pltpu.make_async_copy(held.at[part], target, leave.at[len(writes)])
                write.start()
                writes.append(write)
        for write in writes:
            write.wait()

    return pl.pallas_call(
        kernel,
        grid_spec=pltpu.PrefetchScalarGridSpec(
            num_scalar_prefetch=1,
            grid=(),
            in_specs=[pl.BlockSpec(memory_space=pl.ANY)] * len(sources),
            out_specs=[pl.BlockSpec(memory_space=pl.ANY)] * len(outs),
            scratch_shapes=[
                *[pltpu.VMEM(shape, jnp.bfloat16) for shape in shapes],
                pltpu.SemaphoreType.DMA((len(shapes),)),
                pltpu.SemaphoreType.DMA((32,)),
            ],
        ),
        out_shape=[jax.ShapeDtypeStruct(o.shape, o.dtype) for o in outs],
        compiler_params=pltpu.CompilerParams(vmem_limit_bytes=limit),
        cost_estimate=pl.CostEstimate(flops=0, bytes_accessed=total, transcendentals=0),
    )(info, *sources)


def attend_kernel(tokens, info, *refs):
    core, side = info[0], info[1]
    views, (own, one, two, swap, extra), refs = refs[:4], refs[4:9], refs[-7:]
    table, mine, give, tie, keys, values, least = refs
    tie[...] = jnp.zeros_like(tie)
    rows = tokens // BLK
    slots = WINB * BLK // tokens + 2
    back = WINB * BLK // (2 * tokens)

    def place(ref, pair):
        for slot in range(2):
            half = core if slot == 0 else 1 - core
            keys[pair * 2 + half] = ref[0, slot, 0].T
            values[pair * 2 + half] = ref[0, slot, 1]

    place(two, 0)
    place(one, 2)
    place(swap, jnp.where(side == 0, 3, 1))
    place(own, back)

    place(extra, jnp.where(side == 0, 1, 3))
    for tile in range(2):
        keys[slots + tile] = views[2 * tile + 1][0, 0].T

    def operands(tile, k):
        half = core if tile == 0 else 1 - core
        if k == slots - 1:
            return keys[slots + tile], views[2 * tile + 1][1, 0]
        return keys[half + k], values[half + k]

    def store(tile, out):
        (mine if tile == 0 else give)[...] = out.astype(jnp.bfloat16).reshape(2, tokens, HD)

    ones = jnp.ones((16, HD), jnp.bfloat16)
    longest = None
    for k in range(slots + 2):
        key = keys[k]
        size = jnp.dot(ones, key * key, preferred_element_type=jnp.float32)
        longest = size if longest is None else jnp.maximum(longest, size)
    longest = jnp.max(longest, axis=1, keepdims=True)[0:1] * 1.03
    queries, shifts = [], []
    for tile in range(2):
        query = views[2 * tile][...].reshape(2 * tokens, HD)
        size = jnp.dot(query * query, jnp.ones((HD, HD), jnp.bfloat16),
                       preferred_element_type=jnp.float32)
        queries.append(query)
        shifts.append((jnp.sqrt(size * longest) * SCALE)[:, 0:1])

    steps = [(tile, k) for tile in range(2) for k in range(0, slots, 2)]
    totals, sums = [None, None], [None, None]

    def scores_of(tile, k):
        key = jnp.concatenate([operands(tile, j)[0] for j in range(k, min(k + 2, slots))], 1)
        scores = jnp.dot(queries[tile], key, preferred_element_type=jnp.float32)
        bias = jnp.concatenate([table[tile, j] for j in range(k, min(k + 2, slots))], 1)
        return scores, bias

    def weights_of(tile, scores, bias, shift):
        wide = scores.shape[1]
        shifted = scores * SCALE - shift
        shifted = shifted.reshape(2 * rows, BLK, wide) + bias[:, None, :]
        return jnp.exp(shifted.reshape(2 * tokens, wide))

    def add(tile, k, expo):
        value = jnp.concatenate([operands(tile, j)[1] for j in range(k, min(k + 2, slots))], 0)
        part = jnp.dot(expo, value, preferred_element_type=jnp.float32)
        totals[tile] = part if totals[tile] is None else totals[tile] + part

    scores, last = scores_of(*steps[0]), None
    for at, step in enumerate(steps):
        upcoming = scores_of(*steps[at + 1]) if at + 1 < len(steps) else None
        if last is not None:
            add(*last)
        tile = step[0]
        expo = weights_of(tile, *scores, shifts[tile])
        for lanes in range(0, expo.shape[1], HD):
            part = expo[:, lanes:lanes + HD]
            sums[tile] = part if sums[tile] is None else sums[tile] + part
        last = (*step, expo.astype(jnp.bfloat16))
        scores = upcoming
    add(*last)
    low_sum = None
    for tile, total in enumerate(totals):
        whole = jnp.sum(sums[tile], axis=1, keepdims=True)
        store(tile, total / whole)
        smallest = jnp.min(whole, axis=0, keepdims=True)
        low_sum = smallest if low_sum is None else jnp.minimum(low_sum, smallest)
    least[...] = jnp.broadcast_to(low_sum, least.shape)

    @pl.when(jnp.logical_not(jnp.min(least[...]) > 2.0 ** -40))
    def _():
        for tile in range(2):
            runs = [scores_of(tile, k) for k in range(0, slots, 2)]
            scores = jnp.concatenate([score for score, _ in runs], 1) * SCALE
            bias = jnp.concatenate([bias for _, bias in runs], 1)
            wide = scores.shape[1]
            scores = (scores.reshape(2 * rows, BLK, wide) + bias[:, None, :]).reshape(
                2 * tokens, wide)
            expo = jnp.exp(scores - jnp.max(scores, axis=1, keepdims=True))
            value = jnp.concatenate([operands(tile, k)[1] for k in range(slots)], 0)
            total = jnp.dot(expo.astype(jnp.bfloat16), value, preferred_element_type=jnp.float32)
            store(tile, total / jnp.sum(expo, axis=1, keepdims=True))


def attend(info, queries, keys_values, there, got, own, blocks, table, part, heads_half, after):
    tokens = queries.shape[1]
    slots = WINB * BLK // tokens + 2
    count, first = len(part), part[0]
    here = lambda h, info: (0, 0, info[0] * heads_half + first + h)
    noisy = lambda h, info: (0, 1, 0, info[0] * heads_half + first + h)
    query_spec = pl.BlockSpec((2, tokens, HD), here)
    noisy_spec = pl.BlockSpec((2, 1, tokens, HD), noisy)
    chunk = pl.BlockSpec((1, 2, 2, tokens, HD), lambda h, info: (h, 0, 0, 0, 0))
    out_spec = pl.BlockSpec((2, tokens, HD), lambda h, info: (0, 0, h))
    out = jax.ShapeDtypeStruct((2, tokens, count * HD), jnp.bfloat16)
    work = count * 2 * 2 * tokens * slots * tokens
    return pl.pallas_call(
        lambda *refs: attend_kernel(tokens, *refs),
        grid_spec=pltpu.PrefetchScalarGridSpec(
            num_scalar_prefetch=1,
            grid=(count,),
            in_specs=[
                query_spec, noisy_spec, query_spec, noisy_spec, *[chunk] * 5,
                *[pl.BlockSpec(memory_space=pl.ANY)] * len(after),
                pl.BlockSpec(table.shape, lambda h, info: (0, 0, 0, 0)),
            ],
            out_specs=[out_spec, out_spec, pl.BlockSpec((8, HD), lambda h, info: (0, 0))],
            scratch_shapes=[
                pltpu.VMEM((slots + 2, HD, tokens), jnp.bfloat16),
                pltpu.VMEM((slots, tokens, HD), jnp.bfloat16),
                pltpu.VMEM((8, HD), jnp.float32),
            ],
        ),
        out_shape=[out, out, jax.ShapeDtypeStruct((8, HD), jnp.float32)],
        compiler_params=pltpu.CompilerParams(vmem_limit_bytes=20 * 1024 * 1024),
        cost_estimate=pl.CostEstimate(
            flops=work * 8, bytes_accessed=count * 64 * 1024, transcendentals=0
        ),
    )(info, queries, keys_values, there, got, own, *blocks, *after, table)


def project_kernel(count, groups, add, info, *refs):
    out = refs[-1]
    acts, weights = refs[:count], refs[count:count + groups]
    act = jnp.concatenate([a[...].reshape(-1, a.shape[2]) for a in acts], 1)
    weight = jnp.concatenate([w[...] for w in weights], 0)
    total = jnp.dot(act, weight, preferred_element_type=jnp.float32)
    if add:
        total = total + refs[count + groups][...].reshape(total.shape)
    out[...] = total.astype(out.dtype).reshape(out.shape)


def project(info, pieces, weights, features, dtype, before=None):
    tokens = pieces[0][2].shape[1]
    tile = min(512 if before is None else 1024, features)
    steps = features // tile
    half = weights[0].shape[0] // 2
    used, specs = [], []
    for group, first, act in pieces:
        wide = act.shape[2] if first * HD % act.shape[2] == 0 else HD
        per = half // wide
        for at in range(first * HD // wide, (first * HD + act.shape[2]) // wide):
            used.append(weights[group])
            if group == 0:
                row = lambda s, info, at=at, per=per: (info[0] * per + at, info[2] * steps + s)
            elif group == 1:
                row = lambda s, info, at=at, per=per: (
                    (1 - info[0]) * per + at, info[2] * steps + s)
            else:
                row = lambda s, info, at=at: (at, s)
            specs.append(pl.BlockSpec((wide, tile), row))
    flat = [act for _, _, act in pieces]
    spec = pl.BlockSpec((2, tokens, tile), lambda s, info: (0, 0, s))
    specs = [pl.BlockSpec(a.shape, lambda s, info: (0, 0, 0)) for a in flat] + specs
    operands = flat + used
    if before is not None:
        specs.append(spec)
        operands.append(before)
    depth = sum(a.shape[2] for a in flat)
    return pl.pallas_call(
        lambda *refs: project_kernel(len(flat), len(used), before is not None, *refs),
        grid_spec=pltpu.PrefetchScalarGridSpec(
            num_scalar_prefetch=1, grid=(steps,), in_specs=specs, out_specs=spec
        ),
        out_shape=jax.ShapeDtypeStruct((2, tokens, features), dtype),
        compiler_params=pltpu.CompilerParams(vmem_limit_bytes=24 * 1024 * 1024),
        cost_estimate=pl.CostEstimate(
            flops=2 * 2 * tokens * depth * features // 8,
            bytes_accessed=2 * depth * features // 8,
            transcendentals=0,
        ),
    )(info, *operands)


def on_device(queries, keys_values, block_mask, out_weight):
    tokens = queries.shape[1]
    n, f = lax.axis_size("ctx"), lax.axis_size("fsdp")
    index, place = lax.axis_index("ctx"), lax.axis_index("fsdp")
    core, side = index % 2, (index // 2) % 2
    info = jnp.stack([core, side, place]).astype(jnp.int32)
    width = queries.shape[2] // 2
    heads_half = width // HD
    rows = tokens // BLK
    features = out_weight.shape[1] // f
    bf16 = jnp.bfloat16
    parts = [[0,1],[2,3]] if heads_half == 4 else [[h] for h in range(heads_half)]

    pair = lambda i: i ^ 1
    ahead = lambda i: i + 4 if i + 4 < n else None
    across = lambda i: i ^ 2
    upper = lambda i: i + 2 if i & 2 == 0 else None
    lower = lambda i: i - 2 if i & 2 else None
    lanes = lambda start, size: pl.ds(pl.multiple_of(start, HD), size)

    got = moved(keys_values, n, pair, "pair_kv")
    there = moved(queries, n, pair, "pair_q")

    def cut_panels(core, place, ins, outs):
        pieces = []
        for r in range(1, f):
            column = pl.multiple_of(lax.rem(place + r, f) * features, HD)
            for p in range(cuts):
                row = pl.multiple_of(core * width + p * (width // cuts), width // cuts)
                at = pl.ds(p * (width // cuts), width // cuts)
                pieces.append((ins[0].at[pl.ds(row, width // cuts), pl.ds(column, features)],
                               [(slice(None), outs[r - 1].at[at])]))
        return pieces

    cuts = 4 if f == 2 else 1
    panels = copies(
        info, [out_weight], [jax.ShapeDtypeStruct((width, features), bf16)] * (f - 1),
        [(width // cuts, features)] * (cuts * (f - 1)), cut_panels, VMEM,
    )

    def join(core, ins, outs):
        pieces = []
        for slot, source in enumerate(ins[:2]):
            for head_at, target in outs:
                heads = target.shape[0]
                here = lanes(core * width + head_at * HD, heads * HD)
                pieces.append((source.at[:, 0, :, here], [
                    ((slice(None), slice(None), slice(h * HD, (h + 1) * HD)), target.at[h, slot])
                    for h in range(heads)
                ]))
        return pieces

    pair_shape = lambda heads: jax.ShapeDtypeStruct((heads, 2, 2, tokens, HD), bf16)
    held = lambda heads: (2, tokens, heads * HD)
    first, = copies(
        info, [keys_values, got, *panels], [pair_shape(len(parts[0]))], [held(len(parts[0]))] * 2,
        lambda core, place, ins, outs: join(core, ins, [(0, outs[0])]),
    )
    rest = []
    if len(parts) > 1:
        sizes = [len(part) for part in parts[1:]]
        rest = copies(
            info, [keys_values, got, first], [pair_shape(size) for size in sizes],
            [held(size) for size in sizes] * 2,
            lambda core, place, ins, outs: join(
                core, ins, [(p[0], out) for p, out in zip(parts[1:], outs)]),
        )
    own = [first] + list(rest)

    sames = [
        moved_both(panel, n, f, lambda i, k: (i, (k + r) % f), "panel")
        for r, panel in enumerate(panels, 1)
    ]


    blocks = []
    for k, mine in enumerate(own):
        one = moved(mine, n, ahead, f"near{k}")
        swap = moved(one, n, across, f"nearx{k}")
        two = moved(one, n, ahead, f"far{k}")
        two, = gated([two], swap, *[block[3] for block in blocks])
        extra = moved(jnp.where(side == 0, mine, two), n, across, f"extra{k}")
        blocks.append((one, two, swap, extra))

    mask_there = moved(block_mask, n, pair, "pair_mask")
    table = jnp.stack([
        mask_table(index * rows, rows, block_mask),
        mask_table((index ^ 1) * rows, rows, mask_there),
    ])

    acts = [[] for _ in range(2 * f)]
    ties = []
    for k, part in enumerate(parts):
        after = []
        mine, give, tie = attend(
            info, queries, keys_values, there, got, own[k], blocks[k], table,
            part, heads_half, after + ties[-1:],
        )
        ties.append(tie)
        acts[0].append(mine)
        for r in range(1, f):
            acts[2 * r].append(moved_both(mine, n, f, lambda i, k: (i, (k + r) % f), f"same{k}"))
            acts[2 * r + 1].append(moved_both(give, n, f, lambda i, k: (i ^ 1, (k + r) % f), f"cross{k}"))
        acts[1].append(moved(give, n, pair, f"pair{k}"))
    others = []
    for same in sames:
        same, = gated([same], blocks[-1][3], ties[0])
        others += [same, moved(same, n, pair, "panel_pair")]

    weights = [out_weight, out_weight] + others
    stages = [[], [], []]
    for g in range(2 * f):
        for k, (part, act) in enumerate(zip(parts, acts[g])):
            late = k == len(parts) - 1 and g > 0
            stages[(1 if g % 2 else 2) if late else 0].append((g, part[0], act))
    total = None
    stages = [stage for stage in stages if stage]
    for k, stage in enumerate(stages):
        dtype = jnp.bfloat16 if k == len(stages) - 1 else jnp.float32
        total = project(info, stage, weights, features, dtype, total)
    return total


def solution(mesh):
    in_specs = (
        P(None, "ctx", "fsdp"),
        P(None, None, "ctx", "fsdp"),
        P("ctx", None),
        P("fsdp", None),
    )
    out_specs = P(None, "ctx", "fsdp")
    return jax.shard_map(
        on_device, mesh=mesh, in_specs=in_specs, out_specs=out_specs, check_vma=False
    )
```
